128 devices in a mesh: dp: 4 (over y_lo, core), ctx: 32 (over x, z, y_hi).
Axes of the slice: x: 4, y: 4 (y_hi: 2, y_lo: 2; y = y_hi * 2 + y_lo), z: 4, core: 2. Of those that a mesh axis runs over, the one named last changes fastest.
Arguments:
- hidden_in: bfloat16 [4, 8192, 3584], P('dp', 'ctx'), may hold values from -6 to 6
- norm_gain: float32 [3584], replicated, may hold values from 0.1 to 1.9
- w_query: bfloat16 [3584, 1792], P(('dp', 'ctx')), may hold values from -3 to 3
- w_key: bfloat16 [3584, 256], P(('dp', 'ctx')), may hold values from -3 to 3
- value_weight: bfloat16 [3584, 256], P(('dp', 'ctx')), may hold values from -0.09375 to 0.09375
- marker_key_weight: bfloat16 [3584, 256], P(('dp', 'ctx')), may hold values from -0.09375 to 0.09375
- marker_value_weight: bfloat16 [3584, 256], P(('dp', 'ctx')), may hold values from -0.09375 to 0.09375
- ratio_level: int32 [4, 32], P('dp', 'ctx'), may hold values from 0 to 3, as said below
- hist_len: int32 [4], P('dp'), may hold values from 4097 to 8192, as said below
Outputs:
- attended: bfloat16 [4, 8192, 1792], P('dp', 'ctx')
The draws below stay inside these ranges and needn't reach their ends.
Inputs may be any that keep to these rules, and one draw needn't show every extreme that they name: `ratio_level`: each history has a span at level 0 and a span at level 3, so some span fills all 64 beacon slots. `hist_len`: one history of every draw is used to its full length 8192.
All inputs are finite; a program needn't handle non-finite values.
Results may differ from the reference program's by a relative error of at most 0.0069.
Values may be sent and summed in bfloat16 or wider, within the bound.
No kernel may reach another device: no remote copies, remote signals or barrier semaphores. Data moves between devices by JAX's collectives and lax.ppermute only.
A program may use at most 128 MiB of HBM per device.

```python
import math
import jax
import jax.numpy as jnp
from jax import lax

MODEL_WIDTH = 3584
QUERY_HEADS = 14
KEY_VALUE_HEADS = 2
HEAD_SIZE = 128
TOK_DEV = 256
BEA = 64
NCH = 32
L = 8192
B = 4
N_CTX = 32


def linked_baseline(key):
    return jax.random.normal(jax.random.fold_in(key, 11), (MODEL_WIDTH, KEY_VALUE_HEADS * HEAD_SIZE), jnp.float32) / math.sqrt(MODEL_WIDTH)


def draw_w_key(key, part):
    return linked_baseline(key).astype(jnp.bfloat16)


def draw_w_query(key, part):
    noise_draw = jax.random.normal(jax.random.fold_in(key, 12), (MODEL_WIDTH, QUERY_HEADS * HEAD_SIZE), jnp.float32) / math.sqrt(MODEL_WIDTH)
    result = 0.5 * noise_draw
    return result.astype(jnp.bfloat16)


def draw_ratio_level(key, part):
    levels = jax.random.randint(key, (B, NCH), 0, 4, jnp.int32)
    first_pick = jax.random.randint(jax.random.fold_in(key, 21), (B,), 0, NCH, jnp.int32)
    other_pick = (first_pick + 1 + jax.random.randint(jax.random.fold_in(key, 22), (B,), 0, NCH - 1, jnp.int32)) % NCH
    column = jnp.arange(NCH, dtype=jnp.int32)[None, :]
    levels = jnp.where(column == first_pick[:, None], 0, levels)
    levels = jnp.where(column == other_pick[:, None], 3, levels)
    return levels.astype(jnp.int32)


def draw_hist_len(key, part):
    lengths = L - jax.random.randint(key, (B,), 0, L // 2, jnp.int32)
    full_row = jax.random.randint(jax.random.fold_in(key, 31), (), 0, B, jnp.int32)
    lengths = jnp.where(jnp.arange(B, dtype=jnp.int32) == full_row, L, lengths)
    return lengths.astype(jnp.int32)


def block_scale(key, extent, split, least, high):
    factor_of, own = 1.0, jax.random.fold_in(key, 6)
    for dim, blocks in split:
        heights = jnp.exp(jax.random.uniform(jax.random.fold_in(own, dim), (blocks,), jnp.float32, least / len(split), high / len(split)))
        factor_of = factor_of * jnp.repeat(heights, extent[dim] // blocks).reshape([-1 if axis == dim else 1 for axis in range(len(extent))])
    return factor_of


def gaussian(own_key, dims, width, most, split=(), kind=jnp.bfloat16):
    entries = width * jax.random.normal(own_key, dims, jnp.float32)
    if split:
        entries = entries * block_scale(own_key, dims, split, -0.22, 0.18)
    return jnp.clip(entries, -most, most).astype(kind)


def setup_inputs(seed: int = 0) -> dict:
    splits = jax.random.split(jax.random.key(seed), 10)
    hidden_in = gaussian(splits[0], (B, L, MODEL_WIDTH), 1.0, 6.0, ((0, 4), (1, 32)))
    norm_gain = jnp.clip(1.0 + 0.18 * jax.random.normal(splits[1], (MODEL_WIDTH,), jnp.float32), 0.1, 1.9)
    w_query = draw_w_query(jax.random.fold_in(splits[9], 71), 0)
    w_key = draw_w_key(jax.random.fold_in(splits[9], 71), 0)
    value_weight = gaussian(splits[4], (MODEL_WIDTH, KEY_VALUE_HEADS * HEAD_SIZE), MODEL_WIDTH ** -0.5, 0.09375, ((0, 128),))
    marker_key_weight = gaussian(splits[5], (MODEL_WIDTH, KEY_VALUE_HEADS * HEAD_SIZE), MODEL_WIDTH ** -0.5, 0.09375, ((0, 128),))
    marker_value_weight = gaussian(splits[6], (MODEL_WIDTH, KEY_VALUE_HEADS * HEAD_SIZE), MODEL_WIDTH ** -0.5, 0.09375, ((0, 128),))
    ratio_level = draw_ratio_level(jax.random.fold_in(splits[9], 71), 0)
    hist_len = draw_hist_len(jax.random.fold_in(splits[9], 71), 0)
    return {"hidden_in": hidden_in, "norm_gain": norm_gain, "w_query": w_query, "w_key": w_key, "value_weight": value_weight, "marker_key_weight": marker_key_weight, "marker_value_weight": marker_value_weight, "ratio_level": ratio_level, "hist_len": hist_len}


eps_norm = 1e-06
negative_filler = -1e+30

def norm_rows(tokens, norm_gain):
    values = tokens.astype(jnp.float32)
    factor = lax.rsqrt(lax.optimization_barrier(jnp.mean(values * values, axis=-1, keepdims=True)) + eps_norm)
    return (values * factor * norm_gain).astype(jnp.bfloat16)

def window_table(span_level, begin_offset, length, token_rows, marker_slot_count):
    stride = (4 * jnp.power(2, span_level)).astype(jnp.int32)
    live_count = token_rows // stride
    slot_ids = lax.broadcasted_iota(jnp.int32, (marker_slot_count, token_rows), 0)
    pos_ids = lax.broadcasted_iota(jnp.int32, (marker_slot_count, token_rows), 1)
    inside = (pos_ids // stride == slot_ids) & (slot_ids < live_count) & (begin_offset + pos_ids < length)
    slot_col = jnp.arange(marker_slot_count, dtype=jnp.int32)
    live_slot = (slot_col < live_count) & (begin_offset + slot_col * stride < length)
    return (inside, live_slot)

def pool_rows(inside, normed):
    window_sum = jnp.dot(inside.astype(jnp.bfloat16), normed, preferred_element_type=jnp.float32)
    window_size = lax.optimization_barrier(jnp.sum(inside.astype(jnp.float32), axis=1))
    return (window_sum / jnp.maximum(window_size, 1.0)[:, None]).astype(jnp.bfloat16)

def reference(hidden_in, norm_gain, w_query, w_key, value_weight, marker_key_weight, marker_value_weight, ratio_level, hist_len):
    token_rows = TOK_DEV
    marker_slot_count = BEA
    segment_ranges = N_CTX
    query_group_count = QUERY_HEADS // KEY_VALUE_HEADS
    score_scale = 1.0 / math.sqrt(HEAD_SIZE)

    def one_history(history):
        tokens, levels, length = history
        normed = norm_rows(tokens, norm_gain)
        query_matrix = jnp.dot(normed, w_query, preferred_element_type=jnp.float32).astype(jnp.bfloat16)
        key_matrix = jnp.dot(normed, w_key, preferred_element_type=jnp.float32).astype(jnp.bfloat16)
        value_matrix = jnp.dot(normed, value_weight, preferred_element_type=jnp.float32).astype(jnp.bfloat16)

        def pool_span(span_id):
            block = lax.dynamic_slice_in_dim(normed, span_id * token_rows, token_rows, 0)
            inside, live_slot = window_table(levels[span_id], span_id * token_rows, length, token_rows, marker_slot_count)
            return (pool_rows(inside, block), live_slot)
        pooled, live_slot = lax.map(pool_span, jnp.arange(segment_ranges, dtype=jnp.int32))
        pooled = pooled.reshape(segment_ranges * marker_slot_count, MODEL_WIDTH)
        live_slot = live_slot.reshape(segment_ranges * marker_slot_count)
        marker_key_rows = jnp.dot(pooled, marker_key_weight, preferred_element_type=jnp.float32).astype(jnp.bfloat16)
        marker_value_rows = jnp.dot(pooled, marker_value_weight, preferred_element_type=jnp.float32).astype(jnp.bfloat16)
        marker_key_rows = marker_key_rows.reshape(segment_ranges * marker_slot_count, KEY_VALUE_HEADS, HEAD_SIZE)
        marker_value_rows = marker_value_rows.reshape(segment_ranges * marker_slot_count, KEY_VALUE_HEADS, HEAD_SIZE)
        owner = jnp.arange(segment_ranges * marker_slot_count, dtype=jnp.int32) // marker_slot_count

        def attend_span(span_id):
            begin_offset = span_id * token_rows
            segment_query = lax.dynamic_slice_in_dim(query_matrix, begin_offset, token_rows, 0).astype(jnp.float32)
            segment_query = segment_query.reshape(token_rows, KEY_VALUE_HEADS, query_group_count, HEAD_SIZE)
            segment_key = lax.dynamic_slice_in_dim(key_matrix, begin_offset, token_rows, 0).reshape(token_rows, KEY_VALUE_HEADS, HEAD_SIZE)
            segment_value = lax.dynamic_slice_in_dim(value_matrix, begin_offset, token_rows, 0).reshape(token_rows, KEY_VALUE_HEADS, HEAD_SIZE)
            all_keys = jnp.concatenate([marker_key_rows, segment_key], axis=0).astype(jnp.float32)
            all_values = jnp.concatenate([marker_value_rows, segment_value], axis=0).astype(jnp.float32)
            positions = jnp.arange(token_rows, dtype=jnp.int32)
            seen_beacon = live_slot & (owner < span_id)
            seen_raw = (positions[None, :] <= positions[:, None]) & (begin_offset + positions[None, :] < length)
            visible = jnp.concatenate([jnp.broadcast_to(seen_beacon[None, :], (token_rows, segment_ranges * marker_slot_count)), seen_raw], axis=1)
            scores = jnp.einsum('tkgd,skd->kgts', segment_query, all_keys) * score_scale
            scores = jnp.where(visible, scores, negative_filler)
            top_score = lax.optimization_barrier(jnp.max(scores, axis=-1, keepdims=True))
            weights = jnp.where(visible, jnp.exp(scores - top_score), 0.0)
            weight_sum = lax.optimization_barrier(jnp.sum(weights, axis=-1))
            rounded = weights.astype(jnp.bfloat16).astype(jnp.float32)
            weighted = jnp.einsum('kgts,skd->kgtd', rounded, all_values)
            result = weighted / jnp.where(weight_sum > 0, weight_sum, 1.0)[..., None]
            result = result.transpose(2, 0, 1, 3).reshape(token_rows, QUERY_HEADS * HEAD_SIZE)
            valid = begin_offset + positions < length
            return jnp.where(valid[:, None], result, 0.0).astype(jnp.bfloat16)
        output = lax.map(attend_span, jnp.arange(segment_ranges, dtype=jnp.int32))
        return output.reshape(segment_ranges * token_rows, QUERY_HEADS * HEAD_SIZE)
    return lax.map(one_history, (hidden_in, ratio_level, hist_len))
```

```python
import functools
import math

import jax
import jax.numpy as jnp
import numpy as np
from jax import lax
from jax.experimental import pallas as pl
from jax.experimental.pallas import tpu as pltpu
from jax.sharding import PartitionSpec as P

HEADS = 7
D = 128
WIDTH = 3584
ROWS = 28
TOK = 256
SLOTS = 64
SPANS = 32
EPS = 1e-6
FILL = -1e30
AXES = ("dp", "ctx")
SCALE = 1.0 / math.sqrt(D)


def device_id(x, y, z, c):
    return ((y % 2) * 2 + c) * 32 + (x * 4 + z) * 2 + y // 2


def make_perm(f):
    pairs = []
    for x in range(4):
        for y in range(4):
            for z in range(4):
                for c in range(2):
                    tx, ty, tz, tc = f(x, y, z, c)
                    pairs.append(
                        (device_id(x, y, z, c), device_id(tx % 4, ty % 4, tz % 4, tc % 2))
                    )
    return pairs


SWAP = make_perm(lambda x, y, z, c: (x, y, z, 1 - c))
RING = {
    "x": make_perm(lambda x, y, z, c: (x + 1 - 2 * c, y, z, c)),
    "y": make_perm(lambda x, y, z, c: (x, y + 1 - 2 * c, z, c)),
    "z": make_perm(lambda x, y, z, c: (x, y, z + 1 - 2 * c, c)),
}
HOP = {
    ("x", 1): make_perm(lambda x, y, z, c: (x + 1, y, z, c)),
    ("x", 2): make_perm(lambda x, y, z, c: (x + 2, y, z, c)),
    ("x", 3): make_perm(lambda x, y, z, c: (x + 3, y, z, c)),
    ("z", 1): make_perm(lambda x, y, z, c: (x, y, z + 1, c)),
    ("z", 2): make_perm(lambda x, y, z, c: (x, y, z + 2, c)),
    ("z", 3): make_perm(lambda x, y, z, c: (x, y, z + 3, c)),
    ("y", 2): make_perm(lambda x, y, z, c: (x, y + 2, z, c)),
}


def send(value, pairs):
    return lax.ppermute(value, AXES, pairs)


def feature_runs():
    order = []
    for x in range(4):
        for z in range(4):
            for y in range(4):
                for c in range(2):
                    order.append(device_id(x, y, z, c) * ROWS)
    source = np.concatenate([np.arange(s, s + ROWS) for s in order])
    tiles = []
    for tile in range(WIDTH // 128):
        part = source[tile * 128 : (tile + 1) * 128]
        runs = []
        lane = 0
        while lane < 128:
            end = lane + 1
            while end < 128 and part[end] == part[end - 1] + 1 and part[end] % 128 != 0:
                end += 1
            runs.append((lane, end, int(part[lane])))
            lane = end
        tiles.append(runs)
    return tiles


def norm_body(tokens_ref, gain_ref, out_ref, plain_ref):
    rows = 64

    @pl.loop(0, TOK // rows)
    def _(step):
        here = pl.ds(pl.multiple_of(step * rows, rows), rows)
        values = tokens_ref[here, :].astype(jnp.float32)
        factor = lax.rsqrt(jnp.mean(values * values, axis=-1, keepdims=True) + EPS)
        plain_ref[...] = values * factor * gain_ref[...]
        lane = lax.broadcasted_iota(jnp.int32, (rows, 128), 1)
        for tile, runs in enumerate(feature_runs()):
            joined = jnp.zeros((rows, 128), jnp.float32)
            for first, end, feature in runs:
                block, offset = divmod(feature, 128)
                piece = plain_ref[:, block * 128 : (block + 1) * 128]
                shift = (first - offset) % 128
                if shift:
                    piece = pltpu.roll(piece, shift, 1)
                joined = jnp.where((lane >= first) & (lane < end), piece, joined)
            out_ref[here, tile * 128 : (tile + 1) * 128] = joined.astype(jnp.bfloat16)


def norm_rows(tokens, gain):
    return pl.pallas_call(
        norm_body,
        out_shape=jax.ShapeDtypeStruct((TOK, WIDTH), jnp.bfloat16),
        in_specs=[pl.BlockSpec(memory_space=pltpu.VMEM)] * 2,
        out_specs=pl.BlockSpec(memory_space=pltpu.VMEM),
        scratch_shapes=[pltpu.VMEM((64, WIDTH), jnp.float32)],
        compiler_params=pltpu.CompilerParams(vmem_limit_bytes=24 * 1024 * 1024),
    )(tokens, gain.reshape(1, WIDTH))


def ring_gather(block, axis):
    got = [block]
    for _ in range(3):
        got.append(send(got[-1], RING[axis]))
    return got


def place(pieces, slots, axis, count=4):
    shape = list(pieces[0].shape)
    shape.insert(axis, count)
    joined = jnp.zeros(shape, pieces[0].dtype)
    for piece, slot in zip(pieces, slots):
        joined = lax.dynamic_update_slice_in_dim(joined, jnp.expand_dims(piece, axis), slot, axis)
    return joined


def on_device(tokens, gain, w_query, w_key, w_value, w_mark_key, w_mark_value, level, hist_len):
    dp = lax.axis_index("dp")
    span = lax.axis_index("ctx")
    core = dp % 2
    pos = {"x": span // 8, "z": (span // 2) % 4, "y": (span % 2) * 2 + dp // 2}
    sign = 1 - 2 * core
    slots = {a: [(p - sign * i) % 4 for i in range(4)] for a, p in pos.items()}

    def half(which):
        def cut(w, size):
            return lax.dynamic_slice_in_dim(w, which * size, size, 1)

        return jnp.concatenate(
            [
                cut(w_mark_key, D),
                cut(w_mark_value, D),
                cut(w_key, D),
                cut(w_value, D),
                cut(w_query, HEADS * D),
            ],
            axis=1,
        )

    mine = half(core)
    other = send(half(1 - core), SWAP)
    rows = jnp.where(
        core == 0, jnp.concatenate([mine, other], 0), jnp.concatenate([other, mine], 0)
    )

    normed = norm_rows(tokens[0], gain)
    begin = span * TOK
    length = hist_len[0]
    stride = jnp.left_shift(jnp.int32(4), level[0, 0])
    live = TOK // stride
    slot_ids = lax.broadcasted_iota(jnp.int32, (SLOTS, TOK), 0)
    pos_ids = lax.broadcasted_iota(jnp.int32, (SLOTS, TOK), 1)
    inside = (
        (jnp.right_shift(pos_ids, level[0, 0] + 2) == slot_ids)
        & (slot_ids < live)
        & (begin + pos_ids < length)
    )
    window = jnp.dot(inside.astype(jnp.bfloat16), normed, preferred_element_type=jnp.float32)
    size = jnp.sum(inside.astype(jnp.float32), axis=1)
    pooled = (window / jnp.maximum(size, 1.0)[:, None]).astype(jnp.bfloat16)
    valid = jnp.clip(length - begin, 0, TOK)
    count = jnp.minimum(live, (valid + stride - 1) // stride)
    facts = jnp.concatenate(
        [
            jnp.full((8, WIDTH), count.astype(jnp.bfloat16)),
            jnp.full((8, WIDTH), valid.astype(jnp.bfloat16)),
        ],
        0,
    )
    packed = jnp.concatenate([normed, pooled, facts], 0)
    mate = send(packed, SWAP)
    both = jnp.stack([normed, mate[:TOK]])
    both_pooled = jnp.stack([pooled, mate[TOK : TOK + SLOTS]])
    mate_count = mate[TOK + SLOTS, 0].astype(jnp.int32)
    mate_valid = mate[TOK + SLOTS + 8, 0].astype(jnp.int32)
    counts = jnp.stack([count, mate_count])
    valids = jnp.stack([valid, mate_valid])

    def part(block, order):
        first, second, last = order
        one = place(ring_gather(block, first), slots[first], 0)
        two = place(ring_gather(one, second), slots[second], 0)
        three = place(ring_gather(two, last), slots[last], 0)
        where = {last: 0, second: 1, first: 2}
        full = three.transpose(where["x"], where["z"], where["y"], 3, 4)
        return full.reshape(WIDTH, block.shape[1])

    cols = (256, 896, 1408)
    w_mark = part(rows[:, : cols[0]], ("x", "y", "z"))
    w_a = part(rows[:, cols[0] : cols[1]], ("y", "z", "x"))
    w_b = part(rows[:, cols[1] :], ("z", "x", "y"))

    def project(x, w):
        out = jnp.dot(x.reshape(-1, WIDTH), w, preferred_element_type=jnp.float32)
        return out.astype(jnp.bfloat16).reshape(x.shape[0], x.shape[1], -1)

    beacon = project(both_pooled, w_mark)
    flags = jnp.broadcast_to(counts.astype(jnp.bfloat16)[:, None, None], (2, 8, 256))
    block = jnp.concatenate([beacon, flags], 1)

    pairs = [block, send(block, HOP["y", 2])]
    pairs = jnp.stack(pairs)
    across = jnp.stack([pairs] + [send(pairs, HOP["x", i]) for i in (1, 2, 3)])
    every = jnp.stack([across] + [send(across, HOP["z", i]) for i in (1, 2, 3)])
    back = jnp.arange(4)
    z_of = (pos["z"] - back) % 4
    x_of = (pos["x"] - back) % 4
    h_of = (span % 2) ^ jnp.arange(2)
    owner = (x_of[None, :, None] * 4 + z_of[:, None, None]) * 2 + h_of[None, None, :]
    owner = owner.reshape(SPANS)
    every = every.reshape(SPANS, 2, SLOTS + 8, 256)
    live_counts = every[:, :, SLOTS, 0].astype(jnp.int32)
    beacon_keys = every[:, :, :SLOTS, :D].transpose(1, 0, 2, 3).reshape(2, SPANS * SLOTS, D)
    beacon_values = every[:, :, :SLOTS, D:].transpose(1, 0, 2, 3).reshape(2, SPANS * SLOTS, D)
    seen = (jnp.arange(SLOTS)[None, None, :] < live_counts.T[:, :, None]) & (owner < span)[
        None, :, None
    ]
    seen = seen.reshape(2, SPANS * SLOTS)

    part_a = project(both, w_a)
    part_b = project(both, w_b)
    keys = part_a[..., :D]
    values = part_a[..., D : 2 * D]
    queries = jnp.concatenate([part_a[..., 2 * D :], part_b], -1).reshape(2, TOK, HEADS, D)

    at = jnp.arange(TOK)
    raw_seen = (at[None, None, :] <= at[None, :, None]) & (
        at[None, None, :] < valids[:, None, None]
    )
    raw = jnp.einsum("htgd,hsd->hgts", queries, keys, preferred_element_type=jnp.float32) * SCALE
    raw = jnp.where(raw_seen[:, None], raw, FILL)
    far = (
        jnp.einsum("htgd,hsd->hgts", queries, beacon_keys, preferred_element_type=jnp.float32)
        * SCALE
    )
    far = jnp.where(seen[:, None, None, :], far, FILL)
    top = jnp.maximum(jnp.max(raw, -1), jnp.max(far, -1))[..., None]
    raw_w = jnp.where(raw_seen[:, None], jnp.exp(raw - top), 0.0)
    far_w = jnp.where(seen[:, None, None, :], jnp.exp(far - top), 0.0)
    total = jnp.sum(raw_w, -1) + jnp.sum(far_w, -1)
    summed = jnp.einsum(
        "hgts,hsd->hgtd", raw_w.astype(jnp.bfloat16), values, preferred_element_type=jnp.float32
    ) + jnp.einsum(
        "hgts,hsd->hgtd",
        far_w.astype(jnp.bfloat16),
        beacon_values,
        preferred_element_type=jnp.float32,
    )
    result = summed / jnp.where(total > 0, total, 1.0)[..., None]
    result = jnp.where((at < valids[:, None])[:, None, :, None], result, 0.0)
    result = result.transpose(0, 2, 1, 3).reshape(2, TOK, HEADS * D).astype(jnp.bfloat16)
    back_home = send(result[1], SWAP)
    full = jnp.where(
        core == 0,
        jnp.concatenate([result[0], back_home], -1),
        jnp.concatenate([back_home, result[0]], -1),
    )
    return full[None]


def solution(mesh):
    return jax.shard_map(
        on_device,
        mesh=mesh,
        in_specs=(
            P("dp", "ctx", None),
            P(),
            P(("dp", "ctx"), None),
            P(("dp", "ctx"), None),
            P(("dp", "ctx"), None),
            P(("dp", "ctx"), None),
            P(("dp", "ctx"), None),
            P("dp", "ctx"),
            P("dp"),
        ),
        out_specs=P("dp", "ctx", None),
        check_vma=False,
    )
```

```python
import functools
import math

import jax
import jax.numpy as jnp
import numpy as np
from jax import lax
from jax.experimental import pallas as pl
from jax.experimental.pallas import tpu as pltpu
from jax.sharding import PartitionSpec as P

HEADS = 7
D = 128
WIDTH = 3584
ROWS = 28
TOK = 256
SLOTS = 64
SPANS = 32
EPS = 1e-6
FILL = -1e30
AXES = ("dp", "ctx")
SCALE = 1.0 / math.sqrt(D)


def device_id(x, y, z, c):
    return ((y % 2) * 2 + c) * 32 + (x * 4 + z) * 2 + y // 2


def make_perm(f):
    pairs = []
    for x in range(4):
        for y in range(4):
            for z in range(4):
                for c in range(2):
                    tx, ty, tz, tc = f(x, y, z, c)
                    pairs.append(
                        (device_id(x, y, z, c), device_id(tx % 4, ty % 4, tz % 4, tc % 2))
                    )
    return pairs


SWAP = make_perm(lambda x, y, z, c: (x, y, z, 1 - c))
RING = {
    "x": make_perm(lambda x, y, z, c: (x + 1 - 2 * c, y, z, c)),
    "y": make_perm(lambda x, y, z, c: (x, y + 1 - 2 * c, z, c)),
    "z": make_perm(lambda x, y, z, c: (x, y, z + 1 - 2 * c, c)),
}
ACROSS = make_perm(lambda x, y, z, c: (x, y + 2, z, c))


def flip(axis, turn):
    def partner(x, y, z, c):
        at = {"x": x, "y": y, "z": z}
        at[axis] ^= 1 if (c + turn) % 2 == 0 else 3
        return at["x"], at["y"], at["z"], c

    return make_perm(partner)


FLIP = {(axis, turn): flip(axis, turn) for axis in "xyz" for turn in (0, 1)}

ORDERS = (("z", "x", "y"), ("y", "z", "x"), ("x", "y", "z"))
CUTS = (0, 256, 896, 1408)
KEPT = 3
SLAB = WIDTH // 4
PACK = 2 * TOK + SLOTS + 16


def send(value, pairs):
    return lax.ppermute(value, AXES, pairs)


def feature_runs(order):
    first, second, last = order
    starts = []
    for i in range(4):
        for j in range(4):
            for k in range(4):
                at = {last: i, second: j, first: k}
                for c in range(2):
                    starts.append(device_id(at["x"], at["y"], at["z"], c) * ROWS)
    source = np.concatenate([np.arange(s, s + ROWS) for s in starts])
    tiles = []
    for tile in range(WIDTH // 128):
        part = source[tile * 128 : (tile + 1) * 128]
        runs = []
        lane = 0
        while lane < 128:
            end = lane + 1
            while end < 128 and part[end] == part[end - 1] + 1 and part[end] % 128 != 0:
                end += 1
            runs.append((lane, end, int(part[lane])))
            lane = end
        tiles.append(runs)
    return tiles


def reorder(plain_ref, out_ref, order, count, out_rows):
    lane = lax.broadcasted_iota(jnp.int32, (count, 128), 1)
    for tile, runs in enumerate(feature_runs(order)):
        joined = jnp.zeros((count, 128), jnp.float32)
        for first, end, feature in runs:
            block, offset = divmod(feature, 128)
            piece = plain_ref[:, block * 128 : (block + 1) * 128]
            shift = (first - offset) % 128
            if shift:
                piece = pltpu.roll(piece, shift, 1)
            joined = jnp.where((lane >= first) & (lane < end), piece, joined)
        slab, column = divmod(tile, SLAB // 128)
        out_ref[slab, out_rows, column * 128 : (column + 1) * 128] = joined.astype(jnp.bfloat16)


def norm_body(fact_ref, tokens_ref, gain_ref, out_ref, plain_ref, normed_ref):
    rows = 64
    level, valid, count = fact_ref[0], fact_ref[1], fact_ref[2]

    @pl.loop(0, TOK // rows)
    def _(step):
        here = pl.ds(pl.multiple_of(step * rows, rows), rows)
        below = pl.ds(pl.multiple_of(step * rows + TOK, rows), rows)
        values = tokens_ref[here, :].astype(jnp.float32)
        factor = lax.rsqrt(jnp.mean(values * values, axis=-1, keepdims=True) + EPS)
        plain_ref[...] = values * factor * gain_ref[...]
        normed_ref[here, :] = plain_ref[...].astype(jnp.bfloat16)
        reorder(plain_ref, out_ref, ORDERS[1], rows, here)
        reorder(plain_ref, out_ref, ORDERS[2], rows, below)

    shift = level + 2
    live = jnp.right_shift(TOK, shift)
    slot = lax.broadcasted_iota(jnp.int32, (SLOTS, TOK), 0)
    position = lax.broadcasted_iota(jnp.int32, (SLOTS, TOK), 1)
    inside = (jnp.right_shift(position, shift) == slot) & (slot < live) & (position < valid)
    window = jnp.where(inside, 1.0, 0.0)
    size = jnp.maximum(jnp.sum(window, axis=1, keepdims=True), 1.0)
    sums = jnp.dot(
        window.astype(jnp.bfloat16), normed_ref[...], preferred_element_type=jnp.float32
    )
    plain_ref[...] = sums / size
    reorder(plain_ref, out_ref, ORDERS[0], SLOTS, pl.ds(2 * TOK, SLOTS))
    row = lax.broadcasted_iota(jnp.int32, (16, SLAB), 0)
    facts = jnp.where(row < 8, count, valid).astype(jnp.float32).astype(jnp.bfloat16)
    for slab in range(4):
        out_ref[slab, pl.ds(2 * TOK + SLOTS, 16), :] = facts


def norm_rows(facts, tokens, gain):
    return pl.pallas_call(
        norm_body,
        out_shape=jax.ShapeDtypeStruct((4, PACK, SLAB), jnp.bfloat16),
        in_specs=[pl.BlockSpec(memory_space=pltpu.SMEM)]
        + [pl.BlockSpec(memory_space=pltpu.VMEM)] * 2,
        out_specs=pl.BlockSpec(memory_space=pltpu.VMEM),
        scratch_shapes=[
            pltpu.VMEM((64, WIDTH), jnp.float32),
            pltpu.VMEM((TOK, WIDTH), jnp.bfloat16),
        ],
        compiler_params=pltpu.CompilerParams(vmem_limit_bytes=32 * 1024 * 1024),
    )(facts, tokens, gain.reshape(1, WIDTH))


BLOCK = 512
ROOM = SPANS * SLOTS + BLOCK


def attend_body(which, wide, info_ref, count_ref, part_a_ref, part_b_ref, far_k_ref, far_v_ref, *rest):
    out_ref, near_ref, keys_ref, values_ref, bias_ref, score_ref = rest
    span, valid, column = info_ref[0], info_ref[1], info_ref[2]

    lane = lax.broadcasted_iota(jnp.int32, (1, ROOM), 1)
    bias_ref[...] = jnp.full((1, ROOM), FILL, jnp.float32)

    def pack(i, at):
        place_k, place_v = info_ref[3 + i], info_ref[3 + SPANS + i]
        count = count_ref[place_k]
        here = pl.ds(pl.multiple_of(at, 16), SLOTS)
        keys_ref[here, :] = far_k_ref[place_k, which, :SLOTS, :]
        values_ref[here, :] = far_v_ref[place_v, which]
        bias_ref[...] = jnp.where((lane >= at) & (lane < at + count), 0.0, bias_ref[...])
        return at + ((count + 15) // 16) * 16

    used = lax.fori_loop(0, span, pack, jnp.int32(0))
    rest_rows = pl.ds(pl.multiple_of(used, 16), BLOCK)
    keys_ref[rest_rows, :] = jnp.zeros((BLOCK, D), jnp.bfloat16)
    values_ref[rest_rows, :] = jnp.zeros((BLOCK, D), jnp.bfloat16)
    blocks = (used + BLOCK - 1) // BLOCK

    row = lax.broadcasted_iota(jnp.int32, (TOK, TOK), 0)
    col = lax.broadcasted_iota(jnp.int32, (TOK, TOK), 1)
    near_ref[...] = jnp.where((col <= row) & (col < valid), 0.0, FILL)
    alive = lax.broadcasted_iota(jnp.int32, (TOK, D), 0) < valid
    power = SCALE * math.log2(math.e)
    contract = (((1,), (1,)), ((), ()))

    def fold(op, scores):
        out = scores[:, :D]
        for i in range(1, scores.shape[1] // D):
            out = op(out, scores[:, i * D : (i + 1) * D])
        return out

    for head in range(HEADS):
        if head < KEPT:
            query = part_a_ref[:, (2 + head) * D : (3 + head) * D]
        else:
            query = part_b_ref[:, (head - KEPT) * D : (head - KEPT + 1) * D]
        near = (
            lax.dot_general(
                query, part_a_ref[:, :D], contract, preferred_element_type=jnp.float32
            )
            + near_ref[...]
        )

        def score(i, top, query=query):
            here = pl.ds(pl.multiple_of(i * BLOCK, BLOCK), BLOCK)
            far = lax.dot_general(
                query, keys_ref[here, :], contract, preferred_element_type=jnp.float32
            )
            far = far + bias_ref[:, here]
            score_ref[:, here] = far
            return jnp.maximum(top, fold(jnp.maximum, far))

        top = lax.fori_loop(0, blocks, score, fold(jnp.maximum, near))
        top = jnp.max(top, axis=1, keepdims=True)
        weight = jnp.exp2((near - top) * power)
        total = fold(jnp.add, weight)
        mixed = jnp.dot(
            weight.astype(jnp.bfloat16),
            part_a_ref[:, D : 2 * D],
            preferred_element_type=jnp.float32,
        )

        def mix(i, state, top=top):
            total, mixed = state
            here = pl.ds(pl.multiple_of(i * BLOCK, BLOCK), BLOCK)
            weight = jnp.exp2((score_ref[:, here] - top) * power)
            mixed = mixed + jnp.dot(
                weight.astype(jnp.bfloat16), values_ref[here, :], preferred_element_type=jnp.float32
            )
            return total + fold(jnp.add, weight), mixed

        total, mixed = lax.fori_loop(0, blocks, mix, (total, mixed))
        total = jnp.sum(total, axis=1, keepdims=True)
        result = jnp.where(alive, mixed / total, 0.0).astype(jnp.bfloat16)
        if wide:
            out_ref[:, pl.ds(pl.multiple_of(column + head * D, D), D)] = result
        else:
            out_ref[:, head * D : (head + 1) * D] = result


def attend(which, wide, info, counts, part_a, part_b, far_k, far_v):
    columns = 2 * HEADS * D if wide else HEADS * D
    smem, vmem = pl.BlockSpec(memory_space=pltpu.SMEM), pl.BlockSpec(memory_space=pltpu.VMEM)
    return pl.pallas_call(
        functools.partial(attend_body, which, wide),
        out_shape=jax.ShapeDtypeStruct((TOK, columns), jnp.bfloat16),
        in_specs=[smem, smem, vmem, vmem, vmem, vmem],
        out_specs=vmem,
        scratch_shapes=[
            pltpu.VMEM((TOK, TOK), jnp.float32),
            pltpu.VMEM((ROOM, D), jnp.bfloat16),
            pltpu.VMEM((ROOM, D), jnp.bfloat16),
            pltpu.VMEM((1, ROOM), jnp.float32),
            pltpu.VMEM((TOK, ROOM), jnp.float32),
        ],
        compiler_params=pltpu.CompilerParams(vmem_limit_bytes=32 * 1024 * 1024),
    )(info, counts, part_a, part_b, far_k, far_v)


def double(block, axis):
    pair = jnp.stack([block, send(block, FLIP[axis, 0])])
    return jnp.concatenate([pair, send(pair, FLIP[axis, 1])])


def in_place(pieces, slots, blank):
    joined = blank
    for i, slot in enumerate(slots):
        joined = lax.dynamic_update_slice_in_dim(joined, pieces[i][None], slot, 0)
    return joined


def on_device(tokens, gain, w_query, w_key, w_value, w_mark_key, w_mark_value, level, hist_len):
    dp = lax.axis_index("dp")
    span = lax.axis_index("ctx")
    core = dp % 2
    pos = {"x": span // 8, "z": (span // 2) % 4, "y": (span % 2) * 2 + dp // 2}
    sign = 1 - 2 * core
    near, far = 1 + 2 * core, 3 - 2 * core

    def half(which):
        def cut(w, size):
            return jnp.where(which == 0, w[:, :size], w[:, size:])

        return jnp.concatenate(
            [
                cut(w_mark_key, D),
                cut(w_mark_value, D),
                cut(w_key, D),
                cut(w_value, D),
                cut(w_query, HEADS * D),
            ],
            axis=1,
        )

    mine = half(core)
    other = send(half(1 - core), SWAP)
    rows = jnp.where(
        core == 0, jnp.concatenate([mine, other], 0), jnp.concatenate([other, mine], 0)
    )
    rows, tokens = lax.optimization_barrier((rows, tokens))

    begin = span * TOK
    stride = jnp.left_shift(jnp.int32(4), level[0, 0])
    valid = jnp.clip(hist_len[0] - begin, 0, TOK)
    count = jnp.minimum(TOK // stride, (valid + stride - 1) // stride)
    packed = norm_rows(jnp.stack([level[0, 0], valid, count]), tokens[0], gain)
    mate = send(packed, SWAP)
    facts = mate[0, 2 * TOK + SLOTS :, 0].astype(jnp.int32)
    mate_count, mate_valid = facts[0], facts[8]
    both_a = jnp.concatenate([packed[:, :TOK], mate[:, :TOK]], 1)
    both_b = jnp.concatenate([packed[:, TOK : 2 * TOK], mate[:, TOK : 2 * TOK]], 1)
    pooled = jnp.concatenate(
        [packed[:, 2 * TOK : 2 * TOK + SLOTS], mate[:, 2 * TOK : 2 * TOK + SLOTS]], 1
    )

    def arrive(block, order):
        for axis in order[:2]:
            p = pos[axis]
            blank = jnp.zeros((4,) + block.shape, block.dtype)
            block = in_place(double(block, axis), (p, p ^ near, p ^ far, p ^ 2), blank)
            block = block.reshape(-1, block.shape[-1])
        pieces = [block]
        for _ in range(3):
            pieces.append(send(pieces[-1], RING[order[2]]))
        return pieces

    def project(slabs, pieces, axis):
        out = None
        for i, piece in enumerate(pieces):
            x = lax.dynamic_index_in_dim(slabs, (pos[axis] - sign * i) % 4, 0, keepdims=False)
            term = jnp.dot(x, piece, preferred_element_type=jnp.float32)
            out = term if out is None else out + term
        return out.astype(jnp.bfloat16)

    arrived = [
        arrive(rows[:, CUTS[i] : CUTS[i + 1]], ORDERS[i]) for i in range(3)
    ]
    beacon = project(pooled, arrived[0], ORDERS[0][2]).reshape(2, SLOTS, 2 * D)
    counts = jnp.stack([count, mate_count]).astype(jnp.bfloat16)
    flags = jnp.broadcast_to(counts[:, None, None], (2, 16, D))
    block_k = jnp.concatenate([beacon[..., :D], flags], 1)
    block_v = beacon[..., D:]
    block = jnp.concatenate([block_k, block_v], 1)
    block = jnp.stack([block, send(block, ACROSS)])
    every_k = double(double(block[:, :, : SLOTS + 16], "x"), "z")
    every_v = double(double(block[:, :, SLOTS + 16 :], "z"), "x")
    every_k = every_k.reshape(SPANS, 2, SLOTS + 16, D)
    every_v = every_v.reshape(SPANS, 2, SLOTS, D)

    owner = jnp.arange(SPANS, dtype=jnp.int32)

    def code(axis, at):
        d = at ^ pos[axis]
        return jnp.where(d == 0, 0, jnp.where(d == near, 1, jnp.where(d == far, 2, 3)))

    code_x, code_z = code("x", owner // 8), code("z", (owner // 2) % 4)
    code_h = (owner ^ span) % 2
    at_k = (code_z * 4 + code_x) * 2 + code_h
    at_v = (code_x * 4 + code_z) * 2 + code_h
    live = every_k[:, :, SLOTS, 0].astype(jnp.int32)

    part_a = project(both_a, arrived[1], ORDERS[1][2])
    part_b = project(both_b, arrived[2], ORDERS[2][2])

    def attention(which, valid, wide):
        here = slice(which * TOK, (which + 1) * TOK)
        info = jnp.concatenate(
            [jnp.stack([span, valid, core * (HEADS * D)]), at_k, at_v]
        )
        return attend(
            which,
            wide,
            info,
            live[:, which],
            part_a[here],
            part_b[here],
            every_k,
            every_v,
        )

    away = send(attention(1, mate_valid, False), SWAP)
    home = attention(0, valid, True)
    full = lax.dynamic_update_slice(home, away, (0, (1 - core) * (HEADS * D)))
    return full[None]


def solution(mesh):
    return jax.shard_map(
        on_device,
        mesh=mesh,
        in_specs=(
            P("dp", "ctx", None),
            P(),
            P(("dp", "ctx"), None),
            P(("dp", "ctx"), None),
            P(("dp", "ctx"), None),
            P(("dp", "ctx"), None),
            P(("dp", "ctx"), None),
            P("dp", "ctx"),
            P("dp"),
        ),
        out_specs=P("dp", "ctx", None),
        check_vma=False,
    )
```

```python
import functools
import math

import jax
import jax.numpy as jnp
import numpy as np
from jax import lax
from jax.experimental import pallas as pl
from jax.experimental.pallas import tpu as pltpu
from jax.sharding import PartitionSpec as P

HEADS = 7
D = 128
WIDTH = 3584
ROWS = 28
TOK = 256
SLOTS = 64
SPANS = 32
EPS = 1e-6
FILL = -1e30
AXES = ("dp", "ctx")
SCALE = 1.0 / math.sqrt(D)


def device_id(x, y, z, c):
    return ((y % 2) * 2 + c) * 32 + (x * 4 + z) * 2 + y // 2


def make_perm(f):
    pairs = []
    for x in range(4):
        for y in range(4):
            for z in range(4):
                for c in range(2):
                    tx, ty, tz, tc = f(x, y, z, c)
                    pairs.append(
                        (device_id(x, y, z, c), device_id(tx % 4, ty % 4, tz % 4, tc % 2))
                    )
    return pairs


SWAP = make_perm(lambda x, y, z, c: (x, y, z, 1 - c))
MATE = make_perm(lambda x, y, z, c: (x, y ^ 1, z, c))
ACROSS = make_perm(lambda x, y, z, c: (x, y ^ 3, z, c))
RING = {
    "x": make_perm(lambda x, y, z, c: (x + 1 - 2 * c, y, z, c)),
    "z": make_perm(lambda x, y, z, c: (x, y, z + 1 - 2 * c, c)),
}


def flip(axis, turn):
    def partner(x, y, z, c):
        at = {"x": x, "y": y, "z": z}
        at[axis] ^= 1 if (c + turn) % 2 == 0 else 3
        return at["x"], at["y"], at["z"], c

    return make_perm(partner)


FLIP = {(axis, turn): flip(axis, turn) for axis in "xz" for turn in (0, 1)}

CUTS = (0, 256, 640, 1408)
KEPT = 1
HALF = WIDTH // 2


def send(value, pairs):
    return lax.ppermute(value, AXES, pairs)


def feature_runs():
    starts = []
    for c in range(2):
        for z in range(4):
            for x in range(4):
                for y in (0, 1, 2, 3):
                    starts.append(device_id(x, y, z, c) * ROWS)
    source = np.concatenate([np.arange(s, s + ROWS) for s in starts])
    tiles = []
    for tile in range(WIDTH // 128):
        part = source[tile * 128 : (tile + 1) * 128]
        runs = []
        lane = 0
        while lane < 128:
            end = lane + 1
            while end < 128 and part[end] == part[end - 1] + 1 and part[end] % 128 != 0:
                end += 1
            runs.append((lane, end, int(part[lane])))
            lane = end
        tiles.append(runs)
    return tiles


def reorder(plain_ref, out_ref, count, out_rows):
    lane = lax.broadcasted_iota(jnp.int32, (count, 128), 1)
    for tile, runs in enumerate(feature_runs()):
        joined = jnp.zeros((count, 128), jnp.float32)
        for first, end, feature in runs:
            block, offset = divmod(feature, 128)
            piece = plain_ref[:, block * 128 : (block + 1) * 128]
            shift = (first - offset) % 128
            if shift:
                piece = pltpu.roll(piece, shift, 1)
            joined = jnp.where((lane >= first) & (lane < end), piece, joined)
        side, column = divmod(tile, HALF // 128)
        out_ref[side, out_rows, column * 128 : (column + 1) * 128] = joined.astype(jnp.bfloat16)


def norm_body(fact_ref, tokens_ref, gain_ref, out_ref, pool_ref, plain_ref, normed_ref):
    rows = 64
    level, valid, count = fact_ref[0], fact_ref[1], fact_ref[2]

    @pl.loop(0, TOK // rows)
    def _(step):
        here = pl.ds(pl.multiple_of(step * rows, rows), rows)
        values = tokens_ref[here, :].astype(jnp.float32)
        factor = lax.rsqrt(jnp.mean(values * values, axis=-1, keepdims=True) + EPS)
        plain_ref[...] = values * factor * gain_ref[...]
        normed_ref[here, :] = plain_ref[...].astype(jnp.bfloat16)
        reorder(plain_ref, out_ref, rows, here)

    shift = level + 2
    live = jnp.right_shift(TOK, shift)
    slot = lax.broadcasted_iota(jnp.int32, (SLOTS, TOK), 0)
    position = lax.broadcasted_iota(jnp.int32, (SLOTS, TOK), 1)
    inside = (jnp.right_shift(position, shift) == slot) & (slot < live) & (position < valid)
    window = jnp.where(inside, 1.0, 0.0)
    size = jnp.maximum(jnp.sum(window, axis=1, keepdims=True), 1.0)
    sums = jnp.dot(
        window.astype(jnp.bfloat16), normed_ref[...], preferred_element_type=jnp.float32
    )
    plain_ref[...] = sums / size
    reorder(plain_ref, pool_ref, SLOTS, pl.ds(0, SLOTS))
    row = lax.broadcasted_iota(jnp.int32, (16, HALF), 0)
    facts = jnp.where(row < 8, count, valid).astype(jnp.float32).astype(jnp.bfloat16)
    for side in range(2):
        pool_ref[side, pl.ds(SLOTS, 16), :] = facts


def norm_rows(facts, tokens, gain):
    vmem = pl.BlockSpec(memory_space=pltpu.VMEM)
    return pl.pallas_call(
        norm_body,
        out_shape=[
            jax.ShapeDtypeStruct((2, TOK, HALF), jnp.bfloat16),
            jax.ShapeDtypeStruct((2, SLOTS + 16, HALF), jnp.bfloat16),
        ],
        in_specs=[pl.BlockSpec(memory_space=pltpu.SMEM), vmem, vmem],
        out_specs=[vmem, vmem],
        scratch_shapes=[
            pltpu.VMEM((64, WIDTH), jnp.float32),
            pltpu.VMEM((TOK, WIDTH), jnp.bfloat16),
        ],
        compiler_params=pltpu.CompilerParams(vmem_limit_bytes=32 * 1024 * 1024),
    )(facts, tokens, gain.reshape(1, WIDTH))


BLOCK = 512
ROOM = SPANS * SLOTS + BLOCK


def attend_body(wide, info_ref, count_ref, part_a_ref, part_b_ref, far_k_ref, far_v_ref, *rest):
    out_ref, near_ref, keys_ref, values_ref, bias_ref, score_ref = rest
    span, valid, column, which = info_ref[0], info_ref[1], info_ref[2], info_ref[3]

    lane = lax.broadcasted_iota(jnp.int32, (1, ROOM), 1)
    bias_ref[...] = jnp.full((1, ROOM), FILL, jnp.float32)

    def pack(i, at):
        place_k, place_v = info_ref[4 + i], info_ref[4 + SPANS + i]
        count = count_ref[place_k * 2 + which]
        here = pl.ds(pl.multiple_of(at, 16), SLOTS)
        keys_ref[here, :] = far_k_ref[place_k, which, :SLOTS, :]
        values_ref[here, :] = far_v_ref[place_v, which]
        bias_ref[...] = jnp.where((lane >= at) & (lane < at + count), 0.0, bias_ref[...])
        return at + ((count + 15) // 16) * 16

    used = lax.fori_loop(0, span, pack, jnp.int32(0))
    rest_rows = pl.ds(pl.multiple_of(used, 16), BLOCK)
    keys_ref[rest_rows, :] = jnp.zeros((BLOCK, D), jnp.bfloat16)
    values_ref[rest_rows, :] = jnp.zeros((BLOCK, D), jnp.bfloat16)
    blocks = (used + BLOCK - 1) // BLOCK

    row = lax.broadcasted_iota(jnp.int32, (TOK, TOK), 0)
    col = lax.broadcasted_iota(jnp.int32, (TOK, TOK), 1)
    near_ref[...] = jnp.where((col <= row) & (col < valid), 0.0, FILL)
    alive = lax.broadcasted_iota(jnp.int32, (TOK, D), 0) < valid
    power = SCALE * math.log2(math.e)
    contract = (((1,), (1,)), ((), ()))

    def fold(op, scores):
        out = scores[:, :D]
        for i in range(1, scores.shape[1] // D):
            out = op(out, scores[:, i * D : (i + 1) * D])
        return out

    for head in range(HEADS):
        if head < KEPT:
            query = part_a_ref[:, (2 + head) * D : (3 + head) * D]
        else:
            query = part_b_ref[:, (head - KEPT) * D : (head - KEPT + 1) * D]
        near = (
            lax.dot_general(
                query, part_a_ref[:, :D], contract, preferred_element_type=jnp.float32
            )
            + near_ref[...]
        )

        def score(i, top, query=query):
            here = pl.ds(pl.multiple_of(i * BLOCK, BLOCK), BLOCK)
            far = lax.dot_general(
                query, keys_ref[here, :], contract, preferred_element_type=jnp.float32
            )
            far = far + bias_ref[:, here]
            score_ref[:, here] = far
            return jnp.maximum(top, fold(jnp.maximum, far))

        top = lax.fori_loop(0, blocks, score, fold(jnp.maximum, near))
        top = jnp.max(top, axis=1, keepdims=True)
        weight = jnp.exp2((near - top) * power)
        total = fold(jnp.add, weight)
        mixed = jnp.dot(
            weight.astype(jnp.bfloat16),
            part_a_ref[:, D : 2 * D],
            preferred_element_type=jnp.float32,
        )

        def mix(i, state, top=top):
            total, mixed = state
            here = pl.ds(pl.multiple_of(i * BLOCK, BLOCK), BLOCK)
            weight = jnp.exp2((score_ref[:, here] - top) * power)
            mixed = mixed + jnp.dot(
                weight.astype(jnp.bfloat16), values_ref[here, :], preferred_element_type=jnp.float32
            )
            return total + fold(jnp.add, weight), mixed

        total, mixed = lax.fori_loop(0, blocks, mix, (total, mixed))
        total = jnp.sum(total, axis=1, keepdims=True)
        result = jnp.where(alive, mixed / total, 0.0).astype(jnp.bfloat16)
        if wide:
            out_ref[:, pl.ds(pl.multiple_of(column + head * D, D), D)] = result
        else:
            out_ref[:, head * D : (head + 1) * D] = result


def attend(wide, info, counts, part_a, part_b, far_k, far_v):
    columns = 2 * HEADS * D if wide else HEADS * D
    smem, vmem = pl.BlockSpec(memory_space=pltpu.SMEM), pl.BlockSpec(memory_space=pltpu.VMEM)
    return pl.pallas_call(
        functools.partial(attend_body, wide),
        out_shape=jax.ShapeDtypeStruct((TOK, columns), jnp.bfloat16),
        in_specs=[smem, smem, vmem, vmem, vmem, vmem],
        out_specs=vmem,
        scratch_shapes=[
            pltpu.VMEM((TOK, TOK), jnp.float32),
            pltpu.VMEM((ROOM, D), jnp.bfloat16),
            pltpu.VMEM((ROOM, D), jnp.bfloat16),
            pltpu.VMEM((1, ROOM), jnp.float32),
            pltpu.VMEM((TOK, ROOM), jnp.float32),
        ],
        compiler_params=pltpu.CompilerParams(vmem_limit_bytes=32 * 1024 * 1024),
    )(info, counts, part_a, part_b, far_k, far_v)


def double(block, axis):
    pair = jnp.stack([block, send(block, FLIP[axis, 0])])
    return jnp.concatenate([pair, send(pair, FLIP[axis, 1])])


def in_place(pieces, slots, blank):
    joined = blank
    for i, slot in enumerate(slots):
        joined = lax.dynamic_update_slice_in_dim(joined, pieces[i][None], slot, 0)
    return joined


def on_device(tokens, gain, w_query, w_key, w_value, w_mark_key, w_mark_value, level, hist_len):
    dp = lax.axis_index("dp")
    span = lax.axis_index("ctx")
    core, low, high = dp % 2, dp // 2, span % 2
    head = low ^ high
    pos = {"x": span // 8, "z": (span // 2) % 4}
    sign = 1 - 2 * core
    near, far = 1 + 2 * core, 3 - 2 * core

    def order(first, one, two):
        return jnp.where(first == 0, jnp.concatenate([one, two], 0), jnp.concatenate([two, one], 0))

    def half(which):
        def cut(w, size):
            return jnp.where(which == 0, w[:, :size], w[:, size:])

        return jnp.concatenate(
            [
                cut(w_mark_key, D),
                cut(w_mark_value, D),
                cut(w_key, D),
                cut(w_value, D),
                cut(w_query, HEADS * D),
            ],
            axis=1,
        )

    mine = half(head)
    rows = order(low, mine, send(half(1 - head), MATE))

    begin = span * TOK
    stride = jnp.left_shift(jnp.int32(4), level[0, 0])
    valid = jnp.clip(hist_len[0] - begin, 0, TOK)
    count = jnp.minimum(TOK // stride, (valid + stride - 1) // stride)
    normed, pooled = norm_rows(jnp.stack([level[0, 0], valid, count]), tokens[0], gain)
    mate_pooled = send(pooled, MATE)
    normed, mate_pooled = lax.optimization_barrier((normed, mate_pooled))
    both = jnp.concatenate([normed, send(normed, MATE)], 1)
    facts = mate_pooled[0, SLOTS:, 0].astype(jnp.int32)
    mate_count, mate_valid = facts[0], facts[8]
    both_pooled = jnp.concatenate([pooled[:, :SLOTS], mate_pooled[:, :SLOTS]], 1)

    rows = order(high, rows, send(rows, ACROSS))

    def blank(shape, after):
        return lax.optimization_barrier((jnp.zeros(shape, jnp.bfloat16), after))[0]

    def second(block, axis):
        p = pos[axis]
        joined = blank((4,) + block.shape, block)
        joined = in_place(double(block, axis), (p, p ^ near, p ^ far, p ^ 2), joined)
        return joined.reshape(-1, block.shape[-1])

    def ring(block, axis):
        pieces = [block]
        for _ in range(3):
            pieces.append(send(pieces[-1], RING[axis]))
        return pieces, [(pos[axis] - sign * i) % 4 for i in range(4)]

    early = second(rows[:, : CUTS[2]], "x")
    late = second(rows[:, CUTS[2] :], "z")

    z = pos["z"]
    part_m = double(early[:, : CUTS[1]], "z")
    part_m = in_place(part_m, (z, z ^ near, z ^ far, z ^ 2), blank(part_m.shape, part_m))
    part_m = part_m.reshape(HALF, -1)
    early, part_m = lax.optimization_barrier((early, part_m))

    pieces, slots = ring(early[:, CUTS[1] :], "z")
    part_a = in_place(pieces, slots, blank((4,) + pieces[0].shape, pieces[0])).reshape(HALF, -1)

    pieces, slots = ring(late, "x")
    part_b = blank((4, 4, 4 * ROWS, late.shape[-1]), late)
    for piece, slot in zip(pieces, slots):
        piece = piece.reshape(4, 1, 4 * ROWS, -1)
        part_b = lax.dynamic_update_slice_in_dim(part_b, piece, slot, 1)
    part_b = part_b.reshape(HALF, -1)

    def project(x, own):
        other = send(own, SWAP)

        def term(side, w):
            part = lax.dynamic_index_in_dim(x, side, 0, keepdims=False)
            return jnp.dot(part, w, preferred_element_type=jnp.float32)

        return (term(core, own) + term(1 - core, other)).astype(jnp.bfloat16)

    beacon = project(both_pooled, part_m).reshape(2, SLOTS, 2 * D)
    counts = jnp.stack([count, mate_count]).astype(jnp.bfloat16)
    flags = jnp.broadcast_to(counts[:, None, None], (2, 16, D))
    block_k = jnp.concatenate([beacon[..., :D], flags], 1)
    block_v = beacon[..., D:]
    block = jnp.concatenate([block_k, block_v], 1)
    block = order(low, block[:1], block[1:])
    block = jnp.stack([block, send(block, ACROSS)])
    every_k = double(double(block[:, :, : SLOTS + 16], "x"), "z")
    every_v = double(double(block[:, :, SLOTS + 16 :], "z"), "x")
    every_k = every_k.reshape(SPANS, 2, SLOTS + 16, D)
    every_v = every_v.reshape(SPANS, 2, SLOTS, D)

    owner = jnp.arange(SPANS, dtype=jnp.int32)

    def code(axis, at):
        d = at ^ pos[axis]
        return jnp.where(d == 0, 0, jnp.where(d == near, 1, jnp.where(d == far, 2, 3)))

    code_x, code_z = code("x", owner // 8), code("z", (owner // 2) % 4)
    code_h = (owner ^ span) % 2
    at_k = (code_z * 4 + code_x) * 2 + code_h
    at_v = (code_x * 4 + code_z) * 2 + code_h
    live = every_k[:, :, SLOTS, 0].astype(jnp.int32).reshape(2 * SPANS)

    part_a = project(both, part_a)
    part_b = project(both, part_b)

    def attention(which, valid, wide):
        here = slice(which * TOK, (which + 1) * TOK)
        info = jnp.concatenate(
            [jnp.stack([span, valid, head * (HEADS * D), low ^ which]), at_k, at_v]
        )
        return attend(
            wide,
            info,
            live,
            part_a[here],
            part_b[here],
            every_k,
            every_v,
        )

    away = send(attention(1, mate_valid, False), MATE)
    home = attention(0, valid, True)
    full = lax.dynamic_update_slice(home, away, (0, (1 - head) * (HEADS * D)))
    return full[None]


def solution(mesh):
    return jax.shard_map(
        on_device,
        mesh=mesh,
        in_specs=(
            P("dp", "ctx", None),
            P(),
            P(("dp", "ctx"), None),
            P(("dp", "ctx"), None),
            P(("dp", "ctx"), None),
            P(("dp", "ctx"), None),
            P(("dp", "ctx"), None),
            P("dp", "ctx"),
            P("dp"),
        ),
        out_specs=P("dp", "ctx", None),
        check_vma=False,
    )
```

```python
import functools
import math

import jax
import jax.numpy as jnp
import numpy as np
from jax import lax
from jax.experimental import pallas as pl
from jax.experimental.pallas import tpu as pltpu
from jax.sharding import PartitionSpec as P

HEADS = 7
D = 128
WIDTH = 3584
ROWS = 28
TOK = 256
SLOTS = 64
SPANS = 32
EPS = 1e-6
FILL = -1e30
AXES = ("dp", "ctx")
SCALE = 1.0 / math.sqrt(D)


def device_id(x, y, z, c):
    return ((y % 2) * 2 + c) * 32 + (x * 4 + z) * 2 + y // 2


def make_perm(f):
    pairs = []
    for x in range(4):
        for y in range(4):
            for z in range(4):
                for c in range(2):
                    tx, ty, tz, tc = f(x, y, z, c)
                    pairs.append(
                        (device_id(x, y, z, c), device_id(tx % 4, ty % 4, tz % 4, tc % 2))
                    )
    return pairs


SWAP = make_perm(lambda x, y, z, c: (x, y, z, 1 - c))
MATE = make_perm(lambda x, y, z, c: (x, y ^ 1, z, c))
ACROSS = make_perm(lambda x, y, z, c: (x, y ^ 3, z, c))
RING = {
    "x": make_perm(lambda x, y, z, c: (x + 1 - 2 * c, y, z, c)),
    "z": make_perm(lambda x, y, z, c: (x, y, z + 1 - 2 * c, c)),
}


def flip(axis, turn):
    def partner(x, y, z, c):
        at = {"x": x, "y": y, "z": z}
        at[axis] ^= 1 if (c + turn) % 2 == 0 else 3
        return at["x"], at["y"], at["z"], c

    return make_perm(partner)


FLIP = {(axis, turn): flip(axis, turn) for axis in "xz" for turn in (0, 1)}

CUTS = (0, 256, 640, 1408)
KEPT = 1
HALF = WIDTH // 2


def send(value, pairs):
    return lax.ppermute(value, AXES, pairs)


def feature_runs():
    starts = []
    for c in range(2):
        for z in range(4):
            for x in range(4):
                for y in (0, 1, 2, 3):
                    starts.append(device_id(x, y, z, c) * ROWS)
    source = np.concatenate([np.arange(s, s + ROWS) for s in starts])
    tiles = []
    for tile in range(WIDTH // 128):
        part = source[tile * 128 : (tile + 1) * 128]
        runs = []
        lane = 0
        while lane < 128:
            end = lane + 1
            while end < 128 and part[end] == part[end - 1] + 1 and part[end] % 128 != 0:
                end += 1
            runs.append((lane, end, int(part[lane])))
            lane = end
        tiles.append(runs)
    return tiles


def reorder(plain_ref, out_ref, count, out_rows):
    lane = lax.broadcasted_iota(jnp.int32, (count, 128), 1)
    for tile, runs in enumerate(feature_runs()):
        joined = jnp.zeros((count, 128), jnp.float32)
        for first, end, feature in runs:
            block, offset = divmod(feature, 128)
            piece = plain_ref[:, block * 128 : (block + 1) * 128]
            shift = (first - offset) % 128
            if shift:
                piece = pltpu.roll(piece, shift, 1)
            joined = jnp.where((lane >= first) & (lane < end), piece, joined)
        side, column = divmod(tile, HALF // 128)
        out_ref[side, out_rows, column * 128 : (column + 1) * 128] = joined.astype(jnp.bfloat16)


def norm_body(fact_ref, tokens_ref, gain_ref, out_ref, pool_ref, plain_ref, normed_ref):
    rows = 64
    level, valid, count = fact_ref[0], fact_ref[1], fact_ref[2]

    @pl.loop(0, TOK // rows)
    def _(step):
        here = pl.ds(pl.multiple_of(step * rows, rows), rows)
        values = tokens_ref[here, :].astype(jnp.float32)
        factor = lax.rsqrt(jnp.mean(values * values, axis=-1, keepdims=True) + EPS)
        plain_ref[...] = values * factor * gain_ref[...]
        normed_ref[here, :] = plain_ref[...].astype(jnp.bfloat16)
        reorder(plain_ref, out_ref, rows, here)

    shift = level + 2
    live = jnp.right_shift(TOK, shift)
    slot = lax.broadcasted_iota(jnp.int32, (SLOTS, TOK), 0)
    position = lax.broadcasted_iota(jnp.int32, (SLOTS, TOK), 1)
    inside = (jnp.right_shift(position, shift) == slot) & (slot < live) & (position < valid)
    window = jnp.where(inside, 1.0, 0.0)
    size = jnp.maximum(jnp.sum(window, axis=1, keepdims=True), 1.0)
    sums = jnp.dot(
        window.astype(jnp.bfloat16), normed_ref[...], preferred_element_type=jnp.float32
    )
    plain_ref[...] = sums / size
    reorder(plain_ref, pool_ref, SLOTS, pl.ds(0, SLOTS))
    row = lax.broadcasted_iota(jnp.int32, (16, HALF), 0)
    facts = jnp.where(row < 8, count, valid).astype(jnp.float32).astype(jnp.bfloat16)
    for side in range(2):
        pool_ref[side, pl.ds(SLOTS, 16), :] = facts


def norm_rows(facts, tokens, gain):
    vmem = pl.BlockSpec(memory_space=pltpu.VMEM)
    return pl.pallas_call(
        norm_body,
        out_shape=[
            jax.ShapeDtypeStruct((2, TOK, HALF), jnp.bfloat16),
            jax.ShapeDtypeStruct((2, SLOTS + 16, HALF), jnp.bfloat16),
        ],
        in_specs=[pl.BlockSpec(memory_space=pltpu.SMEM), vmem, vmem],
        out_specs=[vmem, vmem],
        scratch_shapes=[
            pltpu.VMEM((64, WIDTH), jnp.float32),
            pltpu.VMEM((TOK, WIDTH), jnp.bfloat16),
        ],
        compiler_params=pltpu.CompilerParams(vmem_limit_bytes=32 * 1024 * 1024),
    )(facts, tokens, gain.reshape(1, WIDTH))


BLOCK = 256
ROOM = SPANS * SLOTS + BLOCK
LINES = HEADS * TOK


def attend_body(wide, info_ref, count_ref, part_a_ref, part_b_ref, far_k_ref, far_v_ref, *rest):
    out_ref, query_ref, keys_ref, values_ref, bias_ref, score_ref, top_ref, sum_ref, mix_ref = rest
    span, valid, column, which = info_ref[0], info_ref[1], info_ref[2], info_ref[3]

    lane = lax.broadcasted_iota(jnp.int32, (1, ROOM), 1)
    bias_ref[...] = jnp.full((1, ROOM), FILL, jnp.float32)

    def pack(i, at):
        place_k, place_v = info_ref[4 + i], info_ref[4 + SPANS + i]
        count = count_ref[place_k * 2 + which]
        here = pl.ds(pl.multiple_of(at, 16), SLOTS)
        keys_ref[here, :] = far_k_ref[place_k, which, :SLOTS, :]
        values_ref[here, :] = far_v_ref[place_v, which]
        bias_ref[...] = jnp.where((lane >= at) & (lane < at + count), 0.0, bias_ref[...])
        return at + ((count + 15) // 16) * 16

    used = lax.fori_loop(0, span, pack, jnp.int32(0))
    rest_rows = pl.ds(pl.multiple_of(used, 16), BLOCK)
    keys_ref[rest_rows, :] = jnp.zeros((BLOCK, D), jnp.bfloat16)
    values_ref[rest_rows, :] = jnp.zeros((BLOCK, D), jnp.bfloat16)
    blocks = (used + BLOCK - 1) // BLOCK

    power = SCALE * math.log2(math.e)
    contract = (((1,), (1,)), ((), ()))

    def fold(op, scores):
        out = scores[:, :D]
        for i in range(1, scores.shape[1] // D):
            out = op(out, scores[:, i * D : (i + 1) * D])
        return out

    row = lax.broadcasted_iota(jnp.int32, (TOK, TOK), 0)
    col = lax.broadcasted_iota(jnp.int32, (TOK, TOK), 1)
    near_bias = jnp.where((col <= row) & (col < valid), 0.0, FILL)
    for head in range(HEADS):
        here = slice(head * TOK, (head + 1) * TOK)
        if head < KEPT:
            query = part_a_ref[:, (2 + head) * D : (3 + head) * D]
        else:
            query = part_b_ref[:, (head - KEPT) * D : (head - KEPT + 1) * D]
        query_ref[here, :] = query
        near = lax.dot_general(
            query, part_a_ref[:, :D], contract, preferred_element_type=jnp.float32
        )
        near = near + near_bias
        score_ref[here, ROOM:] = near
        top_ref[here, :] = fold(jnp.maximum, near)

    def score(i, carry):
        here = pl.ds(pl.multiple_of(i * BLOCK, BLOCK), BLOCK)
        bias = bias_ref[:, here]
        for head in range(HEADS):
            lines = slice(head * TOK, (head + 1) * TOK)
            far = lax.dot_general(
                query_ref[lines, :],
                keys_ref[here, :],
                contract,
                preferred_element_type=jnp.float32,
            )
            far = far + bias
            score_ref[lines, here] = far
            top_ref[lines, :] = jnp.maximum(top_ref[lines, :], fold(jnp.maximum, far))
        return carry

    lax.fori_loop(0, blocks, score, jnp.int32(0))

    for head in range(HEADS):
        lines = slice(head * TOK, (head + 1) * TOK)
        top = jnp.max(top_ref[lines, :], axis=1, keepdims=True)
        top_ref[lines, :] = jnp.broadcast_to(top, (TOK, D))
        weight = jnp.exp2((score_ref[lines, ROOM:] - top) * power)
        sum_ref[lines, :] = fold(jnp.add, weight)
        mix_ref[lines, :] = jnp.dot(
            weight.astype(jnp.bfloat16),
            part_a_ref[:, D : 2 * D],
            preferred_element_type=jnp.float32,
        )

    def mix(i, carry):
        here = pl.ds(pl.multiple_of(i * BLOCK, BLOCK), BLOCK)
        for head in range(HEADS):
            lines = slice(head * TOK, (head + 1) * TOK)
            top = top_ref[lines, :]
            top = jnp.concatenate([top] * (BLOCK // D), axis=1)
            weight = jnp.exp2((score_ref[lines, here] - top) * power)
            sum_ref[lines, :] = sum_ref[lines, :] + fold(jnp.add, weight)
            mix_ref[lines, :] = mix_ref[lines, :] + jnp.dot(
                weight.astype(jnp.bfloat16), values_ref[here, :], preferred_element_type=jnp.float32
            )
        return carry

    lax.fori_loop(0, blocks, mix, jnp.int32(0))

    alive = lax.broadcasted_iota(jnp.int32, (TOK, D), 0) < valid
    for head in range(HEADS):
        lines = slice(head * TOK, (head + 1) * TOK)
        total = jnp.sum(sum_ref[lines, :], axis=1, keepdims=True)
        result = jnp.where(alive, mix_ref[lines, :] / total, 0.0).astype(jnp.bfloat16)
        if wide:
            out_ref[:, pl.ds(pl.multiple_of(column + head * D, D), D)] = result
        else:
            out_ref[:, head * D : (head + 1) * D] = result


def attend(wide, info, counts, part_a, part_b, far_k, far_v):
    columns = 2 * HEADS * D if wide else HEADS * D
    smem, vmem = pl.BlockSpec(memory_space=pltpu.SMEM), pl.BlockSpec(memory_space=pltpu.VMEM)
    return pl.pallas_call(
        functools.partial(attend_body, wide),
        out_shape=jax.ShapeDtypeStruct((TOK, columns), jnp.bfloat16),
        in_specs=[smem, smem, vmem, vmem, vmem, vmem],
        out_specs=vmem,
        scratch_shapes=[
            pltpu.VMEM((LINES, D), jnp.bfloat16),
            pltpu.VMEM((ROOM, D), jnp.bfloat16),
            pltpu.VMEM((ROOM, D), jnp.bfloat16),
            pltpu.VMEM((1, ROOM), jnp.float32),
            pltpu.VMEM((LINES, ROOM + TOK), jnp.float32),
            pltpu.VMEM((LINES, D), jnp.float32),
            pltpu.VMEM((LINES, D), jnp.float32),
            pltpu.VMEM((LINES, D), jnp.float32),
        ],
        compiler_params=pltpu.CompilerParams(vmem_limit_bytes=44 * 1024 * 1024),
    )(info, counts, part_a, part_b, far_k, far_v)


def project_body(side_ref, x_ref, own_ref, other_ref, out_ref):
    side = side_ref[0]
    columns = own_ref.shape[1]
    for first in range(0, columns, 256):
        here = slice(first, min(first + 256, columns))
        out = jnp.dot(x_ref[side], own_ref[:, here], preferred_element_type=jnp.float32)
        out += jnp.dot(x_ref[1 - side], other_ref[:, here], preferred_element_type=jnp.float32)
        out_ref[:, here] = out.astype(jnp.bfloat16)


def project_kernel(side, x, own, other):
    smem, vmem = pl.BlockSpec(memory_space=pltpu.SMEM), pl.BlockSpec(memory_space=pltpu.VMEM)
    return pl.pallas_call(
        project_body,
        out_shape=jax.ShapeDtypeStruct((x.shape[1], own.shape[1]), jnp.bfloat16),
        in_specs=[smem, vmem, vmem, vmem],
        out_specs=vmem,
        compiler_params=pltpu.CompilerParams(vmem_limit_bytes=32 * 1024 * 1024),
    )(side.reshape(1), x, own, other)


def after(value, other):
    return lax.optimization_barrier((value, other))[0]


def double(block, axis):
    pair = jnp.stack([block, send(block, FLIP[axis, 0])])
    return jnp.concatenate([pair, send(pair, FLIP[axis, 1])])


def in_place(pieces, slots, blank):
    joined = blank
    for i, slot in enumerate(slots):
        joined = lax.dynamic_update_slice_in_dim(joined, pieces[i][None], slot, 0)
    return joined


def on_device(tokens, gain, w_query, w_key, w_value, w_mark_key, w_mark_value, level, hist_len):
    dp = lax.axis_index("dp")
    span = lax.axis_index("ctx")
    core, low, high = dp % 2, dp // 2, span % 2
    head = low ^ high
    pos = {"x": span // 8, "z": (span // 2) % 4}
    sign = 1 - 2 * core
    near, far = 1 + 2 * core, 3 - 2 * core

    def order(first, one, two):
        return jnp.where(first == 0, jnp.concatenate([one, two], 0), jnp.concatenate([two, one], 0))

    def half(which):
        def cut(w, size):
            return jnp.where(which == 0, w[:, :size], w[:, size:])

        return jnp.concatenate(
            [
                cut(w_mark_key, D),
                cut(w_mark_value, D),
                cut(w_key, D),
                cut(w_value, D),
                cut(w_query, HEADS * D),
            ],
            axis=1,
        )

    mine = half(head)
    rows = order(low, mine, send(half(1 - head), MATE))

    begin = span * TOK
    stride = jnp.left_shift(jnp.int32(4), level[0, 0])
    valid = jnp.clip(hist_len[0] - begin, 0, TOK)
    count = jnp.minimum(TOK // stride, (valid + stride - 1) // stride)
    normed, pooled = norm_rows(jnp.stack([level[0, 0], valid, count]), tokens[0], gain)
    mate_pooled = send(pooled, MATE)
    both = jnp.concatenate([normed, send(normed, MATE)], 1)
    facts = mate_pooled[0, SLOTS:, 0].astype(jnp.int32)
    mate_count, mate_valid = facts[0], facts[8]
    both_pooled = jnp.concatenate([pooled[:, :SLOTS], mate_pooled[:, :SLOTS]], 1)

    rows = order(high, rows, send(rows, ACROSS))

    def blank(shape, after):
        return lax.optimization_barrier((jnp.zeros(shape, jnp.bfloat16), after))[0]

    def second(block, axis):
        p = pos[axis]
        joined = blank((4,) + block.shape, block)
        joined = in_place(double(block, axis), (p, p ^ near, p ^ far, p ^ 2), joined)
        return joined.reshape(-1, block.shape[-1])

    early = second(rows[:, : CUTS[2]], "x")
    late = second(rows[:, CUTS[2] :], "z")

    def project(x, own):
        return project_kernel(core, x, own, send(own, SWAP))

    x, z = pos["x"], pos["z"]
    corner = early[:, : CUTS[1]]
    b_0, a_0 = late, early[:, CUTS[1] :]
    pair = jnp.stack([corner, send(corner, FLIP["z", 0])])
    b_1 = send(b_0, RING["x"])
    pair_far = send(pair, FLIP["z", 1])
    part_m = in_place(
        jnp.concatenate([pair, pair_far]),
        (z, z ^ near, z ^ far, z ^ 2),
        blank((4,) + corner.shape, corner),
    ).reshape(HALF, -1)
    b_2 = send(after(b_1, pair_far), RING["x"])
    a_1 = send(after(a_0, pair_far), RING["z"])

    beacon = project(both_pooled, part_m).reshape(2, SLOTS, 2 * D)
    counts = jnp.stack([count, mate_count]).astype(jnp.bfloat16)
    flags = jnp.broadcast_to(counts[:, None, None], (2, 16, D))
    block_k = jnp.concatenate([beacon[..., :D], flags], 1)
    block_v = beacon[..., D:]
    block = jnp.concatenate([block_k, block_v], 1)
    block = order(low, block[:1], block[1:])
    a_2 = send(after(a_1, block), RING["z"])
    across = send(block, ACROSS)
    b_3 = send(after(b_2, across), RING["x"])
    block = jnp.stack([block, across])
    pair_k, pair_v = block[:, :, : SLOTS + 16], block[:, :, SLOTS + 16 :]
    pair_k = jnp.stack([pair_k, send(pair_k, FLIP["x", 0])])
    pair_v = jnp.stack([pair_v, send(pair_v, FLIP["z", 0])])
    a_3 = send(after(a_2, (pair_k, pair_v)), RING["z"])
    half_k = jnp.concatenate([pair_k, send(pair_k, FLIP["x", 1])])
    half_v = jnp.concatenate([pair_v, send(pair_v, FLIP["z", 1])])
    every_k = double(half_k, "z")
    every_v = double(half_v, "x")
    every_k = every_k.reshape(SPANS, 2, SLOTS + 16, D)
    every_v = every_v.reshape(SPANS, 2, SLOTS, D)

    owner = jnp.arange(SPANS, dtype=jnp.int32)

    def code(axis, at):
        d = at ^ pos[axis]
        return jnp.where(d == 0, 0, jnp.where(d == near, 1, jnp.where(d == far, 2, 3)))

    code_x, code_z = code("x", owner // 8), code("z", (owner // 2) % 4)
    code_h = (owner ^ span) % 2
    at_k = (code_z * 4 + code_x) * 2 + code_h
    at_v = (code_x * 4 + code_z) * 2 + code_h
    live = every_k[:, :, SLOTS, 0].astype(jnp.int32).reshape(2 * SPANS)

    pieces = [a_0, a_1, a_2, a_3]
    part_a = blank((4,) + a_0.shape, a_0)
    part_a = in_place(pieces, [(z - sign * i) % 4 for i in range(4)], part_a)
    part_b = blank((4, 4, 4 * ROWS, late.shape[-1]), b_0)
    for i, piece in enumerate([b_0, b_1, b_2, b_3]):
        piece = piece.reshape(4, 1, 4 * ROWS, -1)
        part_b = lax.dynamic_update_slice_in_dim(part_b, piece, (x - sign * i) % 4, 1)
    part_a = project(both, part_a.reshape(HALF, -1))
    part_b = project(both, part_b.reshape(HALF, -1))

    def attention(which, valid, wide):
        here = slice(which * TOK, (which + 1) * TOK)
        info = jnp.concatenate(
            [jnp.stack([span, valid, head * (HEADS * D), low ^ which]), at_k, at_v]
        )
        return attend(
            wide,
            info,
            live,
            part_a[here],
            part_b[here],
            every_k,
            every_v,
        )

    away = send(attention(1, mate_valid, False), MATE)
    home = attention(0, valid, True)
    full = lax.dynamic_update_slice(home, away, (0, (1 - head) * (HEADS * D)))
    return full[None]


def solution(mesh):
    return jax.shard_map(
        on_device,
        mesh=mesh,
        in_specs=(
            P("dp", "ctx", None),
            P(),
            P(("dp", "ctx"), None),
            P(("dp", "ctx"), None),
            P(("dp", "ctx"), None),
            P(("dp", "ctx"), None),
            P(("dp", "ctx"), None),
            P("dp", "ctx"),
            P("dp"),
        ),
        out_specs=P("dp", "ctx", None),
        check_vma=False,
    )
```

```python
import functools
import math

import jax
import jax.numpy as jnp
import numpy as np
from jax import lax
from jax.experimental import pallas as pl
from jax.experimental.pallas import tpu as pltpu
from jax.sharding import PartitionSpec as P

HEADS = 7
D = 128
WIDTH = 3584
ROWS = 28
TOK = 256
SLOTS = 64
SPANS = 32
EPS = 1e-6
FILL = -1e30
AXES = ("dp", "ctx")
SCALE = 1.0 / math.sqrt(D)


def device_id(x, y, z, c):
    return ((y % 2) * 2 + c) * 32 + (x * 4 + z) * 2 + y // 2


def make_perm(f):
    pairs = []
    for x in range(4):
        for y in range(4):
            for z in range(4):
                for c in range(2):
                    tx, ty, tz, tc = f(x, y, z, c)
                    pairs.append(
                        (device_id(x, y, z, c), device_id(tx % 4, ty % 4, tz % 4, tc % 2))
                    )
    return pairs


SWAP = make_perm(lambda x, y, z, c: (x, y, z, 1 - c))
MATE = make_perm(lambda x, y, z, c: (x, y ^ 1, z, c))
ACROSS = make_perm(lambda x, y, z, c: (x, y ^ 3, z, c))

def flip(axis, turn):
    def partner(x, y, z, c):
        at = {"x": x, "y": y, "z": z}
        at[axis] ^= 1 if (c + turn) % 2 == 0 else 3
        return at["x"], at["y"], at["z"], c

    return make_perm(partner)


FLIP = {(axis, turn): flip(axis, turn) for axis in "xz" for turn in (0, 1)}

EARLY = 2 * D
LATE = (2 + HEADS) * D
SLAB = WIDTH // 4
PAIRED = ((0, 1, 2, 3), (0, 3, 1, 2))


def send(value, pairs):
    return lax.ppermute(value, AXES, pairs)


def feature_runs(last):
    starts = []
    for c in range(2):
        for i in PAIRED[c]:
            for j in range(4):
                for y in range(4):
                    x, z = (i, j) if last == "x" else (j, i)
                    starts.append(device_id(x, y, z, c) * ROWS)
    source = np.concatenate([np.arange(s, s + ROWS) for s in starts])
    tiles = []
    for tile in range(WIDTH // 128):
        part = source[tile * 128 : (tile + 1) * 128]
        runs = []
        lane = 0
        while lane < 128:
            end = lane + 1
            while end < 128 and part[end] == part[end - 1] + 1 and part[end] % 128 != 0:
                end += 1
            runs.append((lane, end, int(part[lane])))
            lane = end
        tiles.append(runs)
    return tiles


def reorder(plain_ref, out_ref, last, count, out_rows):
    lane = lax.broadcasted_iota(jnp.int32, (count, 128), 1)
    for tile, runs in enumerate(feature_runs(last)):
        joined = jnp.zeros((count, 128), jnp.float32)
        for first, end, feature in runs:
            block, offset = divmod(feature, 128)
            piece = plain_ref[:, block * 128 : (block + 1) * 128]
            shift = (first - offset) % 128
            if shift:
                piece = pltpu.roll(piece, shift, 1)
            joined = jnp.where((lane >= first) & (lane < end), piece, joined)
        slab, column = divmod(tile, SLAB // 128)
        out_ref[slab, out_rows, column * 128 : (column + 1) * 128] = joined.astype(jnp.bfloat16)


def norm_body(fact_ref, tokens_ref, gain_ref, near_ref, far_ref, *scratch):
    out_ref, pool_ref, plain_ref, normed_ref = scratch
    rows = 64
    level, valid, count = fact_ref[0], fact_ref[1], fact_ref[2]

    @pl.loop(0, TOK // rows)
    def _(step):
        here = pl.ds(pl.multiple_of(step * rows, rows), rows)
        values = tokens_ref[here, :].astype(jnp.float32)
        factor = lax.rsqrt(jnp.mean(values * values, axis=-1, keepdims=True) + EPS)
        plain_ref[...] = values * factor * gain_ref[...]
        normed_ref[here, :] = plain_ref[...].astype(jnp.bfloat16)
        reorder(plain_ref, out_ref, "x", rows, here)

    shift = level + 2
    live = jnp.right_shift(TOK, shift)
    slot = lax.broadcasted_iota(jnp.int32, (SLOTS, TOK), 0)
    position = lax.broadcasted_iota(jnp.int32, (SLOTS, TOK), 1)
    inside = (jnp.right_shift(position, shift) == slot) & (slot < live) & (position < valid)
    window = jnp.where(inside, 1.0, 0.0)
    size = jnp.maximum(jnp.sum(window, axis=1, keepdims=True), 1.0)
    sums = jnp.dot(
        window.astype(jnp.bfloat16), normed_ref[...], preferred_element_type=jnp.float32
    )
    plain_ref[...] = sums / size
    reorder(plain_ref, pool_ref, "z", SLOTS, pl.ds(0, SLOTS))
    row = lax.broadcasted_iota(jnp.int32, (16, SLAB), 0)
    facts = jnp.where(row < 8, count, valid).astype(jnp.float32).astype(jnp.bfloat16)
    for i in range(2):
        near_ref[i, :TOK, :] = out_ref[fact_ref[3 + i]]
        far_ref[i] = out_ref[fact_ref[5 + i]]
        for j in range(2):
            lines = slice(TOK + j * (SLOTS + 16), TOK + j * (SLOTS + 16) + SLOTS)
            near_ref[i, lines, :] = pool_ref[2 * i + j]
            near_ref[i, lines.stop : lines.stop + 16, :] = facts


def norm_rows(facts, tokens, gain):
    vmem = pl.BlockSpec(memory_space=pltpu.VMEM)
    return pl.pallas_call(
        norm_body,
        out_shape=[
            jax.ShapeDtypeStruct((2, TOK + 2 * (SLOTS + 16), SLAB), jnp.bfloat16),
            jax.ShapeDtypeStruct((2, TOK, SLAB), jnp.bfloat16),
        ],
        in_specs=[pl.BlockSpec(memory_space=pltpu.SMEM), vmem, vmem],
        out_specs=[vmem, vmem],
        scratch_shapes=[
            pltpu.VMEM((4, TOK, SLAB), jnp.bfloat16),
            pltpu.VMEM((4, SLOTS, SLAB), jnp.bfloat16),
            pltpu.VMEM((64, WIDTH), jnp.float32),
            pltpu.VMEM((TOK, WIDTH), jnp.bfloat16),
        ],
        compiler_params=pltpu.CompilerParams(vmem_limit_bytes=16 * 1024 * 1024),
    )(facts, tokens, gain.reshape(1, WIDTH))


BLOCK = 256
ROOM = SPANS * SLOTS + BLOCK
LINES = HEADS * TOK


def attend_body(wide, info_ref, count_ref, part_ref, far_k_ref, far_v_ref, *rest):
    out_ref, query_ref, keys_ref, values_ref, bias_ref, score_ref, top_ref, sum_ref, mix_ref = rest
    span, valid, column, which = info_ref[0], info_ref[1], info_ref[2], info_ref[3]

    lane = lax.broadcasted_iota(jnp.int32, (1, ROOM), 1)
    bias_ref[...] = jnp.full((1, ROOM), FILL, jnp.float32)

    def pack(i, at):
        place_k, place_v = info_ref[4 + i], info_ref[4 + SPANS + i]
        count = count_ref[place_k * 2 + which]
        here = pl.ds(pl.multiple_of(at, 16), SLOTS)
        keys_ref[here, :] = far_k_ref[place_k, which, :SLOTS, :]
        values_ref[here, :] = far_v_ref[place_v, which]
        bias_ref[...] = jnp.where((lane >= at) & (lane < at + count), 0.0, bias_ref[...])
        return at + ((count + 15) // 16) * 16

    used = lax.fori_loop(0, span, pack, jnp.int32(0))
    rest_rows = pl.ds(pl.multiple_of(used, 16), BLOCK)
    keys_ref[rest_rows, :] = jnp.zeros((BLOCK, D), jnp.bfloat16)
    values_ref[rest_rows, :] = jnp.zeros((BLOCK, D), jnp.bfloat16)
    blocks = (used + BLOCK - 1) // BLOCK

    power = SCALE * math.log2(math.e)
    contract = (((1,), (1,)), ((), ()))

    def fold(op, scores):
        out = scores[:, :D]
        for i in range(1, scores.shape[1] // D):
            out = op(out, scores[:, i * D : (i + 1) * D])
        return out

    row = lax.broadcasted_iota(jnp.int32, (TOK, TOK), 0)
    col = lax.broadcasted_iota(jnp.int32, (TOK, TOK), 1)
    near_bias = jnp.where((col <= row) & (col < valid), 0.0, FILL)
    for head in range(HEADS):
        here = slice(head * TOK, (head + 1) * TOK)
        query = part_ref[:, (2 + head) * D : (3 + head) * D]
        query_ref[here, :] = query
        near = lax.dot_general(
            query, part_ref[:, :D], contract, preferred_element_type=jnp.float32
        )
        near = near + near_bias
        score_ref[here, ROOM:] = near
        top_ref[here, :] = fold(jnp.maximum, near)

    def score(i, carry):
        here = pl.ds(pl.multiple_of(i * BLOCK, BLOCK), BLOCK)
        bias = bias_ref[:, here]
        for head in range(HEADS):
            lines = slice(head * TOK, (head + 1) * TOK)
            far = lax.dot_general(
                query_ref[lines, :],
                keys_ref[here, :],
                contract,
                preferred_element_type=jnp.float32,
            )
            far = far + bias
            score_ref[lines, here] = far
            top_ref[lines, :] = jnp.maximum(top_ref[lines, :], fold(jnp.maximum, far))
        return carry

    lax.fori_loop(0, blocks, score, jnp.int32(0))

    for head in range(HEADS):
        lines = slice(head * TOK, (head + 1) * TOK)
        top = jnp.max(top_ref[lines, :], axis=1, keepdims=True)
        top_ref[lines, :] = jnp.broadcast_to(top, (TOK, D))
        weight = jnp.exp2((score_ref[lines, ROOM:] - top) * power)
        sum_ref[lines, :] = fold(jnp.add, weight)
        mix_ref[lines, :] = jnp.dot(
            weight.astype(jnp.bfloat16),
            part_ref[:, D : 2 * D],
            preferred_element_type=jnp.float32,
        )

    def mix(i, carry):
        here = pl.ds(pl.multiple_of(i * BLOCK, BLOCK), BLOCK)
        for head in range(HEADS):
            lines = slice(head * TOK, (head + 1) * TOK)
            top = top_ref[lines, :]
            top = jnp.concatenate([top] * (BLOCK // D), axis=1)
            weight = jnp.exp2((score_ref[lines, here] - top) * power)
            sum_ref[lines, :] = sum_ref[lines, :] + fold(jnp.add, weight)
            mix_ref[lines, :] = mix_ref[lines, :] + jnp.dot(
                weight.astype(jnp.bfloat16), values_ref[here, :], preferred_element_type=jnp.float32
            )
        return carry

    lax.fori_loop(0, blocks, mix, jnp.int32(0))

    alive = lax.broadcasted_iota(jnp.int32, (TOK, D), 0) < valid
    for head in range(HEADS):
        lines = slice(head * TOK, (head + 1) * TOK)
        total = jnp.sum(sum_ref[lines, :], axis=1, keepdims=True)
        result = jnp.where(alive, mix_ref[lines, :] / total, 0.0).astype(jnp.bfloat16)
        if wide:
            out_ref[:, pl.ds(pl.multiple_of(column + head * D, D), D)] = result
        else:
            out_ref[:, head * D : (head + 1) * D] = result


def attend(wide, info, counts, part, far_k, far_v):
    columns = 2 * HEADS * D if wide else HEADS * D
    smem, vmem = pl.BlockSpec(memory_space=pltpu.SMEM), pl.BlockSpec(memory_space=pltpu.VMEM)
    return pl.pallas_call(
        functools.partial(attend_body, wide),
        out_shape=jax.ShapeDtypeStruct((TOK, columns), jnp.bfloat16),
        in_specs=[smem, smem, vmem, vmem, vmem],
        out_specs=vmem,
        scratch_shapes=[
            pltpu.VMEM((LINES, D), jnp.bfloat16),
            pltpu.VMEM((ROOM, D), jnp.bfloat16),
            pltpu.VMEM((ROOM, D), jnp.bfloat16),
            pltpu.VMEM((1, ROOM), jnp.float32),
            pltpu.VMEM((LINES, ROOM + TOK), jnp.float32),
            pltpu.VMEM((LINES, D), jnp.float32),
            pltpu.VMEM((LINES, D), jnp.float32),
            pltpu.VMEM((LINES, D), jnp.float32),
        ],
        compiler_params=pltpu.CompilerParams(vmem_limit_bytes=28 * 1024 * 1024),
    )(info, counts, part, far_k, far_v)


def project_body(count, slab_ref, x_ref, *refs):
    weights, total_refs, out_ref = refs[:count], refs[count:-1], refs[-1]
    rows, columns = out_ref.shape
    for first in range(0, columns, 256):
        here = slice(first, min(first + 256, columns))
        out = total_refs[0][:, here] if total_refs else None
        for i in range(count):
            x = x_ref[slab_ref[i], :rows, :]
            term = jnp.dot(x, weights[i][:, here], preferred_element_type=jnp.float32)
            out = term if out is None else out + term
        out_ref[:, here] = out.astype(out_ref.dtype)


def project(slabs, x, weights, total=None, last=False, rows=TOK):
    smem, vmem = pl.BlockSpec(memory_space=pltpu.SMEM), pl.BlockSpec(memory_space=pltpu.VMEM)
    totals = () if total is None else (total,)
    dtype = jnp.bfloat16 if last else jnp.float32
    return pl.pallas_call(
        functools.partial(project_body, len(weights)),
        out_shape=jax.ShapeDtypeStruct((rows, weights[0].shape[1]), dtype),
        in_specs=[smem] + [vmem] * (1 + len(weights) + len(totals)),
        out_specs=vmem,
        compiler_params=pltpu.CompilerParams(vmem_limit_bytes=16 * 1024 * 1024),
    )(jnp.stack(slabs).astype(jnp.int32), x, *weights, *totals)


def after(value, other):
    return lax.optimization_barrier((value, other))[0]


def halves_body(head_ref, *refs):
    mine_ref, other_ref = refs[-2:]

    def copy(mine):
        at = 0
        for ref in refs[:-2]:
            size = ref.shape[1] // 2
            mine_ref[:, at : at + size] = ref[:, mine * size : (mine + 1) * size]
            other_ref[:, at : at + size] = ref[:, (1 - mine) * size : (2 - mine) * size]
            at += size

    for mine in range(2):
        pl.when(head_ref[0] == mine)(functools.partial(copy, mine))


def halves(head, *weights):
    smem, vmem = pl.BlockSpec(memory_space=pltpu.SMEM), pl.BlockSpec(memory_space=pltpu.VMEM)
    return pl.pallas_call(
        halves_body,
        out_shape=[jax.ShapeDtypeStruct((ROWS, EARLY + LATE), jnp.bfloat16)] * 2,
        in_specs=[smem] + [vmem] * len(weights),
        out_specs=[vmem, vmem],
        compiler_params=pltpu.CompilerParams(vmem_limit_bytes=4 * 1024 * 1024),
    )(head.reshape(1), *weights)


def double(block, axis):
    pair = jnp.stack([block, send(block, FLIP[axis, 0])])
    return jnp.concatenate([pair, send(pair, FLIP[axis, 1])])


def in_place(pieces, slots, blank):
    joined = blank
    for i, slot in enumerate(slots):
        joined = lax.dynamic_update_slice_in_dim(joined, pieces[i][None], slot, 0)
    return joined


def on_device(tokens, gain, w_query, w_key, w_value, w_mark_key, w_mark_value, level, hist_len):
    dp = lax.axis_index("dp")
    span = lax.axis_index("ctx")
    core, low, high = dp % 2, dp // 2, span % 2
    head = low ^ high
    pos = {"x": span // 8, "z": (span // 2) % 4}
    near, far = 1 + 2 * core, 3 - 2 * core

    def order(first, one, two):
        return jnp.where(first == 0, jnp.concatenate([one, two], 0), jnp.concatenate([two, one], 0))

    mine, other = halves(head, w_mark_key, w_mark_value, w_key, w_value, w_query)
    rows = order(low, mine, send(other, MATE))

    def pair_of(axis, side):
        p = pos[axis]
        inner = jnp.logical_or(p == 1, p == 2).astype(jnp.int32)
        index = jnp.where(side == 0, p // 2, inner)
        return index, jnp.where(side == 0, p % 2, p // 2)

    def slabs(axis):
        mine, theirs = pair_of(axis, core)[0], pair_of(axis, 1 - core)[0]
        return (
            (core * 2 + mine, 2 * (1 - core) + theirs),
            (core * 2 + 1 - mine, 2 * (1 - core) + 1 - theirs),
        )

    begin = span * TOK
    stride = jnp.left_shift(jnp.int32(4), level[0, 0])
    valid = jnp.clip(hist_len[0] - begin, 0, TOK)
    count = jnp.minimum(TOK // stride, (valid + stride - 1) // stride)
    near_slots, far_slots = slabs("x")
    facts = jnp.stack([level[0, 0], valid, count, *near_slots, *far_slots]).astype(jnp.int32)
    own_near, own_far = norm_rows(facts, tokens[0], gain)
    mate_near = send(own_near, MATE)
    mate_far = send(after(own_far, mate_near), MATE)
    facts = mate_near[0, TOK + SLOTS : TOK + SLOTS + 16, 0].astype(jnp.int32)
    mate_count, mate_valid = facts[0], facts[8]

    def pooled_of(packed):
        return packed[:, TOK:].reshape(4, SLOTS + 16, SLAB)[:, :SLOTS]

    rows = order(high, rows, send(rows, ACROSS))

    def blank(shape, after):
        return lax.optimization_barrier((jnp.zeros(shape, jnp.bfloat16), after))[0]

    def second(block, axis):
        p = pos[axis]
        joined = blank((4,) + block.shape, block)
        joined = in_place(double(block, axis), (p, p ^ near, p ^ far, p ^ 2), joined)
        return joined.reshape(-1, block.shape[-1])

    early = second(rows[:, :EARLY], "x")
    late = second(rows[:, EARLY:], "z")

    early = order(pair_of("z", core)[1], early, send(early, FLIP["z", 0]))
    late = order(pair_of("x", core)[1], late, send(late, FLIP["x", 0]))
    early_far = send(early, FLIP["z", 1])
    gathered = jnp.concatenate([early, early_far], 0)
    swapped = send(gathered, SWAP)
    slab_near, slab_far = slabs("z")
    where_m = (slab_near[0], slab_far[0], slab_near[1], slab_far[1])
    pieces_m = (early, early_far, swapped[:SLAB], swapped[SLAB:])
    both_pooled = jnp.concatenate([pooled_of(own_near), pooled_of(mate_near)], 1)
    beacon = project(where_m, both_pooled, pieces_m, last=True, rows=2 * SLOTS)
    beacon = beacon.reshape(2, SLOTS, 2 * D)
    counts = jnp.stack([count, mate_count]).astype(jnp.bfloat16)
    flags = jnp.broadcast_to(counts[:, None, None], (2, 16, D))
    block_k = jnp.concatenate([beacon[..., :D], flags], 1)
    block_v = beacon[..., D:]
    block = jnp.concatenate([block_k, block_v], 1)
    block = order(low, block[:1], block[1:])
    late_far = send(after(late, block), FLIP["x", 1])
    block = jnp.stack([block, send(block, ACROSS)])
    half_k = double(block[:, :, : SLOTS + 16], "x")
    half_v = double(block[:, :, SLOTS + 16 :], "z")
    zero, one = jnp.int32(0), jnp.int32(1)
    near_w = (late, send(late, SWAP))
    own = project((zero, one), own_near, near_w)
    half_k, half_v = after((half_k, half_v), own)
    pair_k = jnp.stack([half_k, send(half_k, FLIP["z", 0])])
    pair_v = jnp.stack([half_v, send(half_v, FLIP["x", 0])])
    mate = project((zero, one), mate_near, near_w)
    pair_k, pair_v = after((pair_k, pair_v), (mate, mate_far))
    every_k = jnp.concatenate([pair_k, send(pair_k, FLIP["z", 1])])
    every_v = jnp.concatenate([pair_v, send(pair_v, FLIP["x", 1])])
    every_k = every_k.reshape(SPANS, 2, SLOTS + 16, D)
    every_v = every_v.reshape(SPANS, 2, SLOTS, D)

    owner = jnp.arange(SPANS, dtype=jnp.int32)

    def code(axis, at):
        d = at ^ pos[axis]
        return jnp.where(d == 0, 0, jnp.where(d == near, 1, jnp.where(d == far, 2, 3)))

    code_x, code_z = code("x", owner // 8), code("z", (owner // 2) % 4)
    code_h = (owner ^ span) % 2
    at_k = (code_z * 4 + code_x) * 2 + code_h
    at_v = (code_x * 4 + code_z) * 2 + code_h
    live = every_k[:, :, SLOTS, 0].astype(jnp.int32).reshape(2 * SPANS)

    own = project((zero,), own_far, (late_far,), own)
    mate = project((zero,), mate_far, (late_far,), mate)
    own, mate = lax.optimization_barrier((own, mate))
    last_w = (send(late_far, SWAP),)
    mate = project((one,), mate_far, last_w, mate, last=True)
    own = project((one,), own_far, last_w, own, last=True)

    def attention(which, valid, wide):
        info = jnp.concatenate(
            [jnp.stack([span, valid, head * (HEADS * D), low ^ which]), at_k, at_v]
        )
        return attend(
            wide,
            info,
            live,
            mate if which else own,
            every_k,
            every_v,
        )

    away = send(attention(1, mate_valid, False), MATE)
    home = attention(0, valid, True)
    full = lax.dynamic_update_slice(home, away, (0, (1 - head) * (HEADS * D)))
    return full[None]


def solution(mesh):
    return jax.shard_map(
        on_device,
        mesh=mesh,
        in_specs=(
            P("dp", "ctx", None),
            P(),
            P(("dp", "ctx"), None),
            P(("dp", "ctx"), None),
            P(("dp", "ctx"), None),
            P(("dp", "ctx"), None),
            P(("dp", "ctx"), None),
            P("dp", "ctx"),
            P("dp"),
        ),
        out_specs=P("dp", "ctx", None),
        check_vma=False,
    )
```

```python
import functools
import math

import jax
import jax.numpy as jnp
import numpy as np
from jax import lax
from jax.experimental import pallas as pl
from jax.experimental.pallas import tpu as pltpu
from jax.sharding import PartitionSpec as P

HEADS = 7
D = 128
WIDTH = 3584
ROWS = 28
TOK = 256
SLOTS = 64
SPANS = 32
EPS = 1e-6
FILL = -1e30
AXES = ("dp", "ctx")
SCALE = 1.0 / math.sqrt(D)


def device_id(x, y, z, c):
    return ((y % 2) * 2 + c) * 32 + (x * 4 + z) * 2 + y // 2


def make_perm(f):
    pairs = []
    for x in range(4):
        for y in range(4):
            for z in range(4):
                for c in range(2):
                    tx, ty, tz, tc = f(x, y, z, c)
                    pairs.append(
                        (device_id(x, y, z, c), device_id(tx % 4, ty % 4, tz % 4, tc % 2))
                    )
    return pairs


SWAP = make_perm(lambda x, y, z, c: (x, y, z, 1 - c))
MATE = make_perm(lambda x, y, z, c: (x, y ^ 1, z, c))
ACROSS = make_perm(lambda x, y, z, c: (x, y ^ 3, z, c))

def flip(axis, turn):
    def partner(x, y, z, c):
        at = {"x": x, "y": y, "z": z}
        at[axis] ^= 1 if (c + turn) % 2 == 0 else 3
        return at["x"], at["y"], at["z"], c

    return make_perm(partner)


FLIP = {(axis, turn): flip(axis, turn) for axis in "xz" for turn in (0, 1)}

KEPT = 2
CUTS = (0, 2 * D, (4 + KEPT) * D, (4 + HEADS) * D)
SLAB = WIDTH // 4
PAIRED = ((0, 1, 2, 3), (0, 3, 1, 2))


def send(value, pairs):
    return lax.ppermute(value, AXES, pairs)


def feature_runs(last):
    starts = []
    for c in range(2):
        for i in PAIRED[c]:
            for j in range(4):
                for y in range(4):
                    x, z = (i, j) if last == "x" else (j, i)
                    starts.append(device_id(x, y, z, c) * ROWS)
    source = np.concatenate([np.arange(s, s + ROWS) for s in starts])
    tiles = []
    for tile in range(WIDTH // 128):
        part = source[tile * 128 : (tile + 1) * 128]
        runs = []
        lane = 0
        while lane < 128:
            end = lane + 1
            while end < 128 and part[end] == part[end - 1] + 1 and part[end] % 128 != 0:
                end += 1
            runs.append((lane, end, int(part[lane])))
            lane = end
        tiles.append(runs)
    return tiles


def reorder(plain_ref, out_ref, last, count, out_rows):
    lane = lax.broadcasted_iota(jnp.int32, (count, 128), 1)
    for tile, runs in enumerate(feature_runs(last)):
        joined = jnp.zeros((count, 128), jnp.float32)
        for first, end, feature in runs:
            block, offset = divmod(feature, 128)
            piece = plain_ref[:, block * 128 : (block + 1) * 128]
            shift = (first - offset) % 128
            if shift:
                piece = pltpu.roll(piece, shift, 1)
            joined = jnp.where((lane >= first) & (lane < end), piece, joined)
        slab, column = divmod(tile, SLAB // 128)
        out_ref[slab, out_rows, column * 128 : (column + 1) * 128] = joined.astype(jnp.bfloat16)


def norm_body(fact_ref, tokens_ref, gain_ref, near_ref, far_ref, *scratch):
    out_ref, pool_ref, plain_ref, normed_ref = scratch
    rows = 64
    level, valid, count = fact_ref[0], fact_ref[1], fact_ref[2]

    @pl.loop(0, TOK // rows)
    def _(step):
        here = pl.ds(pl.multiple_of(step * rows, rows), rows)
        values = tokens_ref[here, :].astype(jnp.float32)
        factor = lax.rsqrt(jnp.mean(values * values, axis=-1, keepdims=True) + EPS)
        plain_ref[...] = values * factor * gain_ref[...]
        normed_ref[here, :] = plain_ref[...].astype(jnp.bfloat16)
        reorder(plain_ref, out_ref, "x", rows, here)

    shift = level + 2
    live = jnp.right_shift(TOK, shift)
    slot = lax.broadcasted_iota(jnp.int32, (SLOTS, TOK), 0)
    position = lax.broadcasted_iota(jnp.int32, (SLOTS, TOK), 1)
    inside = (jnp.right_shift(position, shift) == slot) & (slot < live) & (position < valid)
    window = jnp.where(inside, 1.0, 0.0)
    size = jnp.maximum(jnp.sum(window, axis=1, keepdims=True), 1.0)
    sums = jnp.dot(
        window.astype(jnp.bfloat16), normed_ref[...], preferred_element_type=jnp.float32
    )
    plain_ref[...] = sums / size
    reorder(plain_ref, pool_ref, "z", SLOTS, pl.ds(0, SLOTS))
    row = lax.broadcasted_iota(jnp.int32, (16, SLAB), 0)
    facts = jnp.where(row < 8, count, valid).astype(jnp.float32).astype(jnp.bfloat16)
    for i in range(2):
        near_ref[i, :TOK, :] = out_ref[fact_ref[3 + i]]
        far_ref[i] = out_ref[fact_ref[5 + i]]
        for j in range(2):
            lines = slice(TOK + j * (SLOTS + 16), TOK + j * (SLOTS + 16) + SLOTS)
            near_ref[i, lines, :] = pool_ref[2 * i + j]
            near_ref[i, lines.stop : lines.stop + 16, :] = facts


def norm_rows(facts, tokens, gain):
    vmem = pl.BlockSpec(memory_space=pltpu.VMEM)
    return pl.pallas_call(
        norm_body,
        out_shape=[
            jax.ShapeDtypeStruct((2, TOK + 2 * (SLOTS + 16), SLAB), jnp.bfloat16),
            jax.ShapeDtypeStruct((2, TOK, SLAB), jnp.bfloat16),
        ],
        in_specs=[pl.BlockSpec(memory_space=pltpu.SMEM), vmem, vmem],
        out_specs=[vmem, vmem],
        scratch_shapes=[
            pltpu.VMEM((4, TOK, SLAB), jnp.bfloat16),
            pltpu.VMEM((4, SLOTS, SLAB), jnp.bfloat16),
            pltpu.VMEM((64, WIDTH), jnp.float32),
            pltpu.VMEM((TOK, WIDTH), jnp.bfloat16),
        ],
        compiler_params=pltpu.CompilerParams(vmem_limit_bytes=16 * 1024 * 1024),
    )(facts, tokens, gain.reshape(1, WIDTH))


BLOCK = 256
ROOM = SPANS * SLOTS + BLOCK
LINES = HEADS * TOK


def attend_body(wide, info_ref, count_ref, part_ref, more_ref, far_k_ref, far_v_ref, *rest):
    out_ref, query_ref, keys_ref, values_ref, bias_ref, score_ref, top_ref, sum_ref, mix_ref = rest
    span, valid, column, which = info_ref[0], info_ref[1], info_ref[2], info_ref[3]
    own = slice(0, TOK) if wide else slice(TOK, 2 * TOK)

    lane = lax.broadcasted_iota(jnp.int32, (1, ROOM), 1)
    bias_ref[...] = jnp.full((1, ROOM), FILL, jnp.float32)

    def pack(i, at):
        place_k, place_v = info_ref[4 + i], info_ref[4 + SPANS + i]
        count = count_ref[place_k * 2 + which]
        here = pl.ds(pl.multiple_of(at, 16), SLOTS)
        keys_ref[here, :] = far_k_ref[place_k, which, :SLOTS, :]
        values_ref[here, :] = far_v_ref[place_v, which]
        bias_ref[...] = jnp.where((lane >= at) & (lane < at + count), 0.0, bias_ref[...])
        return at + ((count + 15) // 16) * 16

    used = lax.fori_loop(0, span, pack, jnp.int32(0))
    rest_rows = pl.ds(pl.multiple_of(used, 16), BLOCK)
    keys_ref[rest_rows, :] = jnp.zeros((BLOCK, D), jnp.bfloat16)
    values_ref[rest_rows, :] = jnp.zeros((BLOCK, D), jnp.bfloat16)
    blocks = (used + BLOCK - 1) // BLOCK

    power = SCALE * math.log2(math.e)
    contract = (((1,), (1,)), ((), ()))

    def fold(op, scores):
        out = scores[:, :D]
        for i in range(1, scores.shape[1] // D):
            out = op(out, scores[:, i * D : (i + 1) * D])
        return out

    row = lax.broadcasted_iota(jnp.int32, (TOK, TOK), 0)
    col = lax.broadcasted_iota(jnp.int32, (TOK, TOK), 1)
    near_bias = jnp.where((col <= row) & (col < valid), 0.0, FILL)
    for head in range(HEADS):
        here = slice(head * TOK, (head + 1) * TOK)
        if head < KEPT:
            query = part_ref[own, (2 + head) * D : (3 + head) * D]
        else:
            query = more_ref[:, (head - KEPT) * D : (head - KEPT + 1) * D]
        query_ref[here, :] = query
        near = lax.dot_general(
            query, part_ref[own, :D], contract, preferred_element_type=jnp.float32
        )
        near = near + near_bias
        score_ref[here, ROOM:] = near
        top_ref[here, :] = fold(jnp.maximum, near)

    def score(i, carry):
        here = pl.ds(pl.multiple_of(i * BLOCK, BLOCK), BLOCK)
        bias = bias_ref[:, here]
        for head in range(HEADS):
            lines = slice(head * TOK, (head + 1) * TOK)
            far = lax.dot_general(
                query_ref[lines, :],
                keys_ref[here, :],
                contract,
                preferred_element_type=jnp.float32,
            )
            far = far + bias
            score_ref[lines, here] = far
            top_ref[lines, :] = jnp.maximum(top_ref[lines, :], fold(jnp.maximum, far))
        return carry

    lax.fori_loop(0, blocks, score, jnp.int32(0))

    for head in range(HEADS):
        lines = slice(head * TOK, (head + 1) * TOK)
        top = jnp.max(top_ref[lines, :], axis=1, keepdims=True)
        top_ref[lines, :] = jnp.broadcast_to(top, (TOK, D))
        weight = jnp.exp2((score_ref[lines, ROOM:] - top) * power)
        sum_ref[lines, :] = fold(jnp.add, weight)
        mix_ref[lines, :] = jnp.dot(
            weight.astype(jnp.bfloat16),
            part_ref[own, D : 2 * D],
            preferred_element_type=jnp.float32,
        )

    def mix(i, carry):
        here = pl.ds(pl.multiple_of(i * BLOCK, BLOCK), BLOCK)
        for head in range(HEADS):
            lines = slice(head * TOK, (head + 1) * TOK)
            top = top_ref[lines, :]
            top = jnp.concatenate([top] * (BLOCK // D), axis=1)
            weight = jnp.exp2((score_ref[lines, here] - top) * power)
            sum_ref[lines, :] = sum_ref[lines, :] + fold(jnp.add, weight)
            mix_ref[lines, :] = mix_ref[lines, :] + jnp.dot(
                weight.astype(jnp.bfloat16), values_ref[here, :], preferred_element_type=jnp.float32
            )
        return carry

    lax.fori_loop(0, blocks, mix, jnp.int32(0))

    alive = lax.broadcasted_iota(jnp.int32, (TOK, D), 0) < valid
    for head in range(HEADS):
        lines = slice(head * TOK, (head + 1) * TOK)
        total = jnp.sum(sum_ref[lines, :], axis=1, keepdims=True)
        result = jnp.where(alive, mix_ref[lines, :] / total, 0.0).astype(jnp.bfloat16)
        if wide:
            out_ref[:, pl.ds(pl.multiple_of(column + head * D, D), D)] = result
        else:
            out_ref[:, head * D : (head + 1) * D] = result


def attend(wide, info, counts, part, more, far_k, far_v):
    columns = 2 * HEADS * D if wide else HEADS * D
    smem, vmem = pl.BlockSpec(memory_space=pltpu.SMEM), pl.BlockSpec(memory_space=pltpu.VMEM)
    return pl.pallas_call(
        functools.partial(attend_body, wide),
        out_shape=jax.ShapeDtypeStruct((TOK, columns), jnp.bfloat16),
        in_specs=[smem, smem, vmem, vmem, vmem, vmem],
        out_specs=vmem,
        scratch_shapes=[
            pltpu.VMEM((LINES, D), jnp.bfloat16),
            pltpu.VMEM((ROOM, D), jnp.bfloat16),
            pltpu.VMEM((ROOM, D), jnp.bfloat16),
            pltpu.VMEM((1, ROOM), jnp.float32),
            pltpu.VMEM((LINES, ROOM + TOK), jnp.float32),
            pltpu.VMEM((LINES, D), jnp.float32),
            pltpu.VMEM((LINES, D), jnp.float32),
            pltpu.VMEM((LINES, D), jnp.float32),
        ],
        compiler_params=pltpu.CompilerParams(vmem_limit_bytes=28 * 1024 * 1024),
    )(info, counts, part, more, far_k, far_v)


def project_body(count, slab_ref, x_ref, *refs):
    weights, total_refs, out_ref = refs[:count], refs[count:-1], refs[-1]
    rows, columns = out_ref.shape
    for first in range(0, columns, 256):
        here = slice(first, min(first + 256, columns))
        out = total_refs[0][:, here] if total_refs else None
        for i in range(count):
            x = x_ref[slab_ref[i], :rows, :]
            term = jnp.dot(x, weights[i][:, here], preferred_element_type=jnp.float32)
            out = term if out is None else out + term
        out_ref[:, here] = out.astype(out_ref.dtype)


def project(slabs, x, weights, total=None, last=False, rows=TOK):
    smem, vmem = pl.BlockSpec(memory_space=pltpu.SMEM), pl.BlockSpec(memory_space=pltpu.VMEM)
    totals = () if total is None else (total,)
    dtype = jnp.bfloat16 if last else jnp.float32
    return pl.pallas_call(
        functools.partial(project_body, len(weights)),
        out_shape=jax.ShapeDtypeStruct((rows, weights[0].shape[1]), dtype),
        in_specs=[smem] + [vmem] * (1 + len(weights) + len(totals)),
        out_specs=vmem,
        compiler_params=pltpu.CompilerParams(vmem_limit_bytes=16 * 1024 * 1024),
    )(jnp.stack(slabs).astype(jnp.int32), x, *weights, *totals)


def crossed_body(info_ref, own_near, own_far, mate_near, mate_far, *refs):
    pieces, out_ref, full_ref = refs[:4], refs[4], refs[5]
    core = info_ref[0]
    block = 4 * ROWS
    for i, piece in enumerate(pieces):
        theirs, is_far = divmod(i, 2)
        side = core if theirs == 0 else 1 - core
        pair_x, pair_z = info_ref[1 + theirs], info_ref[3 + theirs]
        if is_far:
            pair_z = 1 - pair_z
        for t in range(2):
            split = jnp.where(pair_z == 0, PAIRED[1][t], PAIRED[1][2 + t])
            z = jnp.where(side == 0, 2 * pair_z + t, split)
            for x in range(4):
                at = jnp.where(side == 0, x, PAIRED[1].index(x))
                slab = jnp.where(at // 2 == pair_x, 0, 2) + theirs
                line = slab * SLAB + ((at % 2) * 4 + z) * block
                source = slice((t * 4 + x) * block, (t * 4 + x + 1) * block)
                full_ref[pl.ds(pl.multiple_of(line, 16), block), :] = piece[source, :]
    columns = out_ref.shape[1]
    for first in range(0, columns, 256):
        here = slice(first, first + 256)
        for j, (near_ref, far_ref) in enumerate(((own_near, own_far), (mate_near, mate_far))):
            out = None
            for slab in range(4):
                x_ref = near_ref if slab < 2 else far_ref
                w = full_ref[slab * SLAB : (slab + 1) * SLAB, here]
                term = jnp.dot(x_ref[slab % 2, :TOK, :], w, preferred_element_type=jnp.float32)
                out = term if out is None else out + term
            out_ref[j * TOK : (j + 1) * TOK, here] = out.astype(jnp.bfloat16)


def project_crossed(info, tokens, pieces):
    smem, vmem = pl.BlockSpec(memory_space=pltpu.SMEM), pl.BlockSpec(memory_space=pltpu.VMEM)
    columns = pieces[0].shape[1]
    return pl.pallas_call(
        crossed_body,
        out_shape=jax.ShapeDtypeStruct((2 * TOK, columns), jnp.bfloat16),
        in_specs=[smem] + [vmem] * 8,
        out_specs=vmem,
        scratch_shapes=[pltpu.VMEM((WIDTH, columns), jnp.bfloat16)],
        compiler_params=pltpu.CompilerParams(vmem_limit_bytes=16 * 1024 * 1024),
    )(info, *tokens, *pieces)


def after(value, other):
    return lax.optimization_barrier((value, other))[0]


def halves_body(head_ref, *refs):
    mine_ref, other_ref = refs[-2:]

    def copy(mine):
        at = 0
        for ref in refs[:-2]:
            size = ref.shape[1] // 2
            mine_ref[:, at : at + size] = ref[:, mine * size : (mine + 1) * size]
            other_ref[:, at : at + size] = ref[:, (1 - mine) * size : (2 - mine) * size]
            at += size

    for mine in range(2):
        pl.when(head_ref[0] == mine)(functools.partial(copy, mine))


def halves(head, *weights):
    smem, vmem = pl.BlockSpec(memory_space=pltpu.SMEM), pl.BlockSpec(memory_space=pltpu.VMEM)
    return pl.pallas_call(
        halves_body,
        out_shape=[jax.ShapeDtypeStruct((ROWS, CUTS[-1]), jnp.bfloat16)] * 2,
        in_specs=[smem] + [vmem] * len(weights),
        out_specs=[vmem, vmem],
        compiler_params=pltpu.CompilerParams(vmem_limit_bytes=4 * 1024 * 1024),
    )(head.reshape(1), *weights)


def double(block, axis):
    pair = jnp.stack([block, send(block, FLIP[axis, 0])])
    return jnp.concatenate([pair, send(pair, FLIP[axis, 1])])


def in_place(pieces, slots, blank):
    joined = blank
    for i, slot in enumerate(slots):
        joined = lax.dynamic_update_slice_in_dim(joined, pieces[i][None], slot, 0)
    return joined


def on_device(tokens, gain, w_query, w_key, w_value, w_mark_key, w_mark_value, level, hist_len):
    dp = lax.axis_index("dp")
    span = lax.axis_index("ctx")
    core, low, high = dp % 2, dp // 2, span % 2
    head = low ^ high
    pos = {"x": span // 8, "z": (span // 2) % 4}
    near, far = 1 + 2 * core, 3 - 2 * core

    def order(first, one, two):
        return jnp.where(first == 0, jnp.concatenate([one, two], 0), jnp.concatenate([two, one], 0))

    mine, other = halves(head, w_mark_key, w_mark_value, w_key, w_value, w_query)
    rows = order(low, mine, send(other, MATE))

    def pair_of(axis, side):
        p = pos[axis]
        inner = jnp.logical_or(p == 1, p == 2).astype(jnp.int32)
        index = jnp.where(side == 0, p // 2, inner)
        return index, jnp.where(side == 0, p % 2, p // 2)

    def slabs(axis):
        mine, theirs = pair_of(axis, core)[0], pair_of(axis, 1 - core)[0]
        return (
            (core * 2 + mine, 2 * (1 - core) + theirs),
            (core * 2 + 1 - mine, 2 * (1 - core) + 1 - theirs),
        )

    begin = span * TOK
    stride = jnp.left_shift(jnp.int32(4), level[0, 0])
    valid = jnp.clip(hist_len[0] - begin, 0, TOK)
    count = jnp.minimum(TOK // stride, (valid + stride - 1) // stride)
    near_slots, far_slots = slabs("x")
    facts = jnp.stack([level[0, 0], valid, count, *near_slots, *far_slots]).astype(jnp.int32)
    own_near, own_far = norm_rows(facts, tokens[0], gain)
    mate_near = send(own_near, MATE)
    mate_far = send(after(own_far, mate_near), MATE)
    facts = mate_near[0, TOK + SLOTS : TOK + SLOTS + 16, 0].astype(jnp.int32)
    mate_count, mate_valid = facts[0], facts[8]

    def pooled_of(packed):
        return packed[:, TOK:].reshape(4, SLOTS + 16, SLAB)[:, :SLOTS]

    rows = order(high, rows, send(rows, ACROSS))

    def blank(shape, after):
        return lax.optimization_barrier((jnp.zeros(shape, jnp.bfloat16), after))[0]

    def second(block, axis):
        p = pos[axis]
        joined = blank((4,) + block.shape, block)
        joined = in_place(double(block, axis), (p, p ^ near, p ^ far, p ^ 2), joined)
        return joined.reshape(-1, block.shape[-1])

    early = second(rows[:, : CUTS[2]], "x")
    late = second(rows[:, CUTS[2] :], "z")

    early, cross = early[:, : CUTS[1]], early[:, CUTS[1] :]
    z_second, x_second = pair_of("z", core)[1], pair_of("x", core)[1]
    early = order(z_second, early, send(early, FLIP["z", 0]))
    cross = order(z_second, cross, send(cross, FLIP["z", 0]))
    late = order(x_second, late, send(late, FLIP["x", 0]))
    early_far = send(early, FLIP["z", 1])
    cross_far = send(after(cross, early_far), FLIP["z", 1])
    late_far = send(late, FLIP["x", 1])
    gathered = jnp.concatenate([early, early_far], 0)
    swapped = send(gathered, SWAP)
    slab_near, slab_far = slabs("z")
    where_m = (slab_near[0], slab_far[0], slab_near[1], slab_far[1])
    pieces_m = (early, early_far, swapped[:SLAB], swapped[SLAB:])
    both_pooled = jnp.concatenate([pooled_of(own_near), pooled_of(mate_near)], 1)
    beacon = project(where_m, both_pooled, pieces_m, last=True, rows=2 * SLOTS)
    beacon = beacon.reshape(2, SLOTS, 2 * D)
    counts = jnp.stack([count, mate_count]).astype(jnp.bfloat16)
    flags = jnp.broadcast_to(counts[:, None, None], (2, 16, D))
    block_k = jnp.concatenate([beacon[..., :D], flags], 1)
    block_v = beacon[..., D:]
    block = jnp.concatenate([block_k, block_v], 1)
    block = order(low, block[:1], block[1:])
    block = jnp.stack([block, send(block, ACROSS)])
    half_k = double(block[:, :, : SLOTS + 16], "x")
    half_v = double(block[:, :, SLOTS + 16 :], "z")
    zero, one = jnp.int32(0), jnp.int32(1)
    near_w = (late, send(late, SWAP))
    own = project((zero, one), own_near, near_w)
    half_k, half_v = after((half_k, half_v), own)
    crossed = jnp.concatenate([cross, cross_far], 0)
    crossed, far_w = after((crossed, late_far), (half_k, half_v))
    crossed = send(crossed, SWAP)
    far_w = (far_w, send(far_w, SWAP))
    pair_k = jnp.stack([half_k, send(half_k, FLIP["z", 0])])
    pair_v = jnp.stack([half_v, send(half_v, FLIP["x", 0])])
    mate = project((zero, one), mate_near, near_w)
    pair_k, pair_v = after((pair_k, pair_v), (mate, mate_far))
    every_k = jnp.concatenate([pair_k, send(pair_k, FLIP["z", 1])])
    every_v = jnp.concatenate([pair_v, send(pair_v, FLIP["x", 1])])
    every_k = every_k.reshape(SPANS, 2, SLOTS + 16, D)
    every_v = every_v.reshape(SPANS, 2, SLOTS, D)

    owner = jnp.arange(SPANS, dtype=jnp.int32)

    def code(axis, at):
        d = at ^ pos[axis]
        return jnp.where(d == 0, 0, jnp.where(d == near, 1, jnp.where(d == far, 2, 3)))

    code_x, code_z = code("x", owner // 8), code("z", (owner // 2) % 4)
    code_h = (owner ^ span) % 2
    at_k = (code_z * 4 + code_x) * 2 + code_h
    at_v = (code_x * 4 + code_z) * 2 + code_h
    live = every_k[:, :, SLOTS, 0].astype(jnp.int32).reshape(2 * SPANS)

    pairs = [pair_of(axis, side)[0] for axis in "xz" for side in (core, 1 - core)]
    part = project_crossed(
        jnp.stack([core, *pairs]).astype(jnp.int32),
        (own_near, own_far, mate_near, mate_far),
        (cross, cross_far, crossed[:SLAB], crossed[SLAB:]),
    )
    own = project((zero, one), own_far, far_w, own, last=True)
    mate = project((zero, one), mate_far, far_w, mate, last=True)

    def attention(which, valid, wide):
        info = jnp.concatenate(
            [jnp.stack([span, valid, head * (HEADS * D), low ^ which]), at_k, at_v]
        )
        return attend(
            wide,
            info,
            live,
            part,
            mate if which else own,
            every_k,
            every_v,
        )

    away = send(attention(1, mate_valid, False), MATE)
    home = attention(0, valid, True)
    full = lax.dynamic_update_slice(home, away, (0, (1 - head) * (HEADS * D)))
    return full[None]


def solution(mesh):
    return jax.shard_map(
        on_device,
        mesh=mesh,
        in_specs=(
            P("dp", "ctx", None),
            P(),
            P(("dp", "ctx"), None),
            P(("dp", "ctx"), None),
            P(("dp", "ctx"), None),
            P(("dp", "ctx"), None),
            P(("dp", "ctx"), None),
            P("dp", "ctx"),
            P("dp"),
        ),
        out_specs=P("dp", "ctx", None),
        check_vma=False,
    )
```

```python
import functools
import math

import jax
import jax.numpy as jnp
import numpy as np
from jax import lax
from jax.experimental import pallas as pl
from jax.experimental.pallas import tpu as pltpu
from jax.sharding import PartitionSpec as P

HEADS = 7
D = 128
WIDTH = 3584
ROWS = 28
TOK = 256
SLOTS = 64
SPANS = 32
EPS = 1e-6
FILL = -1e30
AXES = ("dp", "ctx")
SCALE = 1.0 / math.sqrt(D)


def device_id(x, y, z, c):
    return ((y % 2) * 2 + c) * 32 + (x * 4 + z) * 2 + y // 2


def make_perm(f):
    pairs = []
    for x in range(4):
        for y in range(4):
            for z in range(4):
                for c in range(2):
                    tx, ty, tz, tc = f(x, y, z, c)
                    pairs.append(
                        (device_id(x, y, z, c), device_id(tx % 4, ty % 4, tz % 4, tc % 2))
                    )
    return pairs


SWAP = make_perm(lambda x, y, z, c: (x, y, z, 1 - c))
MATE = make_perm(lambda x, y, z, c: (x, y ^ 1, z, c))
ACROSS = make_perm(lambda x, y, z, c: (x, y ^ 3, z, c))

def flip(axis, turn):
    def partner(x, y, z, c):
        at = {"x": x, "y": y, "z": z}
        at[axis] ^= 1 if (c + turn) % 2 == 0 else 3
        return at["x"], at["y"], at["z"], c

    return make_perm(partner)


FLIP = {(axis, turn): flip(axis, turn) for axis in "xz" for turn in (0, 1)}

KEPT = 2
CUTS = (0, 2 * D, (4 + KEPT) * D, (4 + HEADS) * D)
SLAB = WIDTH // 4
PAIRED = ((0, 1, 2, 3), (0, 3, 1, 2))


def send(value, pairs):
    return lax.ppermute(value, AXES, pairs)


def feature_runs(last):
    starts = []
    for c in range(2):
        for i in PAIRED[c]:
            for j in range(4):
                for y in range(4):
                    x, z = (i, j) if last == "x" else (j, i)
                    starts.append(device_id(x, y, z, c) * ROWS)
    source = np.concatenate([np.arange(s, s + ROWS) for s in starts])
    tiles = []
    for tile in range(WIDTH // 128):
        part = source[tile * 128 : (tile + 1) * 128]
        runs = []
        lane = 0
        while lane < 128:
            end = lane + 1
            while end < 128 and part[end] == part[end - 1] + 1 and part[end] % 128 != 0:
                end += 1
            runs.append((lane, end, int(part[lane])))
            lane = end
        tiles.append(runs)
    return tiles


def cost(flops, moved):
    return pl.CostEstimate(flops=flops, bytes_accessed=moved, transcendentals=0)


def reorder(plain_ref, out_ref, last, count, out_rows):
    lane = lax.broadcasted_iota(jnp.int32, (count, 128), 1)
    for tile, runs in enumerate(feature_runs(last)):
        joined = jnp.zeros((count, 128), jnp.float32)
        for first, end, feature in runs:
            block, offset = divmod(feature, 128)
            piece = plain_ref[:, block * 128 : (block + 1) * 128]
            shift = (first - offset) % 128
            if shift:
                piece = pltpu.roll(piece, shift, 1)
            joined = jnp.where((lane >= first) & (lane < end), piece, joined)
        slab, column = divmod(tile, SLAB // 128)
        out_ref[slab, out_rows, column * 128 : (column + 1) * 128] = joined.astype(jnp.bfloat16)


def norm_body(fact_ref, tokens_ref, gain_ref, near_ref, far_ref, *scratch):
    out_ref, pool_ref, plain_ref, normed_ref = scratch
    rows = 64
    level, valid, count = fact_ref[0], fact_ref[1], fact_ref[2]

    @pl.loop(0, TOK // rows)
    def _(step):
        here = pl.ds(pl.multiple_of(step * rows, rows), rows)
        values = tokens_ref[here, :].astype(jnp.float32)
        factor = lax.rsqrt(jnp.mean(values * values, axis=-1, keepdims=True) + EPS)
        plain_ref[...] = values * factor * gain_ref[...].reshape(1, WIDTH)
        normed_ref[here, :] = plain_ref[...].astype(jnp.bfloat16)
        reorder(plain_ref, out_ref, "x", rows, here)

    shift = level + 2
    live = jnp.right_shift(TOK, shift)
    slot = lax.broadcasted_iota(jnp.int32, (SLOTS, TOK), 0)
    position = lax.broadcasted_iota(jnp.int32, (SLOTS, TOK), 1)
    inside = (jnp.right_shift(position, shift) == slot) & (slot < live) & (position < valid)
    window = jnp.where(inside, 1.0, 0.0)
    size = jnp.maximum(jnp.sum(window, axis=1, keepdims=True), 1.0)
    sums = jnp.dot(
        window.astype(jnp.bfloat16), normed_ref[...], preferred_element_type=jnp.float32
    )
    plain_ref[...] = sums / size
    reorder(plain_ref, pool_ref, "z", SLOTS, pl.ds(0, SLOTS))
    row = lax.broadcasted_iota(jnp.int32, (16, SLAB), 0)
    facts = jnp.where(row < 8, count, valid).astype(jnp.float32).astype(jnp.bfloat16)
    for i in range(2):
        near_ref[i, :TOK, :] = out_ref[fact_ref[3 + i]]
        far_ref[i] = out_ref[fact_ref[5 + i]]
        for j in range(2):
            lines = slice(TOK + j * (SLOTS + 16), TOK + j * (SLOTS + 16) + SLOTS)
            near_ref[i, lines, :] = pool_ref[2 * i + j]
            near_ref[i, lines.stop : lines.stop + 16, :] = facts


def norm_rows(facts, tokens, gain):
    vmem = pl.BlockSpec(memory_space=pltpu.VMEM)
    return pl.pallas_call(
        norm_body,
        out_shape=[
            jax.ShapeDtypeStruct((2, TOK + 2 * (SLOTS + 16), SLAB), jnp.bfloat16),
            jax.ShapeDtypeStruct((2, TOK, SLAB), jnp.bfloat16),
        ],
        in_specs=[pl.BlockSpec(memory_space=pltpu.SMEM), vmem, vmem],
        out_specs=[vmem, vmem],
        scratch_shapes=[
            pltpu.VMEM((4, TOK, SLAB), jnp.bfloat16),
            pltpu.VMEM((4, SLOTS, SLAB), jnp.bfloat16),
            pltpu.VMEM((64, WIDTH), jnp.float32),
            pltpu.VMEM((TOK, WIDTH), jnp.bfloat16),
        ],
        compiler_params=pltpu.CompilerParams(vmem_limit_bytes=10 * 1024 * 1024),
        cost_estimate=cost(2 * SLOTS * TOK * WIDTH, 16 * TOK * WIDTH),
    )(facts, tokens, gain)


BLOCK = 256
ROOM = SPANS * SLOTS + BLOCK
LINES = HEADS * TOK


def attend_body(wide, info_ref, count_ref, part_ref, more_ref, *rest):
    far_k_refs, far_v_refs, rest = rest[:2], rest[2:4], rest[4:]
    out_ref, query_ref, keys_ref, values_ref, bias_ref, top_ref, sum_ref, mix_ref = rest
    span, valid, column, which = info_ref[0], info_ref[1], info_ref[2], info_ref[3]
    own = slice(0, TOK) if wide else slice(TOK, 2 * TOK)

    lane = lax.broadcasted_iota(jnp.int32, (1, ROOM), 1)
    bias_ref[...] = jnp.full((1, ROOM), FILL, jnp.float32)

    def pack(i, at):
        place_k, place_v = info_ref[4 + i], info_ref[4 + SPANS + i]
        count = count_ref[place_k * 2 + which]
        here = pl.ds(pl.multiple_of(at, 16), SLOTS)
        for j in range(2):

            @pl.when(place_k // (SPANS // 2) == j)
            def _():
                keys_ref[here, :] = far_k_refs[j][place_k % (SPANS // 2), which, :SLOTS, :]

            @pl.when(place_v // (SPANS // 2) == j)
            def _():
                values_ref[here, :] = far_v_refs[j][place_v % (SPANS // 2), which]

        bias_ref[...] = jnp.where((lane >= at) & (lane < at + count), 0.0, bias_ref[...])
        return at + ((count + 15) // 16) * 16

    used = lax.fori_loop(0, span, pack, jnp.int32(0))
    rest_rows = pl.ds(pl.multiple_of(used, 16), BLOCK)
    keys_ref[rest_rows, :] = jnp.zeros((BLOCK, D), jnp.bfloat16)
    values_ref[rest_rows, :] = jnp.zeros((BLOCK, D), jnp.bfloat16)
    blocks = (used + BLOCK - 1) // BLOCK

    power = SCALE * math.log2(math.e)
    contract = (((1,), (1,)), ((), ()))

    def fold(op, scores):
        out = scores[:, :D]
        for i in range(1, scores.shape[1] // D):
            out = op(out, scores[:, i * D : (i + 1) * D])
        return out

    row = lax.broadcasted_iota(jnp.int32, (TOK, TOK), 0)
    col = lax.broadcasted_iota(jnp.int32, (TOK, TOK), 1)
    near_bias = jnp.where((col <= row) & (col < valid), 0.0, FILL)

    def near(lines):
        scores = lax.dot_general(
            query_ref[lines, :], part_ref[own, :D], contract, preferred_element_type=jnp.float32
        )
        return scores + near_bias

    for head in range(HEADS):
        here = slice(head * TOK, (head + 1) * TOK)
        if head < KEPT:
            query = part_ref[own, (2 + head) * D : (3 + head) * D]
        else:
            query = more_ref[own, (head - KEPT) * D : (head - KEPT + 1) * D]
        query_ref[here, :] = query
        top_ref[here, :] = fold(jnp.maximum, near(here))

    def far(here):
        scores = lax.dot_general(
            query_ref[...], keys_ref[here, :], contract, preferred_element_type=jnp.float32
        )
        return scores + bias_ref[:, here]

    def score(i, carry):
        here = pl.ds(pl.multiple_of(i * BLOCK, BLOCK), BLOCK)
        top_ref[...] = jnp.maximum(top_ref[...], fold(jnp.maximum, far(here)))
        return carry

    lax.fori_loop(0, blocks, score, jnp.int32(0))

    for head in range(HEADS):
        lines = slice(head * TOK, (head + 1) * TOK)
        top = jnp.max(top_ref[lines, :], axis=1, keepdims=True)
        top_ref[lines, :] = jnp.broadcast_to(top, (TOK, D))
        weight = jnp.exp2((near(lines) - top) * power)
        sum_ref[lines, :] = fold(jnp.add, weight)
        mix_ref[lines, :] = jnp.dot(
            weight.astype(jnp.bfloat16),
            part_ref[own, D : 2 * D],
            preferred_element_type=jnp.float32,
        )

    def mix(i, carry):
        here = pl.ds(pl.multiple_of(i * BLOCK, BLOCK), BLOCK)
        top = jnp.concatenate([top_ref[...]] * (BLOCK // D), axis=1)
        weight = jnp.exp2((far(here) - top) * power)
        sum_ref[...] += fold(jnp.add, weight)
        mix_ref[...] += jnp.dot(
            weight.astype(jnp.bfloat16), values_ref[here, :], preferred_element_type=jnp.float32
        )
        return carry

    lax.fori_loop(0, blocks, mix, jnp.int32(0))

    alive = lax.broadcasted_iota(jnp.int32, (TOK, D), 0) < valid
    for head in range(HEADS):
        lines = slice(head * TOK, (head + 1) * TOK)
        total = jnp.sum(sum_ref[lines, :], axis=1, keepdims=True)
        result = jnp.where(alive, mix_ref[lines, :] / total, 0.0).astype(jnp.bfloat16)
        if wide:
            out_ref[:, pl.ds(pl.multiple_of(column + head * D, D), D)] = result
        else:
            out_ref[:, head * D : (head + 1) * D] = result


def attend(wide, info, counts, part, more, far):
    columns = 2 * HEADS * D if wide else HEADS * D
    smem, vmem = pl.BlockSpec(memory_space=pltpu.SMEM), pl.BlockSpec(memory_space=pltpu.VMEM)
    return pl.pallas_call(
        functools.partial(attend_body, wide),
        out_shape=jax.ShapeDtypeStruct((TOK, columns), jnp.bfloat16),
        in_specs=[smem, smem] + [vmem] * 6,
        out_specs=vmem,
        scratch_shapes=[
            pltpu.VMEM((LINES, D), jnp.bfloat16),
            pltpu.VMEM((ROOM, D), jnp.bfloat16),
            pltpu.VMEM((ROOM, D), jnp.bfloat16),
            pltpu.VMEM((1, ROOM), jnp.float32),
            pltpu.VMEM((LINES, D), jnp.float32),
            pltpu.VMEM((LINES, D), jnp.float32),
            pltpu.VMEM((LINES, D), jnp.float32),
        ],
        compiler_params=pltpu.CompilerParams(vmem_limit_bytes=14 * 1024 * 1024),
        cost_estimate=cost(4 * LINES * D * 1280, 8 << 20),
    )(info, counts, part, more, *far)


def project_body(slab_ref, x_ref, *refs):
    weights, out_ref = refs[:-1], refs[-1]
    rows, columns = out_ref.shape
    for first in range(0, columns, 256):
        here = slice(first, min(first + 256, columns))
        out, slab = None, 0
        for w in weights:
            for start in range(0, w.shape[0], SLAB):
                x = x_ref[slab_ref[slab], :rows, :]
                term = jnp.dot(
                    x, w[start : start + SLAB, here], preferred_element_type=jnp.float32
                )
                out = term if out is None else out + term
                slab += 1
        out_ref[:, here] = out.astype(out_ref.dtype)


def project(slabs, x, weights):
    smem, vmem = pl.BlockSpec(memory_space=pltpu.SMEM), pl.BlockSpec(memory_space=pltpu.VMEM)
    rows, columns = x.shape[1], weights[0].shape[1]
    return pl.pallas_call(
        project_body,
        out_shape=jax.ShapeDtypeStruct((rows, columns), jnp.bfloat16),
        in_specs=[smem] + [vmem] * (1 + len(weights)),
        out_specs=vmem,
        compiler_params=pltpu.CompilerParams(vmem_limit_bytes=10 * 1024 * 1024),
        cost_estimate=cost(2 * rows * WIDTH * columns, 2 * WIDTH * (rows + columns)),
    )(jnp.stack(slabs).astype(jnp.int32), x, *weights)


def span_body(crossed, info_ref, own_near, own_far, mate_near, mate_far, *refs):
    pieces, out_ref, full_ref = [(w, 0) for w in refs[:4]], refs[4], refs[5]
    if crossed:
        core = info_ref[0]
        block = 4 * ROWS
        for i, (piece, start) in enumerate(pieces):
            theirs, is_far = divmod(i, 2)
            side = core if theirs == 0 else 1 - core
            pair_x, pair_z = info_ref[1 + theirs], info_ref[3 + theirs]
            if is_far:
                pair_z = 1 - pair_z
            for t in range(2):
                split = jnp.where(pair_z == 0, PAIRED[1][t], PAIRED[1][2 + t])
                z = jnp.where(side == 0, 2 * pair_z + t, split)
                for x in range(4):
                    at = jnp.where(side == 0, x, PAIRED[1].index(x))
                    slab = jnp.where(at // 2 == pair_x, 0, 2) + theirs
                    line = slab * SLAB + ((at % 2) * 4 + z) * block
                    source = start + (t * 4 + x) * block
                    full_ref[pl.ds(pl.multiple_of(line, 16), block), :] = piece[
                        source : source + block, :
                    ]
        pieces = [(full_ref, slab * SLAB) for slab in range(4)]
    else:
        pieces = [pieces[0], pieces[2], pieces[1], pieces[3]]
    columns = out_ref.shape[1]
    for first in range(0, columns, 256):
        here = slice(first, min(first + 256, columns))
        for j, (near_ref, far_ref) in enumerate(((own_near, own_far), (mate_near, mate_far))):
            out = None
            for slab, (piece, start) in enumerate(pieces):
                x = (near_ref if slab < 2 else far_ref)[slab % 2, :TOK, :]
                w = piece[start : start + SLAB, here]
                term = jnp.dot(x, w, preferred_element_type=jnp.float32)
                out = term if out is None else out + term
            out_ref[j * TOK : (j + 1) * TOK, here] = out.astype(jnp.bfloat16)


def project_spans(crossed, info, tokens, pieces):
    smem, vmem = pl.BlockSpec(memory_space=pltpu.SMEM), pl.BlockSpec(memory_space=pltpu.VMEM)
    columns = pieces[0].shape[1]
    lines = WIDTH if crossed else 16
    return pl.pallas_call(
        functools.partial(span_body, crossed),
        out_shape=jax.ShapeDtypeStruct((2 * TOK, columns), jnp.bfloat16),
        in_specs=[smem] + [vmem] * 8,
        out_specs=vmem,
        scratch_shapes=[pltpu.VMEM((lines, columns), jnp.bfloat16)],
        compiler_params=pltpu.CompilerParams(vmem_limit_bytes=10 * 1024 * 1024),
        cost_estimate=cost(4 * TOK * WIDTH * columns, 2 * WIDTH * (2 * TOK + columns)),
    )(info, *tokens, *pieces)


def after(value, other):
    return lax.optimization_barrier((value, other))[0]


def halves_body(head_ref, *refs):
    count = (len(refs) - 3) // 2
    sources, (mine_ref, other_ref), held, sem = (
        refs[:count],
        refs[count : count + 2],
        refs[count + 2 : -1],
        refs[-1],
    )
    copies = [pltpu.make_async_copy(a, b, sem.at[i]) for i, (a, b) in enumerate(zip(sources, held))]
    for c in copies:
        c.start()
    for c in copies:
        c.wait()

    def copy(mine):
        at = 0
        for ref in held:
            size = ref.shape[1] // 2
            mine_ref[:, at : at + size] = ref[:, mine * size : (mine + 1) * size]
            other_ref[:, at : at + size] = ref[:, (1 - mine) * size : (2 - mine) * size]
            at += size

    for mine in range(2):
        pl.when(head_ref[0] == mine)(functools.partial(copy, mine))


def halves(head, *weights):
    smem, vmem = pl.BlockSpec(memory_space=pltpu.SMEM), pl.BlockSpec(memory_space=pltpu.VMEM)
    return pl.pallas_call(
        halves_body,
        out_shape=[jax.ShapeDtypeStruct((ROWS, CUTS[-1]), jnp.bfloat16)] * 2,
        in_specs=[smem] + [pl.BlockSpec(memory_space=pltpu.HBM)] * len(weights),
        out_specs=[vmem, vmem],
        scratch_shapes=[pltpu.VMEM(w.shape, w.dtype) for w in weights]
        + [pltpu.SemaphoreType.DMA((len(weights),))],
        compiler_params=pltpu.CompilerParams(vmem_limit_bytes=60 * 1024 * 1024),
    )(head.reshape(1), *weights)


def double(block, axis):
    pair = jnp.stack([block, send(block, FLIP[axis, 0])])
    return jnp.concatenate([pair, send(pair, FLIP[axis, 1])])


def in_place(pieces, slots, blank):
    joined = blank
    for i, slot in enumerate(slots):
        joined = lax.dynamic_update_slice_in_dim(joined, pieces[i][None], slot, 0)
    return joined


def on_device(tokens, gain, w_query, w_key, w_value, w_mark_key, w_mark_value, level, hist_len):
    dp = lax.axis_index("dp")
    span = lax.axis_index("ctx")
    core, low, high = dp % 2, dp // 2, span % 2
    head = low ^ high
    pos = {"x": span // 8, "z": (span // 2) % 4}
    near, far = 1 + 2 * core, 3 - 2 * core

    def order(first, one, two):
        return jnp.where(first == 0, jnp.concatenate([one, two], 0), jnp.concatenate([two, one], 0))

    mine, other = halves(head, w_mark_key, w_mark_value, w_key, w_value, w_query)
    rows = order(low, mine, send(other, MATE))

    def pair_of(axis, side):
        p = pos[axis]
        inner = jnp.logical_or(p == 1, p == 2).astype(jnp.int32)
        index = jnp.where(side == 0, p // 2, inner)
        return index, jnp.where(side == 0, p % 2, p // 2)

    def slabs(axis):
        mine, theirs = pair_of(axis, core)[0], pair_of(axis, 1 - core)[0]
        return (
            (core * 2 + mine, 2 * (1 - core) + theirs),
            (core * 2 + 1 - mine, 2 * (1 - core) + 1 - theirs),
        )

    begin = span * TOK
    stride = jnp.left_shift(jnp.int32(4), level[0, 0])
    valid = jnp.clip(hist_len[0] - begin, 0, TOK)
    count = jnp.minimum(TOK // stride, (valid + stride - 1) // stride)
    near_slots, far_slots = slabs("x")
    facts = jnp.stack([level[0, 0], valid, count, *near_slots, *far_slots]).astype(jnp.int32)
    own_near, own_far = norm_rows(facts, tokens[0], gain)
    mate_near = send(own_near, MATE)
    mate_far = send(after(own_far, mate_near), MATE)
    facts = mate_near[0, TOK + SLOTS : TOK + SLOTS + 16, 0].astype(jnp.int32)
    mate_count, mate_valid = facts[0], facts[8]

    def pooled_of(packed):
        return packed[:, TOK:].reshape(4, SLOTS + 16, SLAB)[:, :SLOTS]

    rows = order(high, rows, send(rows, ACROSS))

    def blank(shape, after):
        return lax.optimization_barrier((jnp.zeros(shape, jnp.bfloat16), after))[0]

    def joined(pieces, axis):
        p = pos[axis]
        out = blank((4,) + pieces[0].shape, pieces[0])
        out = in_place(pieces, (p, p ^ near, p ^ far, p ^ 2), out)
        return out.reshape(-1, out.shape[-1])

    early, late = rows[:, : CUTS[2]], rows[:, CUTS[2] :]
    pair_e = jnp.stack([early, send(early, FLIP["x", 0])])
    late_1 = send(late, FLIP["z", 0])
    pair_l = jnp.stack([late, late_1])
    early = joined(jnp.concatenate([pair_e, send(pair_e, FLIP["x", 1])]), "x")
    late_2 = send(pair_l, FLIP["z", 1])
    late = joined(jnp.concatenate([pair_l, late_2]), "z")

    early, cross = after(early[:, : CUTS[1]], late_1), early[:, CUTS[1] :]
    z_second, x_second = pair_of("z", core)[1], pair_of("x", core)[1]
    early = order(z_second, early, send(early, FLIP["z", 0]))
    cross_near = send(cross, FLIP["z", 0])
    late_near = send(late, FLIP["x", 0])
    early_far = send(after(early, late_2), FLIP["z", 1])
    swapped = send(jnp.concatenate([early, early_far], 0), SWAP)
    cross, late = after((cross, late), swapped)
    cross = order(z_second, cross, cross_near)
    late = order(x_second, late, late_near)
    cross_far = send(cross, FLIP["z", 1])
    late_far = send(late, FLIP["x", 1])
    slab_near, slab_far = slabs("z")
    where_m = (slab_near[0], slab_far[0], slab_near[1], slab_far[1])
    pieces_m = (early, early_far, swapped)
    both_pooled = jnp.concatenate([pooled_of(own_near), pooled_of(mate_near)], 1)
    beacon = project(where_m, both_pooled, pieces_m)
    beacon = beacon.reshape(2, SLOTS, 2 * D)
    counts = jnp.stack([count, mate_count]).astype(jnp.bfloat16)
    flags = jnp.broadcast_to(counts[:, None, None], (2, 16, D))
    block_k = jnp.concatenate([beacon[..., :D], flags], 1)
    block_v = beacon[..., D:]
    block = jnp.concatenate([block_k, block_v], 1)
    block = order(low, block[:1], block[1:])
    block = jnp.stack([block, send(block, ACROSS)])
    half_k = double(block[:, :, : SLOTS + 16], "x")
    half_v = double(block[:, :, SLOTS + 16 :], "z")
    pieces = after((cross, cross_far, late, late_far), (half_k, half_v))
    others = [send(piece, SWAP) for piece in pieces]
    pair_k = jnp.stack([half_k, send(half_k, FLIP["z", 0])])
    pair_v = jnp.stack([half_v, send(half_v, FLIP["x", 0])])
    pair_k, pair_v = after((pair_k, pair_v), (others, mate_far))
    every_k = [pair_k, send(pair_k, FLIP["z", 1])]
    every_v = [pair_v, send(pair_v, FLIP["x", 1])]
    every_k = [k.reshape(SPANS // 2, 2, SLOTS + 16, D) for k in every_k]
    every_v = [v.reshape(SPANS // 2, 2, SLOTS, D) for v in every_v]

    owner = jnp.arange(SPANS, dtype=jnp.int32)

    def code(axis, at):
        d = at ^ pos[axis]
        return jnp.where(d == 0, 0, jnp.where(d == near, 1, jnp.where(d == far, 2, 3)))

    code_x, code_z = code("x", owner // 8), code("z", (owner // 2) % 4)
    code_h = (owner ^ span) % 2
    at_k = (code_z * 4 + code_x) * 2 + code_h
    at_v = (code_x * 4 + code_z) * 2 + code_h
    live = jnp.concatenate([k[:, :, SLOTS, 0].reshape(SPANS) for k in every_k]).astype(jnp.int32)

    pairs = [pair_of(axis, side)[0] for axis in "xz" for side in (core, 1 - core)]
    info = jnp.stack([core, *pairs]).astype(jnp.int32)
    both = (own_near, own_far, mate_near, mate_far)
    part = project_spans(True, info, both, (cross, cross_far, others[0], others[1]))
    more = project_spans(False, info, both, (late, late_far, others[2], others[3]))

    def attention(which, valid, wide):
        info = jnp.concatenate(
            [jnp.stack([span, valid, head * (HEADS * D), low ^ which]), at_k, at_v]
        )
        return attend(
            wide,
            info,
            live,
            part,
            more,
            every_k + every_v,
        )

    away = send(attention(1, mate_valid, False), MATE)
    home = attention(0, valid, True)
    full = lax.dynamic_update_slice(home, away, (0, (1 - head) * (HEADS * D)))
    return full[None]


def solution(mesh):
    return jax.shard_map(
        on_device,
        mesh=mesh,
        in_specs=(
            P("dp", "ctx", None),
            P(),
            P(("dp", "ctx"), None),
            P(("dp", "ctx"), None),
            P(("dp", "ctx"), None),
            P(("dp", "ctx"), None),
            P(("dp", "ctx"), None),
            P("dp", "ctx"),
            P("dp"),
        ),
        out_specs=P("dp", "ctx", None),
        check_vma=False,
    )
```

```python
import functools
import math

import jax
import jax.numpy as jnp
import numpy as np
from jax import lax
from jax.experimental import pallas as pl
from jax.experimental.pallas import tpu as pltpu
from jax.sharding import PartitionSpec as P

HEADS = 7
D = 128
WIDTH = 3584
ROWS = 28
TOK = 256
SLOTS = 64
SPANS = 32
EPS = 1e-6
FILL = -1e30
AXES = ("dp", "ctx")
SCALE = 1.0 / math.sqrt(D)


def device_id(x, y, z, c):
    return ((y % 2) * 2 + c) * 32 + (x * 4 + z) * 2 + y // 2


def make_perm(f):
    pairs = []
    for x in range(4):
        for y in range(4):
            for z in range(4):
                for c in range(2):
                    tx, ty, tz, tc = f(x, y, z, c)
                    pairs.append(
                        (device_id(x, y, z, c), device_id(tx % 4, ty % 4, tz % 4, tc % 2))
                    )
    return pairs


SWAP = make_perm(lambda x, y, z, c: (x, y, z, 1 - c))
MATE = make_perm(lambda x, y, z, c: (x, y ^ 1, z, c))
ACROSS = make_perm(lambda x, y, z, c: (x, y ^ 3, z, c))

def flip(axis, turn):
    def partner(x, y, z, c):
        at = {"x": x, "y": y, "z": z}
        at[axis] ^= 1 if (c + turn) % 2 == 0 else 3
        return at["x"], at["y"], at["z"], c

    return make_perm(partner)


FLIP = {(axis, turn): flip(axis, turn) for axis in "xz" for turn in (0, 1)}

KEPT = 2
CUTS = (0, 2 * D, (4 + KEPT) * D, (4 + HEADS) * D)
SLAB = WIDTH // 4
PAIRED = ((0, 1, 2, 3), (0, 3, 1, 2))


def send(value, pairs):
    return lax.ppermute(value, AXES, pairs)


def feature_runs(last):
    starts = []
    for c in range(2):
        for i in PAIRED[c]:
            for j in range(4):
                for y in range(4):
                    x, z = (i, j) if last == "x" else (j, i)
                    starts.append(device_id(x, y, z, c) * ROWS)
    source = np.concatenate([np.arange(s, s + ROWS) for s in starts])
    tiles = []
    for tile in range(WIDTH // 128):
        part = source[tile * 128 : (tile + 1) * 128]
        runs = []
        lane = 0
        while lane < 128:
            end = lane + 1
            while end < 128 and part[end] == part[end - 1] + 1 and part[end] % 128 != 0:
                end += 1
            runs.append((lane, end, int(part[lane])))
            lane = end
        tiles.append(runs)
    return tiles


def reorder(plain_ref, out_ref, last, count, out_rows):
    lane = lax.broadcasted_iota(jnp.int32, (count, 128), 1)
    for tile, runs in enumerate(feature_runs(last)):
        joined = jnp.zeros((count, 128), jnp.float32)
        for first, end, feature in runs:
            block, offset = divmod(feature, 128)
            piece = plain_ref[:, block * 128 : (block + 1) * 128]
            shift = (first - offset) % 128
            if shift:
                piece = pltpu.roll(piece, shift, 1)
            joined = jnp.where((lane >= first) & (lane < end), piece, joined)
        slab, column = divmod(tile, SLAB // 128)
        out_ref[slab, out_rows, column * 128 : (column + 1) * 128] = joined.astype(jnp.bfloat16)


def norm_body(fact_ref, tokens_ref, gain_ref, near_ref, far_ref, *scratch):
    out_ref, pool_ref, plain_ref, normed_ref = scratch
    rows = 64
    level, valid, count = fact_ref[0], fact_ref[1], fact_ref[2]

    @pl.loop(0, TOK // rows)
    def _(step):
        here = pl.ds(pl.multiple_of(step * rows, rows), rows)
        values = tokens_ref[here, :].astype(jnp.float32)
        factor = lax.rsqrt(jnp.mean(values * values, axis=-1, keepdims=True) + EPS)
        plain_ref[...] = values * factor * gain_ref[...]
        normed_ref[here, :] = plain_ref[...].astype(jnp.bfloat16)
        reorder(plain_ref, out_ref, "x", rows, here)

    shift = level + 2
    live = jnp.right_shift(TOK, shift)
    slot = lax.broadcasted_iota(jnp.int32, (SLOTS, TOK), 0)
    position = lax.broadcasted_iota(jnp.int32, (SLOTS, TOK), 1)
    inside = (jnp.right_shift(position, shift) == slot) & (slot < live) & (position < valid)
    window = jnp.where(inside, 1.0, 0.0)
    size = jnp.maximum(jnp.sum(window, axis=1, keepdims=True), 1.0)
    sums = jnp.dot(
        window.astype(jnp.bfloat16), normed_ref[...], preferred_element_type=jnp.float32
    )
    plain_ref[...] = sums / size
    reorder(plain_ref, pool_ref, "z", SLOTS, pl.ds(0, SLOTS))
    row = lax.broadcasted_iota(jnp.int32, (16, SLAB), 0)
    facts = jnp.where(row < 8, count, valid).astype(jnp.float32).astype(jnp.bfloat16)
    for i in range(2):
        near_ref[i, :TOK, :] = out_ref[fact_ref[3 + i]]
        far_ref[i] = out_ref[fact_ref[5 + i]]
        for j in range(2):
            lines = slice(TOK + j * (SLOTS + 16), TOK + j * (SLOTS + 16) + SLOTS)
            near_ref[i, lines, :] = pool_ref[2 * i + j]
            near_ref[i, lines.stop : lines.stop + 16, :] = facts


def norm_rows(facts, tokens, gain):
    vmem = pl.BlockSpec(memory_space=pltpu.VMEM)
    return pl.pallas_call(
        norm_body,
        out_shape=[
            jax.ShapeDtypeStruct((2, TOK + 2 * (SLOTS + 16), SLAB), jnp.bfloat16),
            jax.ShapeDtypeStruct((2, TOK, SLAB), jnp.bfloat16),
        ],
        in_specs=[pl.BlockSpec(memory_space=pltpu.SMEM), vmem, vmem],
        out_specs=[vmem, vmem],
        scratch_shapes=[
            pltpu.VMEM((4, TOK, SLAB), jnp.bfloat16),
            pltpu.VMEM((4, SLOTS, SLAB), jnp.bfloat16),
            pltpu.VMEM((64, WIDTH), jnp.float32),
            pltpu.VMEM((TOK, WIDTH), jnp.bfloat16),
        ],
        compiler_params=pltpu.CompilerParams(vmem_limit_bytes=16 * 1024 * 1024),
    )(facts, tokens, gain.reshape(1, WIDTH))


BLOCK = 256
ROOM = SPANS * SLOTS + BLOCK
LINES = HEADS * TOK


def attend_body(wide, info_ref, count_ref, part_ref, more_ref, *rest):
    far_k_refs, far_v_refs, rest = rest[:2], rest[2:4], rest[4:]
    out_ref, query_ref, keys_ref, values_ref, bias_ref, score_ref, top_ref, sum_ref, mix_ref = rest
    span, valid, column, which = info_ref[0], info_ref[1], info_ref[2], info_ref[3]
    own = slice(0, TOK) if wide else slice(TOK, 2 * TOK)

    lane = lax.broadcasted_iota(jnp.int32, (1, ROOM), 1)
    bias_ref[...] = jnp.full((1, ROOM), FILL, jnp.float32)

    def pack(i, at):
        place_k, place_v = info_ref[4 + i], info_ref[4 + SPANS + i]
        count = count_ref[place_k * 2 + which]
        here = pl.ds(pl.multiple_of(at, 16), SLOTS)
        for j in range(2):

            @pl.when(place_k // (SPANS // 2) == j)
            def _():
                keys_ref[here, :] = far_k_refs[j][place_k % (SPANS // 2), which, :SLOTS, :]

            @pl.when(place_v // (SPANS // 2) == j)
            def _():
                values_ref[here, :] = far_v_refs[j][place_v % (SPANS // 2), which]

        bias_ref[...] = jnp.where((lane >= at) & (lane < at + count), 0.0, bias_ref[...])
        return at + ((count + 15) // 16) * 16

    used = lax.fori_loop(0, span, pack, jnp.int32(0))
    rest_rows = pl.ds(pl.multiple_of(used, 16), BLOCK)
    keys_ref[rest_rows, :] = jnp.zeros((BLOCK, D), jnp.bfloat16)
    values_ref[rest_rows, :] = jnp.zeros((BLOCK, D), jnp.bfloat16)
    blocks = (used + BLOCK - 1) // BLOCK

    power = SCALE * math.log2(math.e)
    contract = (((1,), (1,)), ((), ()))

    def fold(op, scores):
        out = scores[:, :D]
        for i in range(1, scores.shape[1] // D):
            out = op(out, scores[:, i * D : (i + 1) * D])
        return out

    row = lax.broadcasted_iota(jnp.int32, (TOK, TOK), 0)
    col = lax.broadcasted_iota(jnp.int32, (TOK, TOK), 1)
    near_bias = jnp.where((col <= row) & (col < valid), 0.0, FILL)
    for head in range(HEADS):
        here = slice(head * TOK, (head + 1) * TOK)
        if head < KEPT:
            query = part_ref[own, (2 + head) * D : (3 + head) * D]
        else:
            query = more_ref[own, (head - KEPT) * D : (head - KEPT + 1) * D]
        query_ref[here, :] = query
        near = lax.dot_general(
            query, part_ref[own, :D], contract, preferred_element_type=jnp.float32
        )
        near = near + near_bias
        score_ref[here, ROOM:] = near
        top_ref[here, :] = fold(jnp.maximum, near)

    def score(i, carry):
        here = pl.ds(pl.multiple_of(i * BLOCK, BLOCK), BLOCK)
        bias = bias_ref[:, here]
        for head in range(HEADS):
            lines = slice(head * TOK, (head + 1) * TOK)
            far = lax.dot_general(
                query_ref[lines, :],
                keys_ref[here, :],
                contract,
                preferred_element_type=jnp.float32,
            )
            far = far + bias
            score_ref[lines, here] = far
            top_ref[lines, :] = jnp.maximum(top_ref[lines, :], fold(jnp.maximum, far))
        return carry

    lax.fori_loop(0, blocks, score, jnp.int32(0))

    for head in range(HEADS):
        lines = slice(head * TOK, (head + 1) * TOK)
        top = jnp.max(top_ref[lines, :], axis=1, keepdims=True)
        top_ref[lines, :] = jnp.broadcast_to(top, (TOK, D))
        weight = jnp.exp2((score_ref[lines, ROOM:] - top) * power)
        sum_ref[lines, :] = fold(jnp.add, weight)
        mix_ref[lines, :] = jnp.dot(
            weight.astype(jnp.bfloat16),
            part_ref[own, D : 2 * D],
            preferred_element_type=jnp.float32,
        )

    def mix(i, carry):
        here = pl.ds(pl.multiple_of(i * BLOCK, BLOCK), BLOCK)
        for head in range(HEADS):
            lines = slice(head * TOK, (head + 1) * TOK)
            top = top_ref[lines, :]
            top = jnp.concatenate([top] * (BLOCK // D), axis=1)
            weight = jnp.exp2((score_ref[lines, here] - top) * power)
            sum_ref[lines, :] = sum_ref[lines, :] + fold(jnp.add, weight)
            mix_ref[lines, :] = mix_ref[lines, :] + jnp.dot(
                weight.astype(jnp.bfloat16), values_ref[here, :], preferred_element_type=jnp.float32
            )
        return carry

    lax.fori_loop(0, blocks, mix, jnp.int32(0))

    alive = lax.broadcasted_iota(jnp.int32, (TOK, D), 0) < valid
    for head in range(HEADS):
        lines = slice(head * TOK, (head + 1) * TOK)
        total = jnp.sum(sum_ref[lines, :], axis=1, keepdims=True)
        result = jnp.where(alive, mix_ref[lines, :] / total, 0.0).astype(jnp.bfloat16)
        if wide:
            out_ref[:, pl.ds(pl.multiple_of(column + head * D, D), D)] = result
        else:
            out_ref[:, head * D : (head + 1) * D] = result


def attend(wide, info, counts, part, more, far):
    columns = 2 * HEADS * D if wide else HEADS * D
    smem, vmem = pl.BlockSpec(memory_space=pltpu.SMEM), pl.BlockSpec(memory_space=pltpu.VMEM)
    return pl.pallas_call(
        functools.partial(attend_body, wide),
        out_shape=jax.ShapeDtypeStruct((TOK, columns), jnp.bfloat16),
        in_specs=[smem, smem] + [vmem] * 6,
        out_specs=vmem,
        scratch_shapes=[
            pltpu.VMEM((LINES, D), jnp.bfloat16),
            pltpu.VMEM((ROOM, D), jnp.bfloat16),
            pltpu.VMEM((ROOM, D), jnp.bfloat16),
            pltpu.VMEM((1, ROOM), jnp.float32),
            pltpu.VMEM((LINES, ROOM + TOK), jnp.float32),
            pltpu.VMEM((LINES, D), jnp.float32),
            pltpu.VMEM((LINES, D), jnp.float32),
            pltpu.VMEM((LINES, D), jnp.float32),
        ],
        compiler_params=pltpu.CompilerParams(vmem_limit_bytes=28 * 1024 * 1024),
    )(info, counts, part, more, *far)


def project_body(count, slab_ref, x_ref, *refs):
    weights, total_refs, out_ref = refs[:count], refs[count:-1], refs[-1]
    rows, columns = out_ref.shape
    for first in range(0, columns, 256):
        here = slice(first, min(first + 256, columns))
        out = total_refs[0][:, here] if total_refs else None
        for i in range(count):
            x = x_ref[slab_ref[i], :rows, :]
            term = jnp.dot(x, weights[i][:, here], preferred_element_type=jnp.float32)
            out = term if out is None else out + term
        out_ref[:, here] = out.astype(out_ref.dtype)


def project(slabs, x, weights, total=None, last=False, rows=TOK):
    smem, vmem = pl.BlockSpec(memory_space=pltpu.SMEM), pl.BlockSpec(memory_space=pltpu.VMEM)
    totals = () if total is None else (total,)
    dtype = jnp.bfloat16 if last else jnp.float32
    return pl.pallas_call(
        functools.partial(project_body, len(weights)),
        out_shape=jax.ShapeDtypeStruct((rows, weights[0].shape[1]), dtype),
        in_specs=[smem] + [vmem] * (1 + len(weights) + len(totals)),
        out_specs=vmem,
        compiler_params=pltpu.CompilerParams(vmem_limit_bytes=16 * 1024 * 1024),
    )(jnp.stack(slabs).astype(jnp.int32), x, *weights, *totals)


def span_body(crossed, info_ref, own_near, own_far, mate_near, mate_far, *refs):
    (near_w, far_w, other_w), out_ref, full_ref = refs[:3], refs[3], refs[4]
    pieces = [(near_w, 0), (far_w, 0), (other_w, 0), (other_w, SLAB)]
    if crossed:
        core = info_ref[0]
        block = 4 * ROWS
        for i, (piece, start) in enumerate(pieces):
            theirs, is_far = divmod(i, 2)
            side = core if theirs == 0 else 1 - core
            pair_x, pair_z = info_ref[1 + theirs], info_ref[3 + theirs]
            if is_far:
                pair_z = 1 - pair_z
            for t in range(2):
                split = jnp.where(pair_z == 0, PAIRED[1][t], PAIRED[1][2 + t])
                z = jnp.where(side == 0, 2 * pair_z + t, split)
                for x in range(4):
                    at = jnp.where(side == 0, x, PAIRED[1].index(x))
                    slab = jnp.where(at // 2 == pair_x, 0, 2) + theirs
                    line = slab * SLAB + ((at % 2) * 4 + z) * block
                    source = start + (t * 4 + x) * block
                    full_ref[pl.ds(pl.multiple_of(line, 16), block), :] = piece[
                        source : source + block, :
                    ]
        pieces = [(full_ref, slab * SLAB) for slab in range(4)]
    else:
        pieces = [pieces[0], pieces[2], pieces[1], pieces[3]]
    columns = out_ref.shape[1]
    for first in range(0, columns, 256):
        here = slice(first, min(first + 256, columns))
        for j, (near_ref, far_ref) in enumerate(((own_near, own_far), (mate_near, mate_far))):
            out = None
            for slab, (piece, start) in enumerate(pieces):
                x = (near_ref if slab < 2 else far_ref)[slab % 2, :TOK, :]
                w = piece[start : start + SLAB, here]
                term = jnp.dot(x, w, preferred_element_type=jnp.float32)
                out = term if out is None else out + term
            out_ref[j * TOK : (j + 1) * TOK, here] = out.astype(jnp.bfloat16)


def project_spans(crossed, info, tokens, pieces):
    smem, vmem = pl.BlockSpec(memory_space=pltpu.SMEM), pl.BlockSpec(memory_space=pltpu.VMEM)
    columns = pieces[0].shape[1]
    lines = WIDTH if crossed else 16
    return pl.pallas_call(
        functools.partial(span_body, crossed),
        out_shape=jax.ShapeDtypeStruct((2 * TOK, columns), jnp.bfloat16),
        in_specs=[smem] + [vmem] * 7,
        out_specs=vmem,
        scratch_shapes=[pltpu.VMEM((lines, columns), jnp.bfloat16)],
        compiler_params=pltpu.CompilerParams(vmem_limit_bytes=10 * 1024 * 1024),
    )(info, *tokens, *pieces)


def after(value, other):
    return lax.optimization_barrier((value, other))[0]


def halves_body(head_ref, *refs):
    mine_ref, other_ref = refs[-2:]

    def copy(mine):
        at = 0
        for ref in refs[:-2]:
            size = ref.shape[1] // 2
            mine_ref[:, at : at + size] = ref[:, mine * size : (mine + 1) * size]
            other_ref[:, at : at + size] = ref[:, (1 - mine) * size : (2 - mine) * size]
            at += size

    for mine in range(2):
        pl.when(head_ref[0] == mine)(functools.partial(copy, mine))


def halves(head, *weights):
    smem, vmem = pl.BlockSpec(memory_space=pltpu.SMEM), pl.BlockSpec(memory_space=pltpu.VMEM)
    return pl.pallas_call(
        halves_body,
        out_shape=[jax.ShapeDtypeStruct((ROWS, CUTS[-1]), jnp.bfloat16)] * 2,
        in_specs=[smem] + [vmem] * len(weights),
        out_specs=[vmem, vmem],
        compiler_params=pltpu.CompilerParams(vmem_limit_bytes=4 * 1024 * 1024),
    )(head.reshape(1), *weights)


def gate(flag, other):
    return flag + (other[0, 0].astype(jnp.float32) > 1e38).astype(jnp.int32)


def double(block, axis):
    pair = jnp.stack([block, send(block, FLIP[axis, 0])])
    return jnp.concatenate([pair, send(pair, FLIP[axis, 1])])


def in_place(pieces, slots, blank):
    joined = blank
    for i, slot in enumerate(slots):
        joined = lax.dynamic_update_slice_in_dim(joined, pieces[i][None], slot, 0)
    return joined


def on_device(tokens, gain, w_query, w_key, w_value, w_mark_key, w_mark_value, level, hist_len):
    dp = lax.axis_index("dp")
    span = lax.axis_index("ctx")
    core, low, high = dp % 2, dp // 2, span % 2
    head = low ^ high
    pos = {"x": span // 8, "z": (span // 2) % 4}
    near, far = 1 + 2 * core, 3 - 2 * core

    def order(first, one, two):
        return jnp.where(first == 0, jnp.concatenate([one, two], 0), jnp.concatenate([two, one], 0))

    mine, other = halves(head, w_mark_key, w_mark_value, w_key, w_value, w_query)
    rows = order(low, mine, send(other, MATE))

    def pair_of(axis, side):
        p = pos[axis]
        inner = jnp.logical_or(p == 1, p == 2).astype(jnp.int32)
        index = jnp.where(side == 0, p // 2, inner)
        return index, jnp.where(side == 0, p % 2, p // 2)

    def slabs(axis):
        mine, theirs = pair_of(axis, core)[0], pair_of(axis, 1 - core)[0]
        return (
            (core * 2 + mine, 2 * (1 - core) + theirs),
            (core * 2 + 1 - mine, 2 * (1 - core) + 1 - theirs),
        )

    begin = span * TOK
    stride = jnp.left_shift(jnp.int32(4), level[0, 0])
    valid = jnp.clip(hist_len[0] - begin, 0, TOK)
    count = jnp.minimum(TOK // stride, (valid + stride - 1) // stride)
    near_slots, far_slots = slabs("x")
    facts = jnp.stack([level[0, 0], valid, count, *near_slots, *far_slots]).astype(jnp.int32)
    own_near, own_far = norm_rows(facts, tokens[0], gain)
    mate_near = send(own_near, MATE)
    mate_far = send(after(own_far, mate_near), MATE)
    facts = mate_near[0, TOK + SLOTS : TOK + SLOTS + 16, 0].astype(jnp.int32)
    mate_count, mate_valid = facts[0], facts[8]

    def pooled_of(packed):
        return packed[:, TOK:].reshape(4, SLOTS + 16, SLAB)[:, :SLOTS]

    rows = order(high, rows, send(rows, ACROSS))

    def blank(shape, after):
        return lax.optimization_barrier((jnp.zeros(shape, jnp.bfloat16), after))[0]

    def second(block, axis):
        p = pos[axis]
        joined = blank((4,) + block.shape, block)
        joined = in_place(double(block, axis), (p, p ^ near, p ^ far, p ^ 2), joined)
        return joined.reshape(-1, block.shape[-1])

    early = second(rows[:, : CUTS[2]], "x")
    late = second(rows[:, CUTS[2] :], "z")

    early, cross = early[:, : CUTS[1]], early[:, CUTS[1] :]
    z_second, x_second = pair_of("z", core)[1], pair_of("x", core)[1]
    early = order(z_second, early, send(early, FLIP["z", 0]))
    early_far = send(early, FLIP["z", 1])
    gathered = jnp.concatenate([early, early_far], 0)
    swapped = send(gathered, SWAP)
    ready = gate(jnp.int32(0), swapped) == 0
    cross, late = jnp.where(ready, cross, 0), jnp.where(ready, late, 0)
    cross_near, late_near = send(cross, FLIP["z", 0]), send(late, FLIP["x", 0])
    slab_near, slab_far = slabs("z")
    where_m = (slab_near[0], slab_far[0], slab_near[1], slab_far[1])
    pieces_m = (early, early_far, swapped[:SLAB], swapped[SLAB:])
    both_pooled = jnp.concatenate([pooled_of(own_near), pooled_of(mate_near)], 1)
    beacon = project(where_m, both_pooled, pieces_m, last=True, rows=2 * SLOTS)
    beacon = beacon.reshape(2, SLOTS, 2 * D)
    counts = jnp.stack([count, mate_count]).astype(jnp.bfloat16)
    flags = jnp.broadcast_to(counts[:, None, None], (2, 16, D))
    block_k = jnp.concatenate([beacon[..., :D], flags], 1)
    block_v = beacon[..., D:]
    block = jnp.concatenate([block_k, block_v], 1)
    block = order(low, block[:1], block[1:])
    block = jnp.stack([block, send(block, ACROSS)])
    one_k, one_v = block[:, :, : SLOTS + 16], block[:, :, SLOTS + 16 :]
    got_k, got_v = send(one_k, FLIP["x", 0]), send(one_v, FLIP["z", 0])
    one_k, one_v = jnp.stack([one_k, got_k]), jnp.stack([one_v, got_v])
    half_k = jnp.concatenate([one_k, send(one_k, FLIP["x", 1])])
    half_v = jnp.concatenate([one_v, send(one_v, FLIP["z", 1])])
    cross = order(gate(z_second, got_k[0, 0]), cross, cross_near)
    late = order(gate(x_second, got_v[0, 0]), late, late_near)
    cross_far = send(cross, FLIP["z", 1])
    late_far = send(late, FLIP["x", 1])
    pair_k = jnp.stack([half_k, send(half_k, FLIP["z", 0])])
    pair_v = jnp.stack([half_v, send(half_v, FLIP["x", 0])])
    mate_there = gate(jnp.int32(0), mate_far[0]) == 0
    pair_k, pair_v = jnp.where(mate_there, pair_k, 0), jnp.where(mate_there, pair_v, 0)
    every_k = [pair_k, send(pair_k, FLIP["z", 1])]
    every_v = [pair_v, send(pair_v, FLIP["x", 1])]
    every_k = [k.reshape(SPANS // 2, 2, SLOTS + 16, D) for k in every_k]
    every_v = [v.reshape(SPANS // 2, 2, SLOTS, D) for v in every_v]

    owner = jnp.arange(SPANS, dtype=jnp.int32)

    def code(axis, at):
        d = at ^ pos[axis]
        return jnp.where(d == 0, 0, jnp.where(d == near, 1, jnp.where(d == far, 2, 3)))

    code_x, code_z = code("x", owner // 8), code("z", (owner // 2) % 4)
    code_h = (owner ^ span) % 2
    at_k = (code_z * 4 + code_x) * 2 + code_h
    at_v = (code_x * 4 + code_z) * 2 + code_h
    live = jnp.concatenate([k[:, :, SLOTS, 0].reshape(SPANS) for k in every_k]).astype(jnp.int32)

    pairs = [pair_of(axis, side)[0] for axis in "xz" for side in (core, 1 - core)]
    third = gate(gate(jnp.int32(0), pair_k[1, 0, 0, 0]), pair_v[1, 0, 0, 0]) == 0
    cross_other = send(jnp.where(third, jnp.concatenate([cross, cross_far]), 0), SWAP)
    late_other = send(jnp.where(third, jnp.concatenate([late, late_far]), 0), SWAP)
    info = jnp.stack([core, *pairs]).astype(jnp.int32)
    both = (own_near, own_far, mate_near, mate_far)
    part = project_spans(True, info, both, (cross, cross_far, cross_other))
    more = project_spans(False, info, both, (late, late_far, late_other))

    def attention(which, valid, wide):
        info = jnp.concatenate(
            [jnp.stack([span, valid, head * (HEADS * D), low ^ which]), at_k, at_v]
        )
        return attend(
            wide,
            info,
            live,
            part,
            more,
            every_k + every_v,
        )

    away = send(attention(1, mate_valid, False), MATE)
    home = attention(0, valid, True)
    full = lax.dynamic_update_slice(home, away, (0, (1 - head) * (HEADS * D)))
    return full[None]


def solution(mesh):
    return jax.shard_map(
        on_device,
        mesh=mesh,
        in_specs=(
            P("dp", "ctx", None),
            P(),
            P(("dp", "ctx"), None),
            P(("dp", "ctx"), None),
            P(("dp", "ctx"), None),
            P(("dp", "ctx"), None),
            P(("dp", "ctx"), None),
            P("dp", "ctx"),
            P("dp"),
        ),
        out_specs=P("dp", "ctx", None),
        check_vma=False,
    )
```

```python
import functools
import math

import jax
import jax.numpy as jnp
import numpy as np
from jax import lax
from jax.experimental import pallas as pl
from jax.experimental.pallas import tpu as pltpu
from jax.sharding import PartitionSpec as P

HEADS = 7
D = 128
WIDTH = 3584
ROWS = 28
TOK = 256
SLOTS = 64
SPANS = 32
EPS = 1e-6
FILL = -1e30
AXES = ("dp", "ctx")
SCALE = 1.0 / math.sqrt(D)


def device_id(x, y, z, c):
    return ((y % 2) * 2 + c) * 32 + (x * 4 + z) * 2 + y // 2


def make_perm(f):
    pairs = []
    for x in range(4):
        for y in range(4):
            for z in range(4):
                for c in range(2):
                    tx, ty, tz, tc = f(x, y, z, c)
                    pairs.append(
                        (device_id(x, y, z, c), device_id(tx % 4, ty % 4, tz % 4, tc % 2))
                    )
    return pairs


SWAP = make_perm(lambda x, y, z, c: (x, y, z, 1 - c))
MATE = make_perm(lambda x, y, z, c: (x, y ^ 1, z, c))
ACROSS = make_perm(lambda x, y, z, c: (x, y ^ 3, z, c))

def flip(axis, turn):
    def partner(x, y, z, c):
        at = {"x": x, "y": y, "z": z}
        at[axis] ^= 1 if (c + turn) % 2 == 0 else 3
        return at["x"], at["y"], at["z"], c

    return make_perm(partner)


FLIP = {(axis, turn): flip(axis, turn) for axis in "xz" for turn in (0, 1)}

KEPT = 2
CUTS = (0, 2 * D, (4 + KEPT) * D, (4 + HEADS) * D)
SLAB = WIDTH // 4
PAIRED = ((0, 1, 2, 3), (0, 3, 1, 2))


def send(value, pairs):
    return lax.ppermute(value, AXES, pairs)


def feature_runs(last):
    starts = []
    for c in range(2):
        for i in PAIRED[c]:
            for j in range(4):
                for y in range(4):
                    x, z = (i, j) if last == "x" else (j, i)
                    starts.append(device_id(x, y, z, c) * ROWS)
    source = np.concatenate([np.arange(s, s + ROWS) for s in starts])
    tiles = []
    for tile in range(WIDTH // 128):
        part = source[tile * 128 : (tile + 1) * 128]
        runs = []
        lane = 0
        while lane < 128:
            end = lane + 1
            while end < 128 and part[end] == part[end - 1] + 1 and part[end] % 128 != 0:
                end += 1
            runs.append((lane, end, int(part[lane])))
            lane = end
        tiles.append(runs)
    return tiles


def reorder(plain_ref, out_ref, last, count, out_rows):
    lane = lax.broadcasted_iota(jnp.int32, (count, 128), 1)
    for tile, runs in enumerate(feature_runs(last)):
        joined = jnp.zeros((count, 128), jnp.float32)
        for first, end, feature in runs:
            block, offset = divmod(feature, 128)
            piece = plain_ref[:, block * 128 : (block + 1) * 128]
            shift = (first - offset) % 128
            if shift:
                piece = pltpu.roll(piece, shift, 1)
            joined = jnp.where((lane >= first) & (lane < end), piece, joined)
        slab, column = divmod(tile, SLAB // 128)
        out_ref[slab, out_rows, column * 128 : (column + 1) * 128] = joined.astype(jnp.bfloat16)


def norm_body(fact_ref, tokens_ref, gain_ref, near_ref, far_ref, *scratch):
    out_ref, pool_ref, plain_ref, normed_ref = scratch
    rows = 64
    level, valid, count = fact_ref[0], fact_ref[1], fact_ref[2]

    @pl.loop(0, TOK // rows)
    def _(step):
        here = pl.ds(pl.multiple_of(step * rows, rows), rows)
        values = tokens_ref[here, :].astype(jnp.float32)
        factor = lax.rsqrt(jnp.mean(values * values, axis=-1, keepdims=True) + EPS)
        plain_ref[...] = values * factor * gain_ref[...]
        normed_ref[here, :] = plain_ref[...].astype(jnp.bfloat16)
        reorder(plain_ref, out_ref, "x", rows, here)

    shift = level + 2
    live = jnp.right_shift(TOK, shift)
    slot = lax.broadcasted_iota(jnp.int32, (SLOTS, TOK), 0)
    position = lax.broadcasted_iota(jnp.int32, (SLOTS, TOK), 1)
    inside = (jnp.right_shift(position, shift) == slot) & (slot < live) & (position < valid)
    window = jnp.where(inside, 1.0, 0.0)
    size = jnp.maximum(jnp.sum(window, axis=1, keepdims=True), 1.0)
    sums = jnp.dot(
        window.astype(jnp.bfloat16), normed_ref[...], preferred_element_type=jnp.float32
    )
    plain_ref[...] = sums / size
    reorder(plain_ref, pool_ref, "z", SLOTS, pl.ds(0, SLOTS))
    row = lax.broadcasted_iota(jnp.int32, (16, SLAB), 0)
    facts = jnp.where(row < 8, count, valid).astype(jnp.float32).astype(jnp.bfloat16)
    for i in range(2):
        near_ref[i, :TOK, :] = out_ref[fact_ref[3 + i]]
        far_ref[i] = out_ref[fact_ref[5 + i]]
        for j in range(2):
            lines = slice(TOK + j * (SLOTS + 16), TOK + j * (SLOTS + 16) + SLOTS)
            near_ref[i, lines, :] = pool_ref[2 * i + j]
            near_ref[i, lines.stop : lines.stop + 16, :] = facts


def norm_rows(facts, tokens, gain):
    vmem = pl.BlockSpec(memory_space=pltpu.VMEM)
    return pl.pallas_call(
        norm_body,
        out_shape=[
            jax.ShapeDtypeStruct((2, TOK + 2 * (SLOTS + 16), SLAB), jnp.bfloat16),
            jax.ShapeDtypeStruct((2, TOK, SLAB), jnp.bfloat16),
        ],
        in_specs=[pl.BlockSpec(memory_space=pltpu.SMEM), vmem, vmem],
        out_specs=[vmem, vmem],
        scratch_shapes=[
            pltpu.VMEM((4, TOK, SLAB), jnp.bfloat16),
            pltpu.VMEM((4, SLOTS, SLAB), jnp.bfloat16),
            pltpu.VMEM((64, WIDTH), jnp.float32),
            pltpu.VMEM((TOK, WIDTH), jnp.bfloat16),
        ],
        compiler_params=pltpu.CompilerParams(vmem_limit_bytes=16 * 1024 * 1024),
    )(facts, tokens, gain.reshape(1, WIDTH))


BLOCK = 256
ROOM = SPANS * SLOTS + BLOCK
LINES = HEADS * TOK


def attend_body(wide, info_ref, count_ref, part_ref, more_ref, *rest):
    far_k_refs, far_v_refs, rest = rest[:2], rest[2:4], rest[4:]
    out_ref, query_ref, keys_ref, values_ref, bias_ref, score_ref, top_ref, sum_ref, mix_ref = rest
    span, valid, column, which = info_ref[0], info_ref[1], info_ref[2], info_ref[3]
    own = slice(0, TOK) if wide else slice(TOK, 2 * TOK)

    lane = lax.broadcasted_iota(jnp.int32, (1, ROOM), 1)
    bias_ref[...] = jnp.full((1, ROOM), FILL, jnp.float32)

    def pack(i, at):
        place_k, place_v = info_ref[4 + i], info_ref[4 + SPANS + i]
        count = count_ref[place_k * 2 + which]
        here = pl.ds(pl.multiple_of(at, 16), SLOTS)
        for j in range(2):

            @pl.when(place_k // (SPANS // 2) == j)
            def _():
                keys_ref[here, :] = far_k_refs[j][place_k % (SPANS // 2), which, :SLOTS, :]

            @pl.when(place_v // (SPANS // 2) == j)
            def _():
                values_ref[here, :] = far_v_refs[j][place_v % (SPANS // 2), which]

        bias_ref[...] = jnp.where((lane >= at) & (lane < at + count), 0.0, bias_ref[...])
        return at + ((count + 15) // 16) * 16

    used = lax.fori_loop(0, span, pack, jnp.int32(0))
    rest_rows = pl.ds(pl.multiple_of(used, 16), BLOCK)
    keys_ref[rest_rows, :] = jnp.zeros((BLOCK, D), jnp.bfloat16)
    values_ref[rest_rows, :] = jnp.zeros((BLOCK, D), jnp.bfloat16)
    blocks = (used + BLOCK - 1) // BLOCK

    power = SCALE * math.log2(math.e)
    contract = (((1,), (1,)), ((), ()))

    def fold(op, scores):
        out = scores[:, :D]
        for i in range(1, scores.shape[1] // D):
            out = op(out, scores[:, i * D : (i + 1) * D])
        return out

    row = lax.broadcasted_iota(jnp.int32, (TOK, TOK), 0)
    col = lax.broadcasted_iota(jnp.int32, (TOK, TOK), 1)
    near_bias = jnp.where((col <= row) & (col < valid), 0.0, FILL)
    for head in range(HEADS):
        here = slice(head * TOK, (head + 1) * TOK)
        if head < KEPT:
            query = part_ref[own, (2 + head) * D : (3 + head) * D]
        else:
            query = more_ref[:, (head - KEPT) * D : (head - KEPT + 1) * D]
        query_ref[here, :] = query
        near = lax.dot_general(
            query, part_ref[own, :D], contract, preferred_element_type=jnp.float32
        )
        near = near + near_bias
        score_ref[here, ROOM:] = near
        top_ref[here, :] = fold(jnp.maximum, near)

    def score(i, carry):
        here = pl.ds(pl.multiple_of(i * BLOCK, BLOCK), BLOCK)
        bias = bias_ref[:, here]
        for head in range(HEADS):
            lines = slice(head * TOK, (head + 1) * TOK)
            far = lax.dot_general(
                query_ref[lines, :],
                keys_ref[here, :],
                contract,
                preferred_element_type=jnp.float32,
            )
            far = far + bias
            score_ref[lines, here] = far
            top_ref[lines, :] = jnp.maximum(top_ref[lines, :], fold(jnp.maximum, far))
        return carry

    lax.fori_loop(0, blocks, score, jnp.int32(0))

    for head in range(HEADS):
        lines = slice(head * TOK, (head + 1) * TOK)
        top = jnp.max(top_ref[lines, :], axis=1, keepdims=True)
        top_ref[lines, :] = jnp.broadcast_to(top, (TOK, D))
        weight = jnp.exp2((score_ref[lines, ROOM:] - top) * power)
        sum_ref[lines, :] = fold(jnp.add, weight)
        mix_ref[lines, :] = jnp.dot(
            weight.astype(jnp.bfloat16),
            part_ref[own, D : 2 * D],
            preferred_element_type=jnp.float32,
        )

    def mix(i, carry):
        here = pl.ds(pl.multiple_of(i * BLOCK, BLOCK), BLOCK)
        for head in range(HEADS):
            lines = slice(head * TOK, (head + 1) * TOK)
            top = top_ref[lines, :]
            top = jnp.concatenate([top] * (BLOCK // D), axis=1)
            weight = jnp.exp2((score_ref[lines, here] - top) * power)
            sum_ref[lines, :] = sum_ref[lines, :] + fold(jnp.add, weight)
            mix_ref[lines, :] = mix_ref[lines, :] + jnp.dot(
                weight.astype(jnp.bfloat16), values_ref[here, :], preferred_element_type=jnp.float32
            )
        return carry

    lax.fori_loop(0, blocks, mix, jnp.int32(0))

    alive = lax.broadcasted_iota(jnp.int32, (TOK, D), 0) < valid
    for head in range(HEADS):
        lines = slice(head * TOK, (head + 1) * TOK)
        total = jnp.sum(sum_ref[lines, :], axis=1, keepdims=True)
        result = jnp.where(alive, mix_ref[lines, :] / total, 0.0).astype(jnp.bfloat16)
        if wide:
            out_ref[:, pl.ds(pl.multiple_of(column + head * D, D), D)] = result
        else:
            out_ref[:, head * D : (head + 1) * D] = result


def attend(wide, info, counts, part, more, far):
    columns = 2 * HEADS * D if wide else HEADS * D
    smem, vmem = pl.BlockSpec(memory_space=pltpu.SMEM), pl.BlockSpec(memory_space=pltpu.VMEM)
    return pl.pallas_call(
        functools.partial(attend_body, wide),
        out_shape=jax.ShapeDtypeStruct((TOK, columns), jnp.bfloat16),
        in_specs=[smem, smem] + [vmem] * 6,
        out_specs=vmem,
        scratch_shapes=[
            pltpu.VMEM((LINES, D), jnp.bfloat16),
            pltpu.VMEM((ROOM, D), jnp.bfloat16),
            pltpu.VMEM((ROOM, D), jnp.bfloat16),
            pltpu.VMEM((1, ROOM), jnp.float32),
            pltpu.VMEM((LINES, ROOM + TOK), jnp.float32),
            pltpu.VMEM((LINES, D), jnp.float32),
            pltpu.VMEM((LINES, D), jnp.float32),
            pltpu.VMEM((LINES, D), jnp.float32),
        ],
        compiler_params=pltpu.CompilerParams(vmem_limit_bytes=28 * 1024 * 1024),
    )(info, counts, part, more, *far)


def project_body(count, slab_ref, x_ref, *refs):
    weights, total_refs, out_ref = refs[:count], refs[count:-1], refs[-1]
    rows, columns = out_ref.shape
    for first in range(0, columns, 256):
        here = slice(first, min(first + 256, columns))
        out = total_refs[0][:, here] if total_refs else None
        for i in range(count):
            x = x_ref[slab_ref[i], :rows, :]
            term = jnp.dot(x, weights[i][:, here], preferred_element_type=jnp.float32)
            out = term if out is None else out + term
        out_ref[:, here] = out.astype(out_ref.dtype)


def project(slabs, x, weights, total=None, last=False, rows=TOK):
    smem, vmem = pl.BlockSpec(memory_space=pltpu.SMEM), pl.BlockSpec(memory_space=pltpu.VMEM)
    totals = () if total is None else (total,)
    dtype = jnp.bfloat16 if last else jnp.float32
    return pl.pallas_call(
        functools.partial(project_body, len(weights)),
        out_shape=jax.ShapeDtypeStruct((rows, weights[0].shape[1]), dtype),
        in_specs=[smem] + [vmem] * (1 + len(weights) + len(totals)),
        out_specs=vmem,
        compiler_params=pltpu.CompilerParams(vmem_limit_bytes=16 * 1024 * 1024),
    )(jnp.stack(slabs).astype(jnp.int32), x, *weights, *totals)


def crossed_body(info_ref, own_near, own_far, mate_near, mate_far, *refs):
    pieces, out_ref, full_ref = refs[:4], refs[4], refs[5]
    core = info_ref[0]
    block = 4 * ROWS
    for i, piece in enumerate(pieces):
        theirs, is_far = divmod(i, 2)
        side = core if theirs == 0 else 1 - core
        pair_x, pair_z = info_ref[1 + theirs], info_ref[3 + theirs]
        if is_far:
            pair_z = 1 - pair_z
        for t in range(2):
            split = jnp.where(pair_z == 0, PAIRED[1][t], PAIRED[1][2 + t])
            z = jnp.where(side == 0, 2 * pair_z + t, split)
            for x in range(4):
                at = jnp.where(side == 0, x, PAIRED[1].index(x))
                slab = jnp.where(at // 2 == pair_x, 0, 2) + theirs
                line = slab * SLAB + ((at % 2) * 4 + z) * block
                source = slice((t * 4 + x) * block, (t * 4 + x + 1) * block)
                full_ref[pl.ds(pl.multiple_of(line, 16), block), :] = piece[source, :]
    columns = out_ref.shape[1]
    for first in range(0, columns, 256):
        here = slice(first, first + 256)
        for j, (near_ref, far_ref) in enumerate(((own_near, own_far), (mate_near, mate_far))):
            out = None
            for slab in range(4):
                x_ref = near_ref if slab < 2 else far_ref
                w = full_ref[slab * SLAB : (slab + 1) * SLAB, here]
                term = jnp.dot(x_ref[slab % 2, :TOK, :], w, preferred_element_type=jnp.float32)
                out = term if out is None else out + term
            out_ref[j * TOK : (j + 1) * TOK, here] = out.astype(jnp.bfloat16)


def project_crossed(info, tokens, pieces):
    smem, vmem = pl.BlockSpec(memory_space=pltpu.SMEM), pl.BlockSpec(memory_space=pltpu.VMEM)
    columns = pieces[0].shape[1]
    return pl.pallas_call(
        crossed_body,
        out_shape=jax.ShapeDtypeStruct((2 * TOK, columns), jnp.bfloat16),
        in_specs=[smem] + [vmem] * 8,
        out_specs=vmem,
        scratch_shapes=[pltpu.VMEM((WIDTH, columns), jnp.bfloat16)],
        compiler_params=pltpu.CompilerParams(vmem_limit_bytes=16 * 1024 * 1024),
    )(info, *tokens, *pieces)


def after(value, other):
    return lax.optimization_barrier((value, other))[0]


def halves_body(head_ref, *refs):
    mine_ref, other_ref = refs[-2:]

    def copy(mine):
        at = 0
        for ref in refs[:-2]:
            size = ref.shape[1] // 2
            mine_ref[:, at : at + size] = ref[:, mine * size : (mine + 1) * size]
            other_ref[:, at : at + size] = ref[:, (1 - mine) * size : (2 - mine) * size]
            at += size

    for mine in range(2):
        pl.when(head_ref[0] == mine)(functools.partial(copy, mine))


def halves(head, *weights):
    smem, vmem = pl.BlockSpec(memory_space=pltpu.SMEM), pl.BlockSpec(memory_space=pltpu.VMEM)
    return pl.pallas_call(
        halves_body,
        out_shape=[jax.ShapeDtypeStruct((ROWS, CUTS[-1]), jnp.bfloat16)] * 2,
        in_specs=[smem] + [vmem] * len(weights),
        out_specs=[vmem, vmem],
        compiler_params=pltpu.CompilerParams(vmem_limit_bytes=4 * 1024 * 1024),
    )(head.reshape(1), *weights)


def double(block, axis):
    pair = jnp.stack([block, send(block, FLIP[axis, 0])])
    return jnp.concatenate([pair, send(pair, FLIP[axis, 1])])


def in_place(pieces, slots, blank):
    joined = blank
    for i, slot in enumerate(slots):
        joined = lax.dynamic_update_slice_in_dim(joined, pieces[i][None], slot, 0)
    return joined


def on_device(tokens, gain, w_query, w_key, w_value, w_mark_key, w_mark_value, level, hist_len):
    dp = lax.axis_index("dp")
    span = lax.axis_index("ctx")
    core, low, high = dp % 2, dp // 2, span % 2
    head = low ^ high
    pos = {"x": span // 8, "z": (span // 2) % 4}
    near, far = 1 + 2 * core, 3 - 2 * core

    def order(first, one, two):
        return jnp.where(first == 0, jnp.concatenate([one, two], 0), jnp.concatenate([two, one], 0))

    mine, other = halves(head, w_mark_key, w_mark_value, w_key, w_value, w_query)
    rows = order(low, mine, send(other, MATE))

    def pair_of(axis, side):
        p = pos[axis]
        inner = jnp.logical_or(p == 1, p == 2).astype(jnp.int32)
        index = jnp.where(side == 0, p // 2, inner)
        return index, jnp.where(side == 0, p % 2, p // 2)

    def slabs(axis):
        mine, theirs = pair_of(axis, core)[0], pair_of(axis, 1 - core)[0]
        return (
            (core * 2 + mine, 2 * (1 - core) + theirs),
            (core * 2 + 1 - mine, 2 * (1 - core) + 1 - theirs),
        )

    begin = span * TOK
    stride = jnp.left_shift(jnp.int32(4), level[0, 0])
    valid = jnp.clip(hist_len[0] - begin, 0, TOK)
    count = jnp.minimum(TOK // stride, (valid + stride - 1) // stride)
    near_slots, far_slots = slabs("x")
    facts = jnp.stack([level[0, 0], valid, count, *near_slots, *far_slots]).astype(jnp.int32)
    own_near, own_far = norm_rows(facts, tokens[0], gain)
    mate_near = send(own_near, MATE)
    mate_far = send(after(own_far, mate_near), MATE)
    facts = mate_near[0, TOK + SLOTS : TOK + SLOTS + 16, 0].astype(jnp.int32)
    mate_count, mate_valid = facts[0], facts[8]

    def pooled_of(packed):
        return packed[:, TOK:].reshape(4, SLOTS + 16, SLAB)[:, :SLOTS]

    rows = order(high, rows, send(rows, ACROSS))

    def blank(shape, after):
        return lax.optimization_barrier((jnp.zeros(shape, jnp.bfloat16), after))[0]

    def second(block, axis):
        p = pos[axis]
        joined = blank((4,) + block.shape, block)
        joined = in_place(double(block, axis), (p, p ^ near, p ^ far, p ^ 2), joined)
        return joined.reshape(-1, block.shape[-1])

    early = second(rows[:, : CUTS[2]], "x")
    late = second(rows[:, CUTS[2] :], "z")

    early, cross = early[:, : CUTS[1]], early[:, CUTS[1] :]
    z_second, x_second = pair_of("z", core)[1], pair_of("x", core)[1]
    early = order(z_second, early, send(early, FLIP["z", 0]))
    cross = order(z_second, cross, send(cross, FLIP["z", 0]))
    late = order(x_second, late, send(late, FLIP["x", 0]))
    early_far = send(early, FLIP["z", 1])
    cross_far = send(after(cross, early_far), FLIP["z", 1])
    late_far = send(late, FLIP["x", 1])
    gathered = jnp.concatenate([early, early_far], 0)
    swapped = send(gathered, SWAP)
    slab_near, slab_far = slabs("z")
    where_m = (slab_near[0], slab_far[0], slab_near[1], slab_far[1])
    pieces_m = (early, early_far, swapped[:SLAB], swapped[SLAB:])
    both_pooled = jnp.concatenate([pooled_of(own_near), pooled_of(mate_near)], 1)
    beacon = project(where_m, both_pooled, pieces_m, last=True, rows=2 * SLOTS)
    beacon = beacon.reshape(2, SLOTS, 2 * D)
    counts = jnp.stack([count, mate_count]).astype(jnp.bfloat16)
    flags = jnp.broadcast_to(counts[:, None, None], (2, 16, D))
    block_k = jnp.concatenate([beacon[..., :D], flags], 1)
    block_v = beacon[..., D:]
    block = jnp.concatenate([block_k, block_v], 1)
    block = order(low, block[:1], block[1:])
    block = jnp.stack([block, send(block, ACROSS)])
    half_k = double(block[:, :, : SLOTS + 16], "x")
    half_v = double(block[:, :, SLOTS + 16 :], "z")
    zero, one = jnp.int32(0), jnp.int32(1)
    near_w = (late, send(late, SWAP))
    own = project((zero, one), own_near, near_w)
    half_k, half_v = after((half_k, half_v), own)
    crossed = jnp.concatenate([cross, cross_far], 0)
    crossed, far_w = after((crossed, late_far), (half_k, half_v))
    crossed = send(crossed, SWAP)
    far_w = (far_w, send(far_w, SWAP))
    pair_k = jnp.stack([half_k, send(half_k, FLIP["z", 0])])
    pair_v = jnp.stack([half_v, send(half_v, FLIP["x", 0])])
    mate = project((zero, one), mate_near, near_w)
    pair_k, pair_v = after((pair_k, pair_v), (mate, mate_far))
    every_k = [pair_k, send(pair_k, FLIP["z", 1])]
    every_v = [pair_v, send(pair_v, FLIP["x", 1])]
    every_k = [k.reshape(SPANS // 2, 2, SLOTS + 16, D) for k in every_k]
    every_v = [v.reshape(SPANS // 2, 2, SLOTS, D) for v in every_v]

    owner = jnp.arange(SPANS, dtype=jnp.int32)

    def code(axis, at):
        d = at ^ pos[axis]
        return jnp.where(d == 0, 0, jnp.where(d == near, 1, jnp.where(d == far, 2, 3)))

    code_x, code_z = code("x", owner // 8), code("z", (owner // 2) % 4)
    code_h = (owner ^ span) % 2
    at_k = (code_z * 4 + code_x) * 2 + code_h
    at_v = (code_x * 4 + code_z) * 2 + code_h
    live = jnp.concatenate([k[:, :, SLOTS, 0].reshape(SPANS) for k in every_k]).astype(jnp.int32)

    pairs = [pair_of(axis, side)[0] for axis in "xz" for side in (core, 1 - core)]
    part = project_crossed(
        jnp.stack([core, *pairs]).astype(jnp.int32),
        (own_near, own_far, mate_near, mate_far),
        (cross, cross_far, crossed[:SLAB], crossed[SLAB:]),
    )
    own = project((zero, one), own_far, far_w, own, last=True)
    mate = project((zero, one), mate_far, far_w, mate, last=True)

    def attention(which, valid, wide):
        info = jnp.concatenate(
            [jnp.stack([span, valid, head * (HEADS * D), low ^ which]), at_k, at_v]
        )
        return attend(
            wide,
            info,
            live,
            part,
            mate if which else own,
            every_k + every_v,
        )

    away = send(attention(1, mate_valid, False), MATE)
    home = attention(0, valid, True)
    full = lax.dynamic_update_slice(home, away, (0, (1 - head) * (HEADS * D)))
    return full[None]


def solution(mesh):
    return jax.shard_map(
        on_device,
        mesh=mesh,
        in_specs=(
            P("dp", "ctx", None),
            P(),
            P(("dp", "ctx"), None),
            P(("dp", "ctx"), None),
            P(("dp", "ctx"), None),
            P(("dp", "ctx"), None),
            P(("dp", "ctx"), None),
            P("dp", "ctx"),
            P("dp"),
        ),
        out_specs=P("dp", "ctx", None),
        check_vma=False,
    )
```

```python
import functools
import math

import jax
import jax.numpy as jnp
import numpy as np
from jax import lax
from jax.experimental import pallas as pl
from jax.experimental.pallas import tpu as pltpu
from jax.sharding import PartitionSpec as P

HEADS = 7
D = 128
WIDTH = 3584
ROWS = 28
TOK = 256
SLOTS = 64
SPANS = 32
EPS = 1e-6
FILL = -1e30
AXES = ("dp", "ctx")
SCALE = 1.0 / math.sqrt(D)


def device_id(x, y, z, c):
    return ((y % 2) * 2 + c) * 32 + (x * 4 + z) * 2 + y // 2


def make_perm(f):
    pairs = []
    for x in range(4):
        for y in range(4):
            for z in range(4):
                for c in range(2):
                    tx, ty, tz, tc = f(x, y, z, c)
                    pairs.append(
                        (device_id(x, y, z, c), device_id(tx % 4, ty % 4, tz % 4, tc % 2))
                    )
    return pairs


SWAP = make_perm(lambda x, y, z, c: (x, y, z, 1 - c))
MATE = make_perm(lambda x, y, z, c: (x, y ^ 1, z, c))
ACROSS = make_perm(lambda x, y, z, c: (x, y ^ 3, z, c))

def flip(axis, turn):
    def partner(x, y, z, c):
        at = {"x": x, "y": y, "z": z}
        at[axis] ^= 1 if (c + turn) % 2 == 0 else 3
        return at["x"], at["y"], at["z"], c

    return make_perm(partner)


FLIP = {(axis, turn): flip(axis, turn) for axis in "xz" for turn in (0, 1)}

KEPT = 2
CUTS = (0, 2 * D, (4 + KEPT) * D, (4 + HEADS) * D)
SLAB = WIDTH // 4
PAIRED = ((0, 1, 2, 3), (0, 3, 1, 2))


def send(value, pairs):
    return lax.ppermute(value, AXES, pairs)


def feature_runs(last):
    starts = []
    for c in range(2):
        for i in PAIRED[c]:
            for j in range(4):
                for y in range(4):
                    x, z = (i, j) if last == "x" else (j, i)
                    starts.append(device_id(x, y, z, c) * ROWS)
    source = np.concatenate([np.arange(s, s + ROWS) for s in starts])
    tiles = []
    for tile in range(WIDTH // 128):
        part = source[tile * 128 : (tile + 1) * 128]
        runs = []
        lane = 0
        while lane < 128:
            end = lane + 1
            while end < 128 and part[end] == part[end - 1] + 1 and part[end] % 128 != 0:
                end += 1
            runs.append((lane, end, int(part[lane])))
            lane = end
        tiles.append(runs)
    return tiles


def reorder(plain_ref, out_ref, last, count, out_rows):
    lane = lax.broadcasted_iota(jnp.int32, (count, 128), 1)
    for tile, runs in enumerate(feature_runs(last)):
        joined = jnp.zeros((count, 128), jnp.float32)
        for first, end, feature in runs:
            block, offset = divmod(feature, 128)
            piece = plain_ref[:, block * 128 : (block + 1) * 128]
            shift = (first - offset) % 128
            if shift:
                piece = pltpu.roll(piece, shift, 1)
            joined = jnp.where((lane >= first) & (lane < end), piece, joined)
        slab, column = divmod(tile, SLAB // 128)
        out_ref[slab, out_rows, column * 128 : (column + 1) * 128] = joined.astype(jnp.bfloat16)


def norm_body(fact_ref, tokens_ref, gain_ref, near_ref, far_ref, *scratch):
    out_ref, pool_ref, plain_ref, normed_ref = scratch
    rows = 64
    level, valid, count = fact_ref[0], fact_ref[1], fact_ref[2]

    @pl.loop(0, TOK // rows)
    def _(step):
        here = pl.ds(pl.multiple_of(step * rows, rows), rows)
        values = tokens_ref[here, :].astype(jnp.float32)
        factor = lax.rsqrt(jnp.mean(values * values, axis=-1, keepdims=True) + EPS)
        plain_ref[...] = values * factor * gain_ref[...].reshape(1, WIDTH)
        normed_ref[here, :] = plain_ref[...].astype(jnp.bfloat16)
        reorder(plain_ref, out_ref, "x", rows, here)

    shift = level + 2
    live = jnp.right_shift(TOK, shift)
    slot = lax.broadcasted_iota(jnp.int32, (SLOTS, TOK), 0)
    position = lax.broadcasted_iota(jnp.int32, (SLOTS, TOK), 1)
    inside = (jnp.right_shift(position, shift) == slot) & (slot < live) & (position < valid)
    window = jnp.where(inside, 1.0, 0.0)
    size = jnp.maximum(jnp.sum(window, axis=1, keepdims=True), 1.0)
    sums = jnp.dot(
        window.astype(jnp.bfloat16), normed_ref[...], preferred_element_type=jnp.float32
    )
    plain_ref[...] = sums / size
    reorder(plain_ref, pool_ref, "z", SLOTS, pl.ds(0, SLOTS))
    row = lax.broadcasted_iota(jnp.int32, (16, SLAB), 0)
    facts = jnp.where(row < 8, count, valid).astype(jnp.float32).astype(jnp.bfloat16)
    for i in range(2):
        near_ref[i, :TOK, :] = out_ref[fact_ref[3 + i]]
        far_ref[i] = out_ref[fact_ref[5 + i]]
        for j in range(2):
            lines = slice(TOK + j * (SLOTS + 16), TOK + j * (SLOTS + 16) + SLOTS)
            near_ref[i, lines, :] = pool_ref[2 * i + j]
            near_ref[i, lines.stop : lines.stop + 16, :] = facts


def norm_rows(facts, tokens, gain):
    vmem = pl.BlockSpec(memory_space=pltpu.VMEM)
    return pl.pallas_call(
        norm_body,
        out_shape=[
            jax.ShapeDtypeStruct((2, TOK + 2 * (SLOTS + 16), SLAB), jnp.bfloat16),
            jax.ShapeDtypeStruct((2, TOK, SLAB), jnp.bfloat16),
        ],
        in_specs=[pl.BlockSpec(memory_space=pltpu.SMEM), vmem, vmem],
        out_specs=[vmem, vmem],
        scratch_shapes=[
            pltpu.VMEM((4, TOK, SLAB), jnp.bfloat16),
            pltpu.VMEM((4, SLOTS, SLAB), jnp.bfloat16),
            pltpu.VMEM((64, WIDTH), jnp.float32),
            pltpu.VMEM((TOK, WIDTH), jnp.bfloat16),
        ],
        compiler_params=pltpu.CompilerParams(vmem_limit_bytes=16 * 1024 * 1024),
    )(facts, tokens, gain)


BLOCK = 256
ROOM = SPANS * SLOTS + BLOCK
LINES = HEADS * TOK


def attend_body(wide, info_ref, count_ref, part_ref, more_ref, far_k_ref, far_v_ref, *rest):
    out_ref, query_ref, keys_ref, values_ref, bias_ref, score_ref, top_ref, sum_ref, mix_ref = rest
    span, valid, column, which = info_ref[0], info_ref[1], info_ref[2], info_ref[3]
    own = slice(0, TOK) if wide else slice(TOK, 2 * TOK)

    lane = lax.broadcasted_iota(jnp.int32, (1, ROOM), 1)
    bias_ref[...] = jnp.full((1, ROOM), FILL, jnp.float32)

    def pack(i, at):
        place_k, place_v = info_ref[4 + i], info_ref[4 + SPANS + i]
        count = count_ref[place_k * 2 + which]
        here = pl.ds(pl.multiple_of(at, 16), SLOTS)
        keys_ref[here, :] = far_k_ref[place_k, which, :SLOTS, :]
        values_ref[here, :] = far_v_ref[place_v, which]
        bias_ref[...] = jnp.where((lane >= at) & (lane < at + count), 0.0, bias_ref[...])
        return at + ((count + 15) // 16) * 16

    used = lax.fori_loop(0, span, pack, jnp.int32(0))
    rest_rows = pl.ds(pl.multiple_of(used, 16), BLOCK)
    keys_ref[rest_rows, :] = jnp.zeros((BLOCK, D), jnp.bfloat16)
    values_ref[rest_rows, :] = jnp.zeros((BLOCK, D), jnp.bfloat16)
    blocks = (used + BLOCK - 1) // BLOCK

    power = SCALE * math.log2(math.e)
    contract = (((1,), (1,)), ((), ()))

    def fold(op, scores):
        out = scores[:, :D]
        for i in range(1, scores.shape[1] // D):
            out = op(out, scores[:, i * D : (i + 1) * D])
        return out

    row = lax.broadcasted_iota(jnp.int32, (TOK, TOK), 0)
    col = lax.broadcasted_iota(jnp.int32, (TOK, TOK), 1)
    near_bias = jnp.where((col <= row) & (col < valid), 0.0, FILL)
    for head in range(HEADS):
        here = slice(head * TOK, (head + 1) * TOK)
        if head < KEPT:
            query = part_ref[own, (2 + head) * D : (3 + head) * D]
        else:
            query = more_ref[:, (head - KEPT) * D : (head - KEPT + 1) * D]
        query_ref[here, :] = query
        near = lax.dot_general(
            query, part_ref[own, :D], contract, preferred_element_type=jnp.float32
        )
        near = near + near_bias
        score_ref[here, ROOM:] = near
        top_ref[here, :] = fold(jnp.maximum, near)

    def score(i, carry):
        here = pl.ds(pl.multiple_of(i * BLOCK, BLOCK), BLOCK)
        bias = bias_ref[:, here]
        for head in range(HEADS):
            lines = slice(head * TOK, (head + 1) * TOK)
            far = lax.dot_general(
                query_ref[lines, :],
                keys_ref[here, :],
                contract,
                preferred_element_type=jnp.float32,
            )
            far = far + bias
            score_ref[lines, here] = far
            top_ref[lines, :] = jnp.maximum(top_ref[lines, :], fold(jnp.maximum, far))
        return carry

    lax.fori_loop(0, blocks, score, jnp.int32(0))

    for head in range(HEADS):
        lines = slice(head * TOK, (head + 1) * TOK)
        top = jnp.max(top_ref[lines, :], axis=1, keepdims=True)
        top_ref[lines, :] = jnp.broadcast_to(top, (TOK, D))
        weight = jnp.exp2((score_ref[lines, ROOM:] - top) * power)
        sum_ref[lines, :] = fold(jnp.add, weight)
        mix_ref[lines, :] = jnp.dot(
            weight.astype(jnp.bfloat16),
            part_ref[own, D : 2 * D],
            preferred_element_type=jnp.float32,
        )

    def mix(i, carry):
        here = pl.ds(pl.multiple_of(i * BLOCK, BLOCK), BLOCK)
        for head in range(HEADS):
            lines = slice(head * TOK, (head + 1) * TOK)
            top = top_ref[lines, :]
            top = jnp.concatenate([top] * (BLOCK // D), axis=1)
            weight = jnp.exp2((score_ref[lines, here] - top) * power)
            sum_ref[lines, :] = sum_ref[lines, :] + fold(jnp.add, weight)
            mix_ref[lines, :] = mix_ref[lines, :] + jnp.dot(
                weight.astype(jnp.bfloat16), values_ref[here, :], preferred_element_type=jnp.float32
            )
        return carry

    lax.fori_loop(0, blocks, mix, jnp.int32(0))

    alive = lax.broadcasted_iota(jnp.int32, (TOK, D), 0) < valid
    for head in range(HEADS):
        lines = slice(head * TOK, (head + 1) * TOK)
        total = jnp.sum(sum_ref[lines, :], axis=1, keepdims=True)
        result = jnp.where(alive, mix_ref[lines, :] / total, 0.0).astype(jnp.bfloat16)
        if wide:
            out_ref[:, pl.ds(pl.multiple_of(column + head * D, D), D)] = result
        else:
            out_ref[:, head * D : (head + 1) * D] = result


def attend(wide, info, counts, part, more, far_k, far_v):
    columns = 2 * HEADS * D if wide else HEADS * D
    smem, vmem = pl.BlockSpec(memory_space=pltpu.SMEM), pl.BlockSpec(memory_space=pltpu.VMEM)
    return pl.pallas_call(
        functools.partial(attend_body, wide),
        out_shape=jax.ShapeDtypeStruct((TOK, columns), jnp.bfloat16),
        in_specs=[smem, smem, vmem, vmem, vmem, vmem],
        out_specs=vmem,
        scratch_shapes=[
            pltpu.VMEM((LINES, D), jnp.bfloat16),
            pltpu.VMEM((ROOM, D), jnp.bfloat16),
            pltpu.VMEM((ROOM, D), jnp.bfloat16),
            pltpu.VMEM((1, ROOM), jnp.float32),
            pltpu.VMEM((LINES, ROOM + TOK), jnp.float32),
            pltpu.VMEM((LINES, D), jnp.float32),
            pltpu.VMEM((LINES, D), jnp.float32),
            pltpu.VMEM((LINES, D), jnp.float32),
        ],
        compiler_params=pltpu.CompilerParams(vmem_limit_bytes=28 * 1024 * 1024),
    )(info, counts, part, more, far_k, far_v)


def project_body(count, slab_ref, x_ref, *refs):
    weights, total_refs, out_ref = refs[:count], refs[count:-1], refs[-1]
    rows, columns = out_ref.shape
    for first in range(0, columns, 256):
        here = slice(first, min(first + 256, columns))
        out = total_refs[0][:, here] if total_refs else None
        for i in range(count):
            x = x_ref[slab_ref[i], :rows, :]
            term = jnp.dot(x, weights[i][:, here], preferred_element_type=jnp.float32)
            out = term if out is None else out + term
        out_ref[:, here] = out.astype(out_ref.dtype)


def project(slabs, x, weights, total=None, last=False, rows=TOK):
    smem, vmem = pl.BlockSpec(memory_space=pltpu.SMEM), pl.BlockSpec(memory_space=pltpu.VMEM)
    totals = () if total is None else (total,)
    dtype = jnp.bfloat16 if last else jnp.float32
    return pl.pallas_call(
        functools.partial(project_body, len(weights)),
        out_shape=jax.ShapeDtypeStruct((rows, weights[0].shape[1]), dtype),
        in_specs=[smem] + [vmem] * (1 + len(weights) + len(totals)),
        out_specs=vmem,
        compiler_params=pltpu.CompilerParams(vmem_limit_bytes=16 * 1024 * 1024),
    )(jnp.stack(slabs).astype(jnp.int32), x, *weights, *totals)


def crossed_body(info_ref, own_near, own_far, mate_near, mate_far, *refs):
    (near_w, far_w, other_w), out_ref, full_ref = refs[:3], refs[3], refs[4]
    pieces = ((near_w, 0), (far_w, 0), (other_w, 0), (other_w, SLAB))
    core = info_ref[0]
    block = 4 * ROWS
    for i, (piece, start) in enumerate(pieces):
        theirs, is_far = divmod(i, 2)
        side = core if theirs == 0 else 1 - core
        pair_x, pair_z = info_ref[1 + theirs], info_ref[3 + theirs]
        if is_far:
            pair_z = 1 - pair_z
        for t in range(2):
            split = jnp.where(pair_z == 0, PAIRED[1][t], PAIRED[1][2 + t])
            z = jnp.where(side == 0, 2 * pair_z + t, split)
            for x in range(4):
                at = jnp.where(side == 0, x, PAIRED[1].index(x))
                slab = jnp.where(at // 2 == pair_x, 0, 2) + theirs
                line = slab * SLAB + ((at % 2) * 4 + z) * block
                source = slice(start + (t * 4 + x) * block, start + (t * 4 + x + 1) * block)
                full_ref[pl.ds(pl.multiple_of(line, 16), block), :] = piece[source, :]
    columns = out_ref.shape[1]
    for first in range(0, columns, 256):
        here = slice(first, first + 256)
        for j, (near_ref, far_ref) in enumerate(((own_near, own_far), (mate_near, mate_far))):
            out = None
            for slab in range(4):
                x_ref = near_ref if slab < 2 else far_ref
                w = full_ref[slab * SLAB : (slab + 1) * SLAB, here]
                term = jnp.dot(x_ref[slab % 2, :TOK, :], w, preferred_element_type=jnp.float32)
                out = term if out is None else out + term
            out_ref[j * TOK : (j + 1) * TOK, here] = out.astype(jnp.bfloat16)


def project_crossed(info, tokens, pieces):
    smem, vmem = pl.BlockSpec(memory_space=pltpu.SMEM), pl.BlockSpec(memory_space=pltpu.VMEM)
    columns = pieces[0].shape[1]
    return pl.pallas_call(
        crossed_body,
        out_shape=jax.ShapeDtypeStruct((2 * TOK, columns), jnp.bfloat16),
        in_specs=[smem] + [vmem] * 7,
        out_specs=vmem,
        scratch_shapes=[pltpu.VMEM((WIDTH, columns), jnp.bfloat16)],
        compiler_params=pltpu.CompilerParams(vmem_limit_bytes=16 * 1024 * 1024),
    )(info, *tokens, *pieces)


def after(value, other):
    return lax.optimization_barrier((value, other))[0]


def halves_body(head_ref, *refs):
    mine_ref, other_ref = refs[-2:]

    def copy(mine):
        at = 0
        for ref in refs[:-2]:
            size = ref.shape[1] // 2
            mine_ref[:, at : at + size] = ref[:, mine * size : (mine + 1) * size]
            other_ref[:, at : at + size] = ref[:, (1 - mine) * size : (2 - mine) * size]
            at += size

    for mine in range(2):
        pl.when(head_ref[0] == mine)(functools.partial(copy, mine))


def halves(head, *weights):
    smem, vmem = pl.BlockSpec(memory_space=pltpu.SMEM), pl.BlockSpec(memory_space=pltpu.VMEM)
    return pl.pallas_call(
        halves_body,
        out_shape=[jax.ShapeDtypeStruct((ROWS, CUTS[-1]), jnp.bfloat16)] * 2,
        in_specs=[smem] + [vmem] * len(weights),
        out_specs=[vmem, vmem],
        compiler_params=pltpu.CompilerParams(vmem_limit_bytes=4 * 1024 * 1024),
    )(head.reshape(1), *weights)


def double(block, axis):
    pair = jnp.stack([block, send(block, FLIP[axis, 0])])
    return jnp.concatenate([pair, send(pair, FLIP[axis, 1])])


def in_place(pieces, slots, blank):
    joined = blank
    for i, slot in enumerate(slots):
        joined = lax.dynamic_update_slice_in_dim(joined, pieces[i][None], slot, 0)
    return joined


def on_device(tokens, gain, w_query, w_key, w_value, w_mark_key, w_mark_value, level, hist_len):
    dp = lax.axis_index("dp")
    span = lax.axis_index("ctx")
    core, low, high = dp % 2, dp // 2, span % 2
    head = low ^ high
    pos = {"x": span // 8, "z": (span // 2) % 4}
    near, far = 1 + 2 * core, 3 - 2 * core

    def order(first, one, two):
        return jnp.where(first == 0, jnp.concatenate([one, two], 0), jnp.concatenate([two, one], 0))

    mine, other = halves(head, w_mark_key, w_mark_value, w_key, w_value, w_query)
    rows = order(low, mine, send(other, MATE))

    def pair_of(axis, side):
        p = pos[axis]
        inner = jnp.logical_or(p == 1, p == 2).astype(jnp.int32)
        index = jnp.where(side == 0, p // 2, inner)
        return index, jnp.where(side == 0, p % 2, p // 2)

    def slabs(axis):
        mine, theirs = pair_of(axis, core)[0], pair_of(axis, 1 - core)[0]
        return (
            (core * 2 + mine, 2 * (1 - core) + theirs),
            (core * 2 + 1 - mine, 2 * (1 - core) + 1 - theirs),
        )

    begin = span * TOK
    stride = jnp.left_shift(jnp.int32(4), level[0, 0])
    valid = jnp.clip(hist_len[0] - begin, 0, TOK)
    count = jnp.minimum(TOK // stride, (valid + stride - 1) // stride)
    near_slots, far_slots = slabs("x")
    facts = jnp.stack([level[0, 0], valid, count, *near_slots, *far_slots]).astype(jnp.int32)
    own_near, own_far = norm_rows(facts, tokens[0], gain)
    mate_near = send(own_near, MATE)
    mate_far = send(after(own_far, mate_near), MATE)
    facts = mate_near[0, TOK + SLOTS : TOK + SLOTS + 16, 0].astype(jnp.int32)
    mate_count, mate_valid = facts[0], facts[8]

    def pooled_of(packed):
        return packed[:, TOK:].reshape(4, SLOTS + 16, SLAB)[:, :SLOTS]

    rows = order(high, rows, send(rows, ACROSS))

    def blank(shape, after):
        return lax.optimization_barrier((jnp.zeros(shape, jnp.bfloat16), after))[0]

    def second(block, axis):
        p = pos[axis]
        joined = blank((4,) + block.shape, block)
        joined = in_place(double(block, axis), (p, p ^ near, p ^ far, p ^ 2), joined)
        return joined.reshape(-1, block.shape[-1])

    early = second(rows[:, : CUTS[2]], "x")
    late = second(rows[:, CUTS[2] :], "z")

    early, cross = early[:, : CUTS[1]], early[:, CUTS[1] :]
    z_second, x_second = pair_of("z", core)[1], pair_of("x", core)[1]
    early = order(z_second, early, send(early, FLIP["z", 0]))
    cross = order(z_second, cross, send(cross, FLIP["z", 0]))
    late = order(x_second, late, send(late, FLIP["x", 0]))
    early_far = send(early, FLIP["z", 1])
    cross_far = send(after(cross, early_far), FLIP["z", 1])
    late_far = send(late, FLIP["x", 1])
    gathered = jnp.concatenate([early, early_far], 0)
    swapped = send(gathered, SWAP)
    slab_near, slab_far = slabs("z")
    where_m = (slab_near[0], slab_far[0], slab_near[1], slab_far[1])
    pieces_m = (early, early_far, swapped[:SLAB], swapped[SLAB:])
    both_pooled = jnp.concatenate([pooled_of(own_near), pooled_of(mate_near)], 1)
    beacon = project(where_m, both_pooled, pieces_m, last=True, rows=2 * SLOTS)
    beacon = beacon.reshape(2, SLOTS, 2 * D)
    counts = jnp.stack([count, mate_count]).astype(jnp.bfloat16)
    flags = jnp.broadcast_to(counts[:, None, None], (2, 16, D))
    block_k = jnp.concatenate([beacon[..., :D], flags], 1)
    block_v = beacon[..., D:]
    block = jnp.concatenate([block_k, block_v], 1)
    block = order(low, block[:1], block[1:])
    block = jnp.stack([block, send(block, ACROSS)])
    half_k = double(block[:, :, : SLOTS + 16], "x")
    half_v = double(block[:, :, SLOTS + 16 :], "z")
    zero, one = jnp.int32(0), jnp.int32(1)
    near_w = (late, send(late, SWAP))
    own = project((zero, one), own_near, near_w)
    half_k, half_v = after((half_k, half_v), own)
    crossed = jnp.concatenate([cross, cross_far], 0)
    crossed, far_w = after((crossed, late_far), (half_k, half_v))
    crossed = send(crossed, SWAP)
    far_w = (far_w, send(far_w, SWAP))
    pair_k = jnp.stack([half_k, send(half_k, FLIP["z", 0])])
    pair_v = jnp.stack([half_v, send(half_v, FLIP["x", 0])])
    mate = project((zero, one), mate_near, near_w)
    pair_k, pair_v = after((pair_k, pair_v), (mate, mate_far))
    every_k = jnp.concatenate([pair_k, send(pair_k, FLIP["z", 1])])
    every_v = jnp.concatenate([pair_v, send(pair_v, FLIP["x", 1])])
    every_k = every_k.reshape(SPANS, 2, SLOTS + 16, D)
    every_v = every_v.reshape(SPANS, 2, SLOTS, D)

    owner = jnp.arange(SPANS, dtype=jnp.int32)

    def code(axis, at):
        d = at ^ pos[axis]
        return jnp.where(d == 0, 0, jnp.where(d == near, 1, jnp.where(d == far, 2, 3)))

    code_x, code_z = code("x", owner // 8), code("z", (owner // 2) % 4)
    code_h = (owner ^ span) % 2
    at_k = (code_z * 4 + code_x) * 2 + code_h
    at_v = (code_x * 4 + code_z) * 2 + code_h
    live = every_k[:, :, SLOTS, 0].astype(jnp.int32).reshape(2 * SPANS)

    pairs = [pair_of(axis, side)[0] for axis in "xz" for side in (core, 1 - core)]
    part = project_crossed(
        jnp.stack([core, *pairs]).astype(jnp.int32),
        (own_near, own_far, mate_near, mate_far),
        (cross, cross_far, crossed),
    )
    own = project((zero, one), own_far, far_w, own, last=True)
    mate = project((zero, one), mate_far, far_w, mate, last=True)

    def attention(which, valid, wide):
        info = jnp.concatenate(
            [jnp.stack([span, valid, head * (HEADS * D), low ^ which]), at_k, at_v]
        )
        return attend(
            wide,
            info,
            live,
            part,
            mate if which else own,
            every_k,
            every_v,
        )

    away = send(attention(1, mate_valid, False), MATE)
    home = attention(0, valid, True)
    full = lax.dynamic_update_slice(home, away, (0, (1 - head) * (HEADS * D)))
    return full[None]


def solution(mesh):
    return jax.shard_map(
        on_device,
        mesh=mesh,
        in_specs=(
            P("dp", "ctx", None),
            P(),
            P(("dp", "ctx"), None),
            P(("dp", "ctx"), None),
            P(("dp", "ctx"), None),
            P(("dp", "ctx"), None),
            P(("dp", "ctx"), None),
            P("dp", "ctx"),
            P("dp"),
        ),
        out_specs=P("dp", "ctx", None),
        check_vma=False,
    )
```
